128 devices in a mesh: row: 8 (over z, core), col: 16 (over x, y).
Axes of the slice: x: 4, y: 4, z: 4, core: 2. Of those that a mesh axis runs over, the one named last changes fastest.
Arguments:
- matrix: float32 [18432, 18432], P('row', 'col'), may hold values from -0.5 to 1.5
- first_step: int32 [1], replicated, may hold values from 0 to 66
- lower_inverse: float32 [6, 128, 128], replicated, may hold values from -1 to 1, as said below
- upper_inverse: float32 [6, 128, 128], replicated, may hold values from -1 to 1.5, as said below
Outputs:
- factored: float32 [18432, 18432], P('row', 'col')
The draws below stay inside these ranges and needn't reach their ends.
Inputs may be any that keep to these rules, and one draw needn't show every extreme that they name: Each lower_inverse[t] is zero above its diagonal and one on it. Each upper_inverse[t] is zero below its diagonal, with positive diagonal entries.
All inputs are finite; a program needn't handle non-finite values.
Results may differ from the reference program's by a relative error of at most 0.0003.
Values sent between devices are 32-bit elements; how exact they have to be, the bound alone decides.
No kernel may reach another device: no remote copies, remote signals or barrier semaphores. Data moves between devices by JAX's collectives and lax.ppermute only.
A program may use at most 128 MiB of HBM per device.

```python
import jax
import jax.numpy as jnp
from jax import lax

NB = 128
MB = 18
STEPS = 6
KB = 9
NBLK = 144
N_ROW = 8
N_COL = 16


def storage_blocks(blocks_dev, devices):
    places = jnp.arange(blocks_dev * devices * NB, dtype=jnp.int32)
    owner = places // (blocks_dev * NB)
    local = places % (blocks_dev * NB) // NB
    return (local * devices + owner) * NB + places % NB


def draw_matrix(key, part):
    key = jax.random.fold_in(key, 11)
    order = MB * N_ROW * NB
    row_place = storage_blocks(MB, N_ROW)
    col_place = storage_blocks(KB, N_COL)
    values = 0.06 * jax.random.truncated_normal(key, -4.0, 4.0, (order, order), jnp.float32)
    ones = (row_place[:, None] == col_place[None, :]).astype(jnp.float32)
    return values + ones


def triangle_draw(key, lower_side, diagonal_low, diagonal_high):
    first, second = jax.random.split(key)
    values = 0.5 * jax.random.truncated_normal(first, -3.0, 3.0, (STEPS, NB, NB), jnp.float32) / jnp.sqrt(jnp.float32(NB))
    diagonal = jnp.exp(jax.random.uniform(second, (STEPS, NB, 1), jnp.float32, jnp.log(diagonal_low), jnp.log(diagonal_high)))
    rows = jnp.arange(NB, dtype=jnp.int32)[:, None]
    cols = jnp.arange(NB, dtype=jnp.int32)[None, :]
    below = jnp.where(rows > cols, 1.0, 0.0) if lower_side else jnp.where(rows < cols, 1.0, 0.0)
    same = jnp.where(rows == cols, 1.0, 0.0)
    return values * below + diagonal * same


def draw_lower_inverse(key, part):
    key = jax.random.fold_in(key, 23)
    return triangle_draw(key, True, 1.0, 1.0)


def draw_upper_inverse(key, part):
    key = jax.random.fold_in(key, 37)
    return triangle_draw(key, False, 0.7, 1.4)


def setup_inputs(seed: int = 0) -> dict:
    seeds = jax.random.split(jax.random.key(seed), 5)
    matrix = draw_matrix(jax.random.fold_in(seeds[4], 71), 0)
    first_step = jax.random.randint(seeds[1], (1,), 0, NBLK // 2 - STEPS + 1).astype(jnp.int32)
    lower_inverse = draw_lower_inverse(jax.random.fold_in(seeds[4], 71), 0)
    upper_inverse = draw_upper_inverse(jax.random.fold_in(seeds[4], 71), 0)
    return dict(matrix=matrix, first_step=first_step, lower_inverse=lower_inverse, upper_inverse=upper_inverse)


def precise_dot(left, right):
    return jnp.dot(left, right, precision=lax.Precision.HIGHEST, preferred_element_type=jnp.float32)


def global_blocks(blocks_dev, devices):
    places = jnp.arange(blocks_dev * devices * NB, dtype=jnp.int32)
    owner = places // (blocks_dev * NB)
    local = (places % (blocks_dev * NB)) // NB
    return local * devices + owner


def reference(matrix, first_step, lower_inverse, upper_inverse):
    row_block = global_blocks(MB, N_ROW)
    col_block = global_blocks(KB, N_COL)
    start = first_step[0].astype(jnp.int32)
    current = matrix
    for turn in range(STEPS):
        pivot = start + turn
        col_start = (((pivot % N_COL) * KB + pivot // N_COL) * NB).astype(jnp.int32)
        row_start = (((pivot % N_ROW) * MB + pivot // N_ROW) * NB).astype(jnp.int32)
        column = lax.dynamic_slice_in_dim(current, col_start, NB, 1)
        panel = precise_dot(column, upper_inverse[turn])
        rows = lax.dynamic_slice_in_dim(current, row_start, NB, 0)
        top = precise_dot(lower_inverse[turn], rows)
        row_live = (row_block > pivot)[:, None]
        col_live = (col_block > pivot)[None, :]
        left = jnp.where(row_live, panel, jnp.float32(0.0))
        right = jnp.where(col_live, top, jnp.float32(0.0))
        current = current - precise_dot(left, right)
        column = lax.dynamic_slice_in_dim(current, col_start, NB, 1)
        current = lax.dynamic_update_slice_in_dim(current, jnp.where(row_live, panel, column), col_start, 1)
        rows = lax.dynamic_slice_in_dim(current, row_start, NB, 0)
        current = lax.dynamic_update_slice_in_dim(current, jnp.where(col_live, top, rows), row_start, 0)
    return current
```

```python
import functools

import jax
import jax.numpy as jnp
from jax import lax
from jax.experimental import pallas as pl
from jax.experimental.pallas import tpu as pltpu
from jax.sharding import PartitionSpec as P

B = 128
STEPS = 6
ROWS = 2304
COLS = 1152
SHARE = 144
HALF = 72
N_ROW = 8
N_COL = 16
WIDE = STEPS * B

F32 = jnp.float32
BF16 = jnp.bfloat16
ANY = pl.BlockSpec(memory_space=pl.ANY)
VM = pl.BlockSpec(memory_space=pltpu.VMEM)
SM = pl.BlockSpec(memory_space=pltpu.SMEM)
PARAMS = pltpu.CompilerParams(vmem_limit_bytes=48 * 1024 * 1024)


def split(value):
    high = value.astype(BF16)
    low = (value - high.astype(F32)).astype(BF16)
    return high, low


def mul(left, right):
    return jnp.dot(left, right, preferred_element_type=F32)


def dot3(left, right):
    lh, ll = left
    rh, rl = right
    return mul(lh, rh) + (mul(ll, rh) + mul(lh, rl))


def place(first):
    k0 = first[0]
    p = lax.axis_index("row")
    q = lax.axis_index("col")
    own_col = lax.rem(q - k0 + 8 * N_COL, N_COL)
    own_row = lax.rem(p - k0 + 16 * N_ROW, N_ROW)
    col_block = lax.div(k0 + jnp.minimum(own_col, STEPS - 1), N_COL)
    row_block = lax.div(k0 + jnp.minimum(own_row, STEPS - 1), N_ROW)
    return k0, p, q, own_col, own_row, col_block, row_block


def send_kernel(first, matrix, *refs):
    messages = refs[:N_COL]
    tops = refs[N_COL:N_COL + 2]
    sem = refs[-1]
    k0, p, q, own_col, own_row, col_block, row_block = place(first)
    lanes = pl.ds(pl.multiple_of(col_block * B, B), B)
    pivot = pl.multiple_of(row_block * B, B)
    copies = []
    for j in range(N_COL):
        start = pl.multiple_of(lax.rem(q + j, N_COL) * SHARE, 8)
        copies.append(pltpu.make_async_copy(
            matrix.at[pl.ds(pivot, B), lanes], messages[j].at[pl.ds(SHARE, B)], sem.at[2 * j]))
        copies.append(pltpu.make_async_copy(
            matrix.at[pl.ds(start, SHARE), lanes], messages[j].at[pl.ds(0, SHARE)], sem.at[2 * j + 1]))
    for h in range(2):
        copies.append(pltpu.make_async_copy(
            matrix.at[pl.ds(pivot + h * 64, 64)], tops[h], sem.at[2 * N_COL + h]))
    for copy in copies:
        copy.start()
    for copy in copies:
        copy.wait()


def pick(refs, index, target, sem):
    for n, ref in enumerate(refs):
        @pl.when(index == n)
        def _():
            pltpu.make_async_copy(ref, target, sem).start()
    return pltpu.make_async_copy(refs[0], target, sem)


def select_kernel(first, *refs):
    messages = refs[:N_COL]
    one, two, corner, sem = refs[N_COL:]
    k0 = first[0]
    q = lax.axis_index("col")
    waits = []
    for t in range(STEPS):
        index = lax.rem(q - k0 - t + 8 * N_COL, N_COL)
        waits.append(pick([m.at[pl.ds(SHARE, B)] for m in messages], index, corner.at[t], sem.at[t, 0]))
        waits.append(pick([m.at[pl.ds(0, HALF)] for m in messages], index, one.at[t], sem.at[t, 1]))
        waits.append(pick([m.at[pl.ds(HALF, HALF)] for m in messages], index, two.at[t], sem.at[t, 2]))
    for wait in waits:
        wait.wait()


def factor_kernel(first, lower, upper, *refs):
    corners = refs[:8]
    top_a = refs[8:16]
    top_b = refs[16:24]
    t_hi, t_lo, c_hi, c_lo, patch, cur, blocks, sem, sem_top = refs[24:]
    k0, p, q, own_col, own_row, col_block, row_block = place(first)
    z = lax.div(p, 2)
    core = lax.rem(p, 2)
    waits, waits_top = [], []
    for a in range(STEPS):
        source = lax.rem(k0 + a, N_ROW)
        dz = lax.rem(z - lax.div(source, 2) + 4, 4)
        other = jnp.where(lax.rem(source, 2) == core, 0, 1)
        index = other * 4 + dz
        waits.append(pick(corners, index, blocks.at[a], sem.at[a]))
        waits_top.append(pick(top_a, index, cur.at[pl.ds(a * B, 64), pl.ds(WIDE, COLS)], sem_top.at[a, 0]))
        waits_top.append(pick(top_b, index, cur.at[pl.ds(a * B + 64, 64), pl.ds(WIDE, COLS)], sem_top.at[a, 1]))
    for wait in waits:
        wait.wait()
    for a in range(STEPS):
        for t in range(STEPS):
            cur[a * B:(a + 1) * B, t * B:(t + 1) * B] = blocks[a, t]
    for wait in waits_top:
        wait.wait()
    lane_block = (lax.broadcasted_iota(jnp.int32, (1, COLS), 1) >> 7) * N_COL + q
    for t in range(STEPS):
        here = slice(t * B, (t + 1) * B)
        below = slice((t + 1) * B, WIDE)
        after = slice((t + 1) * B, WIDE + COLS)
        low = split(lower[t])
        rows = cur[here, after]
        top = dot3(low, split(rows))
        live = lane_block > k0 + t
        if t + 1 < STEPS:
            keep = (STEPS - 1 - t) * B
            panel = dot3(split(cur[below, here]), split(upper[t]))
            cur[below, here] = panel
            corner_top = top[:, :keep]
            right = jnp.where(live, top[:, keep:], 0.0)
            ch, cl = split(corner_top)
            c_hi[here, after.start:WIDE] = ch
            c_lo[here, after.start:WIDE] = cl
            rh, rl = split(right)
            panels = split(panel)
            cur[below, (t + 1) * B:WIDE] -= dot3(panels, (ch, cl))
            cur[below, WIDE:] -= dot3(panels, (rh, rl))
            old = rows[:, keep:]
        else:
            right = jnp.where(live, top, 0.0)
            rh, rl = split(right)
            old = rows
        t_hi[here, :] = rh
        t_lo[here, :] = rl

        @pl.when(own_row == t)
        def _():
            patch[...] = jnp.where(live, right, old)
            if t > 0:
                @pl.when(own_col < t)
                def _():
                    source = pl.multiple_of(own_col * B, B)
                    target = pl.multiple_of(col_block * B, B)
                    patch[:, pl.ds(target, B)] = cur[here, pl.ds(source, B)]


def update_kernel(turn, last, first, *refs):
    pieces = refs[:4]
    matrix, t_hi, t_lo, c_hi, c_lo, upper, patch = refs[4:11]
    refs = refs[11:]
    if turn > 0:
        refs = refs[1:]
    out, rows, panel_hi, panel_lo, panel, sem_in, sem_out, sem_patch = refs
    k0, p, q, own_col, own_row, col_block, row_block = place(first)
    x = lax.div(q, 4)
    y = lax.rem(q, 4)
    starts = []
    for n in range(8):
        d = n % 4
        if n < 4:
            owner = lax.rem(x + 4 - d, 4) * 4 + lax.rem(y + 4 - turn, 4)
            starts.append(owner * SHARE)
        else:
            owner = lax.rem(x + 4 - turn, 4) * 4 + lax.rem(y + 4 - d, 4)
            starts.append(owner * SHARE + HALF)
    starts = [pl.multiple_of(s, 8) for s in starts]
    ins = [pltpu.make_async_copy(matrix.at[pl.ds(s, HALF)], rows.at[pl.ds(n * HALF, HALF)], sem_in.at[n])
           for n, s in enumerate(starts)]
    outs = [pltpu.make_async_copy(rows.at[pl.ds(n * HALF, HALF)], out.at[pl.ds(s, HALF)], sem_out.at[n])
            for n, s in enumerate(starts)]
    for copy in ins:
        copy.start()
    count = 8 * HALF
    block = jnp.concatenate(
        [lax.broadcasted_iota(jnp.int32, (HALF, B), 0) + s for s in starts], axis=0)
    block = (block >> 7) * N_ROW + p
    for t in range(STEPS):
        raw = jnp.concatenate([pieces[n // 2][n % 2, t] for n in range(8)], axis=0)
        if t > 0:
            raw = raw - dot3((panel_hi[:, :t * B], panel_lo[:, :t * B]),
                             (c_hi[:t * B, t * B:(t + 1) * B], c_lo[:t * B, t * B:(t + 1) * B]))
        value = dot3(split(raw), split(upper[t]))
        value = jnp.where(block > k0 + t, value, 0.0)
        high, low = split(value)
        panel_hi[:, t * B:(t + 1) * B] = high
        panel_lo[:, t * B:(t + 1) * B] = low

        @pl.when(own_col == t)
        def _():
            panel[...] = value
    for copy in ins:
        copy.wait()
    for start in range(0, COLS, 256):
        stop = min(start + 256, COLS)
        rows[:, start:stop] -= dot3((panel_hi[...], panel_lo[...]), (t_hi[:, start:stop], t_lo[:, start:stop]))

    @pl.when(own_col < STEPS)
    def _():
        lanes = pl.ds(pl.multiple_of(col_block * B, B), B)
        rows[:, lanes] = jnp.where(block > k0 + own_col, panel[...], rows[:, lanes])
    for copy in outs:
        copy.start()
    for copy in outs:
        copy.wait()
    if last:
        @pl.when(own_row < STEPS)
        def _():
            copy = pltpu.make_async_copy(
                patch, out.at[pl.ds(pl.multiple_of(row_block * B, B), B)], sem_patch)
            copy.start()
            copy.wait()


def shards(matrix, first_step, lower_inverse, upper_inverse):
    def shape(*dims, dtype=F32):
        return jax.ShapeDtypeStruct(dims, dtype)

    dma = pltpu.SemaphoreType.DMA
    *messages, top_a, top_b = pl.pallas_call(
        send_kernel,
        out_shape=[shape(SHARE + B, B)] * N_COL + [shape(64, COLS)] * 2,
        in_specs=[SM, ANY], out_specs=[ANY] * (N_COL + 2),
        scratch_shapes=[dma((2 * N_COL + 2,))], compiler_params=PARAMS,
    )(first_step, matrix)

    spin = lambda j: [(i, (i + j) % N_COL) for i in range(N_COL)]
    along_x = lambda d: spin(4 * d)
    along_y = lambda d: [(i, i // 4 * 4 + (i + d) % 4) for i in range(N_COL)]
    along_z = lambda d: [(i, (i + 2 * d) % N_ROW) for i in range(N_ROW)]
    swap = [(i, i ^ 1) for i in range(N_ROW)]
    col = lambda v, pairs: lax.ppermute(v, "col", pairs)
    row = lambda v, pairs: lax.ppermute(v, "row", pairs)

    def ring(move, a, b):
        a1, b1 = move(a, 1), move(b, 1)
        a3, b3 = move(a, 3), move(b, 3)
        a2, b2 = move(a1, 1), move(b3, 3)
        return [a, a1, a2, a3], [b, b1, b2, b3]

    got = [messages[0]] + [col(messages[j], spin(j)) for j in range(1, N_COL)]
    one, two, corner = pl.pallas_call(
        select_kernel,
        out_shape=[shape(STEPS, HALF, B)] * 2 + [shape(STEPS, B, B)],
        in_specs=[SM] + [ANY] * N_COL, out_specs=[ANY] * 3,
        scratch_shapes=[dma((STEPS, 3))], compiler_params=PARAMS,
    )(first_step, *got)

    tops_a, tops_b = ring(lambda v, d: row(v, along_z(d)), top_a, top_b)
    corners = [corner] + [row(corner, along_z(d)) for d in range(1, 4)]
    corners += [row(v, swap) for v in corners]
    tops_a += [row(v, swap) for v in tops_a]
    tops_b += [row(v, swap) for v in tops_b]

    one_x = [one] + [col(one, along_x(d)) for d in range(1, 4)]
    two_y = [two] + [col(two, along_y(d)) for d in range(1, 4)]
    one_a, one_b = ring(lambda v, d: col(v, along_y(d)), jnp.stack(one_x[:2]), jnp.stack(one_x[2:]))
    two_a, two_b = ring(lambda v, d: col(v, along_x(d)), jnp.stack(two_y[:2]), jnp.stack(two_y[2:]))

    t_hi, t_lo, c_hi, c_lo, patch = pl.pallas_call(
        factor_kernel,
        out_shape=[shape(WIDE, COLS, dtype=BF16)] * 2 + [shape(WIDE, WIDE, dtype=BF16)] * 2 + [shape(B, COLS)],
        in_specs=[SM, VM, VM] + [ANY] * 24, out_specs=[VM] * 5,
        scratch_shapes=[pltpu.VMEM((WIDE, WIDE + COLS), F32), pltpu.VMEM((STEPS, STEPS, B, B), F32),
                        dma((STEPS,)), dma((STEPS, 2))],
        compiler_params=PARAMS,
        cost_estimate=pl.CostEstimate(flops=12_000_000_000, bytes_accessed=12_000_000, transcendentals=0),
    )(first_step, lower_inverse, upper_inverse, *corners, *tops_a, *tops_b)

    count = 8 * HALF
    out = None
    order = [0, 1, 3, 2]
    for turn in order:
        held = [] if out is None else [out]
        out = pl.pallas_call(
            functools.partial(update_kernel, turn, turn == order[-1]),
            out_shape=shape(ROWS, COLS),
            in_specs=[SM] + [VM] * 4 + [ANY] + [VM] * 5 + [ANY] + [ANY] * len(held), out_specs=ANY,
            input_output_aliases={12: 0} if held else {},
            scratch_shapes=[pltpu.VMEM((count, COLS), F32), pltpu.VMEM((count, WIDE), BF16),
                            pltpu.VMEM((count, WIDE), BF16), pltpu.VMEM((count, B), F32),
                            dma((8,)), dma((8,)), dma],
            compiler_params=PARAMS,
            cost_estimate=pl.CostEstimate(flops=6_000_000_000, bytes_accessed=12_000_000, transcendentals=0),
        )(first_step, one_a[turn], one_b[turn], two_a[turn], two_b[turn], matrix,
          t_hi, t_lo, c_hi, c_lo, upper_inverse, patch, *held)
    return out


def solution(mesh):
    placed = (P("row", "col"), P(), P(), P())
    return jax.shard_map(
        shards, mesh=mesh, in_specs=placed, out_specs=P("row", "col"), check_vma=False
    )
```

```python
import functools

import jax
import jax.numpy as jnp
from jax import lax
from jax.experimental import pallas as pl
from jax.experimental.pallas import tpu as pltpu
from jax.sharding import PartitionSpec as P

B = 128
STEPS = 6
ROWS = 2304
COLS = 1152
SHARE = 144
HALF = 72
N_ROW = 8
N_COL = 16
WIDE = STEPS * B
PART = 8 * HALF
TILE = 256

F32 = jnp.float32
BF16 = jnp.bfloat16
ANY = pl.BlockSpec(memory_space=pl.ANY)
VM = pl.BlockSpec(memory_space=pltpu.VMEM)
SM = pl.BlockSpec(memory_space=pltpu.SMEM)


def params(mebibytes):
    return pltpu.CompilerParams(vmem_limit_bytes=mebibytes * 1024 * 1024)


def split(value):
    high = value.astype(BF16)
    low = (value - high.astype(F32)).astype(BF16)
    return high, low


def mul(left, right):
    return jnp.dot(left, right, preferred_element_type=F32)


def dot3(left, right):
    lh, ll = left
    rh, rl = right
    return mul(lh, rh) + (mul(ll, rh) + mul(lh, rl))


def place(first):
    k0 = first[0]
    p = lax.axis_index("row")
    q = lax.axis_index("col")
    own_col = lax.rem(q - k0 + 8 * N_COL, N_COL)
    own_row = lax.rem(p - k0 + 16 * N_ROW, N_ROW)
    col_block = lax.div(k0 + jnp.minimum(own_col, STEPS - 1), N_COL)
    row_block = lax.div(k0 + jnp.minimum(own_row, STEPS - 1), N_ROW)
    return k0, p, q, own_col, own_row, col_block, row_block


def send_kernel(first, matrix, messages, top, sem):
    k0, p, q, own_col, own_row, col_block, row_block = place(first)
    lanes = pl.ds(pl.multiple_of(col_block * B, B), B)
    pivot = pl.multiple_of(row_block * B, B)
    copies = []
    for j in range(N_COL):
        copies.append(pltpu.make_async_copy(
            matrix.at[pl.ds(pivot, B), lanes], messages.at[j, pl.ds(SHARE, B)], sem.at[2 * j]))
        copies.append(pltpu.make_async_copy(
            matrix.at[pl.ds(j * SHARE, SHARE), lanes], messages.at[j, pl.ds(0, SHARE)], sem.at[2 * j + 1]))
    for h in range(2):
        copies.append(pltpu.make_async_copy(
            matrix.at[pl.ds(pivot + h * 64, 64)], top.at[h], sem.at[2 * N_COL + h]))
    for copy in copies:
        copy.start()
    for copy in copies:
        copy.wait()


def select_kernel(first, messages, one, two, corner, sem):
    k0 = first[0]
    copies = []
    for t in range(STEPS):
        owner = lax.rem(k0 + t, N_COL)
        copies.append(pltpu.make_async_copy(
            messages.at[owner, pl.ds(SHARE, B)], corner.at[:, pl.ds(t * B, B)], sem.at[t, 0]))
        copies.append(pltpu.make_async_copy(messages.at[owner, pl.ds(0, HALF)], one.at[t], sem.at[t, 1]))
        copies.append(pltpu.make_async_copy(messages.at[owner, pl.ds(HALF, HALF)], two.at[t], sem.at[t, 2]))
    for copy in copies:
        copy.start()
    for copy in copies:
        copy.wait()


def pick(refs, index, target, sem):
    for n, ref in enumerate(refs):
        @pl.when(index == n)
        def _():
            pltpu.make_async_copy(ref, target, sem).start()
    return pltpu.make_async_copy(refs[0], target, sem)


def ring_pieces(own, near, far):
    return [(own.at[0], own.at[1]), (near.at[0, 0], near.at[0, 1]),
            (far.at[0], far.at[1]), (near.at[1, 0], near.at[1, 1])]


def factor_kernel(first, lower, upper, *refs):
    corners = ring_pieces(*refs[0:3]) + ring_pieces(*refs[3:6])
    tops = ring_pieces(*refs[6:9]) + ring_pieces(*refs[9:12])
    t_hi, t_lo, c_hi, c_lo, patch, cur, sem, sem_top = refs[12:]
    k0, p, q, own_col, own_row, col_block, row_block = place(first)
    z = lax.div(p, 2)
    core = lax.rem(p, 2)
    waits, waits_top = [], []
    for a in range(STEPS):
        source = lax.rem(k0 + a, N_ROW)
        dz = lax.rem(z - lax.div(source, 2) + 4, 4)
        other = jnp.where(lax.rem(source, 2) == core, 0, 1)
        index = other * 4 + dz
        for h in range(2):
            half = pl.ds(a * B + h * 64, 64)
            waits.append(pick([c[h] for c in corners], index, cur.at[half, pl.ds(0, WIDE)], sem.at[a, h]))
            waits_top.append(pick([c[h] for c in tops], index, cur.at[half, pl.ds(WIDE, COLS)], sem_top.at[a, h]))
    for wait in waits + waits_top:
        wait.wait()
    lane_block = (lax.broadcasted_iota(jnp.int32, (1, COLS), 1) >> 7) * N_COL + q
    for t in range(STEPS):
        here = slice(t * B, (t + 1) * B)
        below = slice((t + 1) * B, WIDE)
        after = slice((t + 1) * B, WIDE + COLS)
        low = split(lower[t])
        rows = cur[here, after]
        top = dot3(low, split(rows))
        live = lane_block > k0 + t
        keep = (STEPS - 1 - t) * B
        if keep:
            panel = dot3(split(cur[below, here]), split(upper[t]))
            cur[below, here] = panel
            right = jnp.where(live, top[:, keep:], 0.0)
            ch, cl = split(top[:, :keep])
            c_hi[here, after.start:WIDE] = ch
            c_lo[here, after.start:WIDE] = cl
            rh, rl = split(right)
            panels = split(panel)
            cur[below, (t + 1) * B:WIDE] -= dot3(panels, (ch, cl))
            cur[below, WIDE:] -= dot3(panels, (rh, rl))
            old = rows[:, keep:]
        else:
            right = jnp.where(live, top, 0.0)
            rh, rl = split(right)
            old = rows
        t_hi[here, :] = rh
        t_lo[here, :] = rl

        @pl.when(own_row == t)
        def _():
            patch[...] = jnp.where(live, right, old)
            if t > 0:
                @pl.when(own_col < t)
                def _():
                    source = pl.multiple_of(own_col * B, B)
                    target = pl.multiple_of(col_block * B, B)
                    patch[:, pl.ds(target, B)] = cur[here, pl.ds(source, B)]


def pack(value):
    return jnp.concatenate([value[:PART // 2], value[PART // 2:]], axis=1)


def unpack(value):
    return jnp.concatenate([value[:, :B], value[:, B:]], axis=0)


def twice(value):
    zero = jnp.zeros_like(value)
    return jnp.concatenate(
        [jnp.concatenate([value, zero], axis=1), jnp.concatenate([zero, value], axis=1)], axis=0)


def update_kernel(turn, last, first, pieces, matrix, t_hi, t_lo, c_hi, c_lo, upper, patch, *refs):
    if turn > 0:
        refs = refs[1:]
    out, rows, panel_hi, panel_lo, panel, sem_in, sem_out, sem_patch = refs
    k0, p, q, own_col, own_row, col_block, row_block = place(first)
    starts = [n * SHARE + turn * HALF for n in range(N_COL)]
    ins = [pltpu.make_async_copy(matrix.at[pl.ds(s, HALF)], rows.at[pl.ds(n * HALF, HALF)], sem_in.at[n])
           for n, s in enumerate(starts)]
    for copy in ins:
        copy.start()
    tiles = [(s, min(TILE, COLS - s)) for s in range(0, COLS, TILE)]
    diagonal = [tuple(twice(v) for v in split(upper[t])) for t in range(STEPS)]
    beside = [tuple(twice(c[t * B:(t + 1) * B, (t + 1) * B:(t + 2) * B]) for c in (c_hi, c_lo))
              for t in range(0, STEPS, 2)]
    outs = []
    for s in range(2):
        span = slice(s * PART, (s + 1) * PART)
        block = jnp.concatenate(
            [lax.broadcasted_iota(jnp.int32, (HALF, B), 0) + starts[s * 8 + n] for n in range(8)], axis=0)
        block = (block >> 7) * N_ROW + p
        for pair in range(STEPS // 2):
            t = 2 * pair
            raw = [jnp.concatenate([pieces[s * 8 + n, t + u] for n in range(8)], axis=0) for u in range(2)]
            if pair > 0:
                both = slice(t * B, (t + 2) * B)
                change = dot3((panel_hi[span, :t * B], panel_lo[span, :t * B]),
                              (c_hi[:t * B, both], c_lo[:t * B, both]))
                raw = [raw[0] - change[:, :B], raw[1] - change[:, B:]]
            value = unpack(dot3(split(pack(raw[0])), diagonal[t]))
            value = jnp.where(block > k0 + t, value, 0.0)
            parts = split(value)
            later = pack(raw[1]) - dot3((pack(parts[0]), pack(parts[1])), beside[pair])
            value_next = unpack(dot3(split(later), diagonal[t + 1]))
            value_next = jnp.where(block > k0 + t + 1, value_next, 0.0)
            parts_next = split(value_next)
            for u, (step_value, step_parts) in enumerate(((value, parts), (value_next, parts_next))):
                lanes = slice((t + u) * B, (t + u + 1) * B)
                panel_hi[span, lanes] = step_parts[0]
                panel_lo[span, lanes] = step_parts[1]

                @pl.when(own_col == t + u)
                def _():
                    panel[span, :] = step_value
        for n in range(8):
            ins[s * 8 + n].wait()
        high = panel_hi[span, :]
        low = panel_lo[span, :]
        for n, (start, size) in enumerate(tiles):
            stop = start + size
            rows[span, start:stop] -= dot3((high, low), (t_hi[:, start:stop], t_lo[:, start:stop]))

            @pl.when((own_col < STEPS) & (lax.div(col_block * B, TILE) == n))
            def _():
                lanes = pl.ds(pl.multiple_of(col_block * B, B), B)
                rows[span, lanes] = jnp.where(block > k0 + own_col, panel[span, :], rows[span, lanes])
            for m in range(s * 8, s * 8 + 8):
                outs.append(pltpu.make_async_copy(
                    rows.at[pl.ds(m * HALF, HALF), pl.ds(start, size)],
                    out.at[pl.ds(starts[m], HALF), pl.ds(start, size)], sem_out.at[n, m]))
                outs[-1].start()
    for copy in outs:
        copy.wait()
    if last:
        @pl.when(own_row < STEPS)
        def _():
            copy = pltpu.make_async_copy(
                patch, out.at[pl.ds(pl.multiple_of(row_block * B, B), B)], sem_patch)
            copy.start()
            copy.wait()


def shards(matrix, first_step, lower_inverse, upper_inverse):
    def shape(*dims, dtype=F32):
        return jax.ShapeDtypeStruct(dims, dtype)

    dma = pltpu.SemaphoreType.DMA
    messages, top = pl.pallas_call(
        send_kernel,
        out_shape=[shape(N_COL, SHARE + B, B), shape(2, 64, COLS)],
        in_specs=[SM, ANY], out_specs=[ANY] * 2,
        scratch_shapes=[dma((2 * N_COL + 2,))], compiler_params=params(8),
    )(first_step, matrix)

    swap = [(i, i ^ 1) for i in range(N_ROW)]

    def along_z(value, distance):
        return lax.ppermute(value, "row", [(i, (i + 2 * distance) % N_ROW) for i in range(N_ROW)])

    def near_of(value):
        return along_z(value, 1), along_z(value, 3)

    def rest_of(value, near):
        ahead, back = near
        far = jnp.stack([along_z(ahead[0], 1), along_z(back[1], 3)])
        near = jnp.stack([ahead, back])
        mine = (value, near, far)
        return mine + tuple(lax.ppermute(v, "row", swap) for v in mine)

    near = near_of(top)
    got = lax.all_to_all(messages, "col", 0, 0)
    one, two, corner = pl.pallas_call(
        select_kernel,
        out_shape=[shape(STEPS, HALF, B)] * 2 + [shape(B, WIDE)],
        in_specs=[SM, ANY], out_specs=[ANY] * 3,
        scratch_shapes=[dma((STEPS, 3))], compiler_params=params(8),
    )(first_step, got)
    all_one = lax.all_gather(one, "col")
    all_two = lax.all_gather(two, "col")
    corner = corner.reshape(2, 64, WIDE)
    corners = rest_of(corner, near_of(corner))
    tops = rest_of(top, near)

    t_hi, t_lo, c_hi, c_lo, patch = pl.pallas_call(
        factor_kernel,
        out_shape=[shape(WIDE, COLS, dtype=BF16)] * 2 + [shape(WIDE, WIDE, dtype=BF16)] * 2 + [shape(B, COLS)],
        in_specs=[SM, VM, VM] + [ANY] * 12, out_specs=[VM] * 5,
        scratch_shapes=[pltpu.VMEM((WIDE, WIDE + COLS), F32), dma((STEPS, 2)), dma((STEPS, 2))],
        compiler_params=params(24),
        cost_estimate=pl.CostEstimate(flops=6_000_000_000, bytes_accessed=12_000_000, transcendentals=0),
    )(first_step, lower_inverse, upper_inverse, *corners, *tops)

    count = 2 * PART
    out = None
    for turn, pieces in enumerate((all_one, all_two)):
        held = [] if out is None else [out]
        out = pl.pallas_call(
            functools.partial(update_kernel, turn, turn == 1),
            out_shape=shape(ROWS, COLS),
            in_specs=[SM, VM, ANY] + [VM] * 5 + [ANY] + [ANY] * len(held), out_specs=ANY,
            input_output_aliases={9: 0} if held else {},
            scratch_shapes=[pltpu.VMEM((count, COLS), F32), pltpu.VMEM((count, WIDE), BF16),
                            pltpu.VMEM((count, WIDE), BF16), pltpu.VMEM((count, B), F32),
                            dma((N_COL,)), dma((5, N_COL)), dma],
            compiler_params=params(36),
            cost_estimate=pl.CostEstimate(flops=12_000_000_000, bytes_accessed=20_000_000, transcendentals=0),
        )(first_step, pieces, matrix, t_hi, t_lo, c_hi, c_lo, upper_inverse, patch, *held)
    return out


def solution(mesh):
    placed = (P("row", "col"), P(), P(), P())
    return jax.shard_map(
        shards, mesh=mesh, in_specs=placed, out_specs=P("row", "col"), check_vma=False
    )
```

```python
import functools

import jax
import jax.numpy as jnp
from jax import lax
from jax.experimental import pallas as pl
from jax.experimental.pallas import tpu as pltpu
from jax.sharding import PartitionSpec as P

B = 128
STEPS = 6
ROWS = 2304
COLS = 1152
GROUP = 288
SHARE = 144
HALF = 72
N_ROW = 8
N_COL = 16
WIDE = STEPS * B
CHUNK = 8 * SHARE
PART = CHUNK // 2
TILE = 256

F32 = jnp.float32
BF16 = jnp.bfloat16
ANY = pl.BlockSpec(memory_space=pl.ANY)
VM = pl.BlockSpec(memory_space=pltpu.VMEM)
SM = pl.BlockSpec(memory_space=pltpu.SMEM)


def params(mebibytes):
    return pltpu.CompilerParams(vmem_limit_bytes=mebibytes * 1024 * 1024)


def split(value):
    high = value.astype(BF16)
    low = (value - high.astype(F32)).astype(BF16)
    return high, low


def mul(left, right):
    return jnp.dot(left, right, preferred_element_type=F32)


def dot3(left, right):
    lh, ll = left
    rh, rl = right
    return mul(lh, rh) + (mul(ll, rh) + mul(lh, rl))


def place(first):
    k0 = first[0]
    p = lax.axis_index("row")
    q = lax.axis_index("col")
    own_col = lax.rem(q - k0 + 8 * N_COL, N_COL)
    own_row = lax.rem(p - k0 + 16 * N_ROW, N_ROW)
    col_block = lax.div(k0 + jnp.minimum(own_col, STEPS - 1), N_COL)
    row_block = lax.div(k0 + jnp.minimum(own_row, STEPS - 1), N_ROW)
    return k0, p, q, own_col, own_row, col_block, row_block


def held(offset, slot):
    pick = lambda a, b, c, d, e: jnp.where(
        offset < 6, a, jnp.where(offset < 10, b, jnp.where(offset < 12, c, jnp.where(offset < 14, d, e))))
    if slot < 2:
        step = pick(offset, offset - 4, offset - 10, offset - 12, offset - 12)
        group = pick(slot, 3 + slot, 6 + slot, 3 + slot, 6 + slot)
    else:
        step = pick(offset, offset - 4, offset - 6, offset - 12, offset - 10)
        group = pick(slot, 3 + slot, 7, 3 + slot, 6)
    return step, group


def send_kernel(first, matrix, corner, keep, ahead, back, ten, six, top, sem):
    k0, p, q, own_col, own_row, col_block, row_block = place(first)
    lanes = pl.ds(pl.multiple_of(col_block * B, B), B)
    pivot = pl.multiple_of(row_block * B, B)

    def group(g, target, n):
        rows = g * GROUP if isinstance(g, int) else pl.multiple_of(g * GROUP, 8)
        return pltpu.make_async_copy(matrix.at[pl.ds(rows, GROUP), lanes], target, sem.at[n])

    first_back = jnp.where(own_col < 2, 3, 6)
    copies = [pltpu.make_async_copy(matrix.at[pl.ds(pivot, B), lanes], corner, sem.at[0])]
    copies += [group(3 + n, ahead.at[n], 1 + n) for n in range(3)]
    copies += [group(jnp.minimum(first_back + n, 7), back.at[n], 4 + n) for n in range(3)]
    copies += [group(6 + n, ten.at[n], 7 + n) for n in range(2)]
    copies += [group(7, six.at[0], 9)]
    copies += [group(n, keep.at[n], 10 + n) for n in range(3)]
    copies += [pltpu.make_async_copy(matrix.at[pl.ds(pivot + h * 64, 64)], top.at[h], sem.at[13 + h])
               for h in range(2)]
    for copy in copies:
        copy.start()
    for copy in copies:
        copy.wait()


def pick(refs, index, target, sem):
    for n, ref in enumerate(refs):
        @pl.when(index == n)
        def _():
            pltpu.make_async_copy(ref, target, sem).start()
    return pltpu.make_async_copy(refs[0], target, sem)


def column_kernel(first, *refs):
    pieces, two, sem = refs[:4], refs[4], refs[5]
    offset = place(first)[3]
    residue = lax.rem(offset, 4)
    waits = []
    for u in range(2):
        distance = lax.rem(lax.div(offset - residue, 4) - u + 4, 4)
        waits.append(pick(pieces, distance, two.at[u], sem.at[u]))
    for wait in waits:
        wait.wait()


def row_kernel(first, *refs):
    pieces, corner, sem = refs[:4], refs[4], refs[5]
    offset = place(first)[3]
    waits = []
    for t in range(STEPS):
        distance = lax.rem(offset - t + 8, 4)
        for h in range(2):
            waits.append(pick([piece.at[t // 4, pl.ds(h * 64, 64)] for piece in pieces], distance,
                              corner.at[h, :, pl.ds(t * B, B)], sem.at[t, h]))
    for wait in waits:
        wait.wait()


def share_kernel(first, keep, ahead, back, ten, six, one, two, rest, sem):
    offset = place(first)[3]
    targets = [(one, 0, HALF), (two, HALF, HALF), (rest, SHARE, SHARE)]

    def take(sources):
        for i, (ref, slot) in enumerate(sources):
            for n, (target, start, size) in enumerate(targets):
                pltpu.make_async_copy(ref.at[slot, pl.ds(start, size)], target.at[i], sem.at[i, n]).start()

    cases = [(offset < 6, [(keep, 0), (keep, 1), (keep, 2)]),
             ((offset >= 6) & (offset < 10), [(ahead, 0), (ahead, 1), (ahead, 2)]),
             ((offset >= 10) & (offset < 12), [(ten, 0), (ten, 1), (six, 0)]),
             ((offset >= 12) & (offset < 14), [(back, 0), (back, 1), (back, 2)]),
             (offset >= 14, [(back, 0), (back, 1), (ten, 0)])]
    for case, sources in cases:
        @pl.when(case)
        def _():
            take(sources)
    for i in range(3):
        for n, (target, start, size) in enumerate(targets):
            pltpu.make_async_copy(keep.at[i, pl.ds(start, size)], target.at[i], sem.at[i, n]).wait()


def ring_pieces(own, near, far):
    return [(own.at[0], own.at[1]), (near.at[0, 0], near.at[0, 1]),
            (far.at[0], far.at[1]), (near.at[1, 0], near.at[1, 1])]


def pivot_rows(first, refs, lanes, target, sem):
    k0, p = first[0], lax.axis_index("row")
    z = lax.div(p, 2)
    core = lax.rem(p, 2)
    pieces = ring_pieces(*refs[0:3]) + ring_pieces(*refs[3:6])
    waits = []
    for a in range(STEPS):
        source = lax.rem(k0 + a, N_ROW)
        dz = lax.rem(z - lax.div(source, 2) + 4, 4)
        index = jnp.where(lax.rem(source, 2) == core, 0, 4) + dz
        for h in range(2):
            waits.append(pick([piece[h] for piece in pieces], index,
                              target.at[pl.ds(a * B + h * 64, 64), pl.ds(0, lanes)], sem.at[a, h]))
    return waits


def factor_kernel(first, lower, upper, *refs):
    c_hi, c_lo, p_hi, p_lo, cur, sem = refs[6:]
    waits = pivot_rows(first, refs[:6], WIDE, cur, sem)
    for wait in waits:
        wait.wait()
    for t in range(STEPS - 1):
        here = slice(t * B, (t + 1) * B)
        after = slice((t + 1) * B, WIDE)
        tops = split(dot3(split(lower[t]), split(cur[here, after])))
        panels = split(dot3(split(cur[after, here]), split(upper[t])))
        c_hi[here, after], c_lo[here, after] = tops
        p_hi[after, here], p_lo[after, here] = panels
        cur[after, after] -= dot3(panels, tops)


def top_kernel(first, lower, p_hi, p_lo, *refs):
    t_hi, t_lo, patch, cur, sem = refs[6:]
    k0, p, q, own_col, own_row, col_block, row_block = place(first)
    waits = pivot_rows(first, refs[:6], COLS, cur, sem)
    for wait in waits:
        wait.wait()
    lane_block = (lax.broadcasted_iota(jnp.int32, (1, COLS), 1) >> 7) * N_COL + q
    for t in range(STEPS):
        here = slice(t * B, (t + 1) * B)
        after = slice((t + 1) * B, WIDE)
        rows = cur[here, :]
        live = lane_block > k0 + t
        top = jnp.where(live, dot3(split(lower[t]), split(rows)), 0.0)
        tops = split(top)
        t_hi[here, :], t_lo[here, :] = tops

        @pl.when(own_row == t)
        def _():
            patch[...] = jnp.where(live, top, cur[here, :])
            if t > 0:
                @pl.when(own_col < t)
                def _():
                    source = pl.ds(pl.multiple_of(own_col * B, B), B)
                    target = pl.ds(pl.multiple_of(col_block * B, B), B)
                    patch[:, target] = p_hi[here, source].astype(F32) + p_lo[here, source].astype(F32)
        if t + 1 < STEPS:
            cur[after, :] -= dot3((p_hi[after, here], p_lo[after, here]), tops)


def pack(value):
    return jnp.concatenate([value[:PART // 2], value[PART // 2:]], axis=1)


def unpack(value):
    return jnp.concatenate([value[:, :B], value[:, B:]], axis=0)


def twice(value):
    zero = jnp.zeros_like(value)
    return jnp.concatenate(
        [jnp.concatenate([value, zero], axis=1), jnp.concatenate([zero, value], axis=1)], axis=0)


def update_kernel(turn, last, first, matrix, t_hi, t_lo, c_hi, c_lo, upper, patch, *refs):
    count = 1 if last else 16
    pieces, refs = refs[:count], refs[count:]
    if last:
        refs = refs[1:]
    (out, raw, rows, panels, panel, tops, corner,
     sem_raw, sem_in, sem_top, sem_corner, sem_out, sem_patch) = refs
    k0, p, q, own_col, own_row, col_block, row_block = place(first)
    x = lax.div(q, 4)
    y = lax.rem(q, 4)
    corner_in = [pltpu.make_async_copy(ref, corner.at[n], sem_corner.at[n]) for n, ref in enumerate((c_hi, c_lo))]
    raw_in = []

    def bring(ref, source, start, size):
        offset = lax.rem(source - k0 + 8 * N_COL, N_COL)
        for i in range(3):
            step, group = held(offset, i)
            target = raw.at[pl.ds(pl.multiple_of(group * SHARE + start, 8), size),
                            pl.ds(pl.multiple_of(step * B, B), B)]
            raw_in.append(pltpu.make_async_copy(ref.at[i], target, sem_raw.at[len(raw_in)]))

    if last:
        for source in range(N_COL):
            bring(pieces[0].at[source], source, 0, SHARE)
    else:
        for h in range(2):
            for near in range(4):
                for d in range(4):
                    dx, dy = (d, near) if h == 0 else (near, d)
                    source = lax.rem(x + 4 - dx, 4) * 4 + lax.rem(y + 4 - dy, 4)
                    bring(pieces[8 * h + 2 * near + d // 2].at[d % 2], source, h * HALF, HALF)
    starts = [g * GROUP + turn * SHARE for g in range(8)]
    ins = [pltpu.make_async_copy(matrix.at[pl.ds(s, SHARE)], rows.at[pl.ds(g * SHARE, SHARE)], sem_in.at[g])
           for g, s in enumerate(starts)]
    tops_in = [pltpu.make_async_copy(ref, tops.at[pl.ds(n * WIDE, WIDE)], sem_top.at[n])
               for n, ref in enumerate((t_hi, t_hi, t_lo))]
    for copy in corner_in + raw_in + ins + tops_in:
        copy.start()
    tiles = [(s, min(TILE, COLS - s)) for s in range(0, COLS, TILE)]
    diagonal = [tuple(twice(v) for v in split(upper[t])) for t in range(STEPS)]
    for copy in corner_in:
        copy.wait()
    beside = [tuple(twice(corner[n, t * B:(t + 1) * B, (t + 1) * B:(t + 2) * B]) for n in range(2))
              for t in range(0, STEPS, 2)]
    for copy in raw_in:
        copy.wait()
    outs = []
    for s in range(2):
        span = slice(s * PART, (s + 1) * PART)
        block = jnp.concatenate(
            [lax.broadcasted_iota(jnp.int32, (SHARE, B), 0) + starts[4 * s + g] for g in range(4)], axis=0)
        block = (block >> 7) * N_ROW + p
        for pair in range(STEPS // 2):
            t = 2 * pair
            both = slice(t * B, (t + 2) * B)
            now = raw[span, both]
            if pair > 0:
                now = now - dot3((panels[span, :t * B], panels[span, WIDE:WIDE + t * B]),
                                 (corner[0, :t * B, both], corner[1, :t * B, both]))
            value = unpack(dot3(split(pack(now[:, :B])), diagonal[t]))
            value = jnp.where(block > k0 + t, value, 0.0)
            parts = split(value)
            later = pack(now[:, B:]) - dot3((pack(parts[0]), pack(parts[1])), beside[pair])
            value_next = unpack(dot3(split(later), diagonal[t + 1]))
            value_next = jnp.where(block > k0 + t + 1, value_next, 0.0)
            parts_next = split(value_next)
            for u, (step_value, step_parts) in enumerate(((value, parts), (value_next, parts_next))):
                for n, part in enumerate((step_parts[0], step_parts[1], step_parts[0])):
                    panels[span, n * WIDE + (t + u) * B:n * WIDE + (t + u + 1) * B] = part

                @pl.when(own_col == t + u)
                def _():
                    panel[span, :] = step_value
        for g in range(4):
            ins[4 * s + g].wait()
        if s == 0:
            for copy in tops_in:
                copy.wait()
        left = panels[span, :]
        for n, (start, size) in enumerate(tiles):
            lanes = slice(start, start + size)
            rows[span, lanes] -= mul(left, tops[:, lanes])

            @pl.when((own_col < STEPS) & (lax.div(col_block * B, TILE) == n))
            def _():
                own = pl.ds(pl.multiple_of(col_block * B, B), B)
                rows[span, own] = jnp.where(block > k0 + own_col, panel[span, :], rows[span, own])
            for g in range(4 * s, 4 * s + 4):
                outs.append(pltpu.make_async_copy(
                    rows.at[pl.ds(g * SHARE, SHARE), pl.ds(start, size)],
                    out.at[pl.ds(starts[g], SHARE), pl.ds(start, size)], sem_out.at[n, g]))
                outs[-1].start()
    for copy in outs:
        copy.wait()
    if last:
        @pl.when(own_row < STEPS)
        def _():
            copy = pltpu.make_async_copy(
                patch, out.at[pl.ds(pl.multiple_of(row_block * B, B), B)], sem_patch)
            copy.start()
            copy.wait()


def shards(matrix, first_step, lower_inverse, upper_inverse):
    def shape(*dims, dtype=F32):
        return jax.ShapeDtypeStruct(dims, dtype)

    dma = pltpu.SemaphoreType.DMA

    def small(kernel, outs, sems, *args):
        return pl.pallas_call(
            kernel, out_shape=outs, in_specs=[SM] + [ANY] * len(args), out_specs=[ANY] * len(outs),
            scratch_shapes=[dma(sems)], compiler_params=params(48),
        )(first_step, *args)

    def spin(value, distance):
        return lax.ppermute(value, "col", [(i, (i + distance) % N_COL) for i in range(N_COL)])

    def along_x(value, distance):
        return spin(value, 4 * distance)

    def along_y(value, distance):
        return lax.ppermute(value, "col", [(i, i // 4 * 4 + (i + distance) % 4) for i in range(N_COL)])

    def along_z(value, distance):
        return lax.ppermute(value, "row", [(i, (i + 2 * distance) % N_ROW) for i in range(N_ROW)])

    def swap(value):
        return lax.ppermute(value, "row", [(i, i ^ 1) for i in range(N_ROW)])

    def around(move, value):
        return [value] + [move(value, d) for d in (1, 2, 3)]

    def depth(value):
        ahead, back = along_z(value, 1), along_z(value, 3)
        far = jnp.stack([along_z(ahead[0], 1), along_z(back[1], 3)])
        mine = (value, jnp.stack([ahead, back]), far)
        return mine + tuple(swap(v) for v in mine)

    def ring(move, pieces):
        a, b = jnp.stack(pieces[:2]), jnp.stack(pieces[2:])
        a1, b1 = move(a, 1), move(b, 1)
        a3, b3 = move(a, 3), move(b, 3)
        a2, b2 = move(a1, 1), move(b3, 3)
        return [a, b, a1, b1, a2, b2, a3, b3]

    corner, keep, ahead, back, ten, six, top = small(
        send_kernel,
        [shape(B, B)] + [shape(n, GROUP, B) for n in (3, 3, 3, 2, 1)] + [shape(2, 64, COLS)],
        (15,), matrix)

    corner = around(along_x, corner)
    ahead, back, ten, six = spin(ahead, 4), spin(back, 12), spin(ten, 10), spin(six, 6)
    corner, = small(column_kernel, [shape(2, B, B)], (2,), *corner)
    corner, = small(row_kernel, [shape(2, 64, WIDE)], (STEPS, 2), *around(along_y, corner))
    corners = depth(corner)
    tops = depth(top)

    one, two, rest = small(
        share_kernel, [shape(3, HALF, B)] * 2 + [shape(3, SHARE, B)], (3, 3), keep, ahead, back, ten, six)
    rest = lax.all_gather(rest, "col")
    near = ring(along_y, around(along_x, one)) + ring(along_x, around(along_y, two))

    c_hi, c_lo, p_hi, p_lo = pl.pallas_call(
        factor_kernel,
        out_shape=[shape(WIDE, WIDE, dtype=BF16)] * 4,
        in_specs=[SM, VM, VM] + [ANY] * 6, out_specs=[VM] * 4,
        scratch_shapes=[pltpu.VMEM((WIDE, WIDE), F32), dma((STEPS, 2))],
        compiler_params=params(48),
        cost_estimate=pl.CostEstimate(flops=4_000_000_000, bytes_accessed=8_000_000, transcendentals=0),
    )(first_step, lower_inverse, upper_inverse, *corners)
    t_hi, t_lo, patch = pl.pallas_call(
        top_kernel,
        out_shape=[shape(WIDE, COLS, dtype=BF16)] * 2 + [shape(B, COLS)],
        in_specs=[SM, VM, VM, VM] + [ANY] * 6, out_specs=[VM] * 3,
        scratch_shapes=[pltpu.VMEM((WIDE, COLS), F32), dma((STEPS, 2))],
        compiler_params=params(48),
        cost_estimate=pl.CostEstimate(flops=4_000_000_000, bytes_accessed=8_000_000, transcendentals=0),
    )(first_step, lower_inverse, p_hi, p_lo, *tops)

    out = []
    for turn, pieces in enumerate((near, [rest])):
        out = [pl.pallas_call(
            functools.partial(update_kernel, turn, turn == 1),
            out_shape=shape(ROWS, COLS),
            in_specs=[SM] + [ANY] * 5 + [VM] + [ANY] * (1 + len(pieces) + len(out)), out_specs=ANY,
            input_output_aliases={8 + len(pieces): 0} if out else {},
            scratch_shapes=[pltpu.VMEM((CHUNK, WIDE), F32), pltpu.VMEM((CHUNK, COLS), F32),
                            pltpu.VMEM((CHUNK, 3 * WIDE), BF16), pltpu.VMEM((CHUNK, B), F32),
                            pltpu.VMEM((3 * WIDE, COLS), BF16), pltpu.VMEM((2, WIDE, WIDE), BF16),
                            dma((96,)), dma((8,)), dma((3,)), dma((2,)), dma((5, 8)), dma],
            compiler_params=params(56),
            cost_estimate=pl.CostEstimate(flops=12_000_000_000, bytes_accessed=20_000_000, transcendentals=0),
        )(first_step, matrix, t_hi, t_lo, c_hi, c_lo, upper_inverse, patch, *pieces, *out)]
    return out[0]


def solution(mesh):
    placed = (P("row", "col"), P(), P(), P())
    return jax.shard_map(
        shards, mesh=mesh, in_specs=placed, out_specs=P("row", "col"), check_vma=False
    )
```

```python
import functools

import jax
import jax.numpy as jnp
from jax import lax
from jax.experimental import pallas as pl
from jax.experimental.pallas import tpu as pltpu
from jax.sharding import PartitionSpec as P

B = 128
STEPS = 6
ROWS = 2304
COLS = 1152
SHARE = 144
HALF = 72
N_ROW = 8
N_COL = 16
WIDE = STEPS * B
PART = 8 * HALF
OUTER = COLS + B
SAFE = 100.0
TILE = 256

F32 = jnp.float32
BF16 = jnp.bfloat16
ANY = pl.BlockSpec(memory_space=pl.ANY)
VM = pl.BlockSpec(memory_space=pltpu.VMEM)
SM = pl.BlockSpec(memory_space=pltpu.SMEM)


def params(mebibytes):
    return pltpu.CompilerParams(vmem_limit_bytes=mebibytes * 1024 * 1024)


def split(value):
    high = value.astype(BF16)
    low = (value - high.astype(F32)).astype(BF16)
    return high, low


def mul(left, right):
    return jnp.dot(left, right, preferred_element_type=F32)


def dot3(left, right):
    lh, ll = left
    rh, rl = right
    return mul(lh, rh) + (mul(ll, rh) + mul(lh, rl))


def place(first):
    k0 = first[0]
    p = lax.axis_index("row")
    q = lax.axis_index("col")
    own_col = lax.rem(q - k0 + 8 * N_COL, N_COL)
    own_row = lax.rem(p - k0 + 16 * N_ROW, N_ROW)
    col_block = lax.div(k0 + jnp.minimum(own_col, STEPS - 1), N_COL)
    row_block = lax.div(k0 + jnp.minimum(own_row, STEPS - 1), N_ROW)
    return k0, p, q, own_col, own_row, col_block, row_block


def send_kernel(first, matrix, messages, top, sem):
    k0, p, q, own_col, own_row, col_block, row_block = place(first)
    lanes = pl.ds(pl.multiple_of(col_block * B, B), B)
    pivot = pl.ds(pl.multiple_of(row_block * B, B), B)
    copies = [pltpu.make_async_copy(matrix.at[pivot], top, sem.at[2 * N_COL])]
    for j in range(N_COL):
        copies.append(pltpu.make_async_copy(
            matrix.at[pivot, lanes], messages.at[j, pl.ds(SHARE, B)], sem.at[2 * j]))
        copies.append(pltpu.make_async_copy(
            matrix.at[pl.ds(j * SHARE, SHARE), lanes], messages.at[j, pl.ds(0, SHARE)], sem.at[2 * j + 1]))
    for copy in copies:
        copy.start()
    for copy in copies:
        copy.wait()


def select_kernel(first, messages, corner, one, two, sem):
    k0 = first[0]
    copies = []
    for t in range(STEPS):
        owner = lax.rem(k0 + t, N_COL)
        lanes = pl.ds(t * B, B)
        for n, (target, start, size) in enumerate((
                (corner.at[0, :, lanes], SHARE, 64), (corner.at[1, :, lanes], SHARE + 64, 64),
                (one.at[:, lanes], 0, HALF), (two.at[:, lanes], HALF, HALF))):
            copies.append(pltpu.make_async_copy(messages.at[owner, pl.ds(start, size)], target, sem.at[t, n]))
    for copy in copies:
        copy.start()
    for copy in copies:
        copy.wait()


def pick(refs, index, target, sem):
    for n, ref in enumerate(refs):
        @pl.when(index == n)
        def _():
            pltpu.make_async_copy(ref, target, sem).start()
    return pltpu.make_async_copy(refs[0], target, sem)


def ring_pieces(own, near, far):
    return [(own.at[0], own.at[1]), (near.at[0, 0], near.at[0, 1]),
            (far.at[0], far.at[1]), (near.at[1, 0], near.at[1, 1])]


def bring_corner(first, refs, target, sem):
    k0, p = first[0], lax.axis_index("row")
    z = lax.div(p, 2)
    core = lax.rem(p, 2)
    pieces = ring_pieces(*refs[0:3]) + ring_pieces(*refs[3:6])
    waits = []
    for a in range(STEPS):
        source = lax.rem(k0 + a, N_ROW)
        dz = lax.rem(z - lax.div(source, 2) + 4, 4)
        index = jnp.where(lax.rem(source, 2) == core, 0, 4) + dz
        for h in range(2):
            waits.append(pick([piece[h] for piece in pieces], index,
                              target.at[pl.ds(a * B + h * 64, 64)], sem.at[a, h]))
    for wait in waits:
        wait.wait()


def bring_tops(first, tops, target, sem):
    copies = []
    for a in range(STEPS):
        source = lax.rem(first[0] + a, N_ROW)
        copies.append(pltpu.make_async_copy(tops.at[source], target.at[pl.ds(a * B, B)], sem.at[a]))
    for copy in copies:
        copy.start()
    for copy in copies:
        copy.wait()


def largest(value):
    value = jnp.abs(value)
    return jnp.max(value.reshape(-1, 8, value.shape[-1]), axis=0)


def corner_kernel(first, lower, upper, *refs):
    z_hi, z_lo, m_hi, m_lo, n_hi, n_lo, special, safe, cur, panel, sem = refs[6:]
    k0, p, q, own_col, own_row, col_block, row_block = place(first)
    bring_corner(first, refs[:6], cur, sem)
    ones = jnp.where(lax.broadcasted_iota(jnp.int32, (B, B), 0) == lax.broadcasted_iota(jnp.int32, (B, B), 1),
                     jnp.float32(1.0), jnp.float32(0.0))
    above = lax.broadcasted_iota(jnp.int32, (WIDE, B), 0)
    before = lax.broadcasted_iota(jnp.int32, (B, WIDE), 1)
    peak_col = jnp.zeros((8, B), F32)
    peak_row = jnp.zeros((8, WIDE), F32)
    for t in range(STEPS):
        here = slice(t * B, (t + 1) * B)
        diagonal = cur[here, here]
        cur[here, here] = ones
        left = dot3(split(cur[:, here]), split(upper[t]))
        right = dot3(split(lower[t]), split(cur[here, :]))
        lefts = split(left)
        rights = split(right)
        peak_col = jnp.maximum(peak_col, largest(left))
        peak_row = jnp.maximum(peak_row, largest(right))

        @pl.when(own_col == t)
        def _():
            panel[...] = left
            m_hi[...], m_lo[...] = split(jnp.where(above < (t + 1) * B, left, 0.0))

        @pl.when(own_row == t)
        def _():
            n_hi[...], n_lo[...] = split(jnp.where(before < (t + 1) * B, right, 0.0))

            @pl.when(own_col == t)
            def _():
                special[...] = diagonal
        cur[:, here] = jnp.zeros((WIDE, B), F32)
        cur[here, :] = jnp.zeros((B, WIDE), F32)
        cur[...] -= dot3(lefts, rights)

    @pl.when((own_col < own_row) & (own_row < STEPS))
    def _():
        special[...] = panel[pl.ds(pl.multiple_of(own_row * B, B), B), :]
    z_hi[...], z_lo[...] = split(cur[...])
    peak = jnp.maximum(jnp.max(peak_col), jnp.max(peak_row))
    safe[0] = jnp.where(peak < SAFE, 1, 0)


def top_kernel(first, z_hi, z_lo, m_hi, m_lo, n_hi, n_lo, special, tops, w_hi, w_lo, patch, cur, sem):
    k0, p, q, own_col, own_row, col_block, row_block = place(first)
    bring_tops(first, tops, cur, sem)
    own = pl.ds(pl.multiple_of(jnp.minimum(own_row, STEPS - 1) * B, B), B)
    zs = (z_hi[...], z_lo[...])
    ns = (n_hi[...], n_lo[...])
    for start in range(0, COLS, TILE):
        size = min(TILE, COLS - start)
        lanes = slice(start, start + size)
        block = ((lax.broadcasted_iota(jnp.int32, (1, size), 1) + start) >> 7) * N_COL + q
        rows = split(cur[:, lanes])
        w_hi[:, lanes], w_lo[:, lanes] = split(jnp.where(block > k0 + STEPS - 1, dot3(zs, rows), 0.0))
        patch[:, lanes] = jnp.where(block > k0 + own_row, dot3(ns, rows), cur[own, lanes])
    w_hi[:, COLS:] = m_hi[...]
    w_lo[:, COLS:] = m_lo[...]

    @pl.when((own_col <= own_row) & (own_row < STEPS))
    def _():
        patch[:, pl.ds(pl.multiple_of(col_block * B, B), B)] = special[...]


def piece_start(n, x, y):
    h = lax.div(n, 16)
    near = lax.div(lax.rem(n, 16), 4)
    d = lax.rem(n, 4)
    dx = jnp.where(h == 0, d, near)
    dy = jnp.where(h == 0, near, d)
    owner = lax.rem(x + 4 - dx, 4) * 4 + lax.rem(y + 4 - dy, 4)
    return pl.multiple_of(owner * SHARE + h * HALF, 8)


def piece_copies(pieces, matrix, out, raw, rows, sem_raw, sem_in, sem_out):
    q = lax.axis_index("col")
    x = lax.div(q, 4)
    y = lax.rem(q, 4)
    raws, ins, outs = [], [], []
    for n in range(32):
        here = pl.ds(n * HALF, HALF)
        there = pl.ds(piece_start(n, x, y), HALF)
        raws.append(pltpu.make_async_copy(pieces[n // 2].at[n % 2], raw.at[here], sem_raw.at[n]))
        ins.append(pltpu.make_async_copy(matrix.at[there], rows.at[here], sem_in.at[n]))
        outs.append(pltpu.make_async_copy(rows.at[here], out.at[there], sem_out.at[n]))
    return raws, ins, outs


def row_blocks(s, p, x, y):
    block = jnp.concatenate([lax.broadcasted_iota(jnp.int32, (HALF, B), 0) + piece_start(8 * s + n, x, y)
                             for n in range(8)], axis=0)
    return (block >> 7) * N_ROW + p


def finish(outs, own_row, row_block, patch, out, sem):
    for copy in outs:
        copy.wait()

    @pl.when(own_row < STEPS)
    def _():
        copy = pltpu.make_async_copy(patch, out.at[pl.ds(pl.multiple_of(row_block * B, B), B)], sem)
        copy.start()
        copy.wait()


def update_kernel(first, patch, matrix, w_hi, w_lo, *refs):
    pieces = refs[:16]
    out, raw, rows, left, tops, sem_raw, sem_in, sem_out, sem_top, sem_patch = refs[16:]
    k0, p, q, own_col, own_row, col_block, row_block = place(first)
    x = lax.div(q, 4)
    y = lax.rem(q, 4)
    raws, ins, outs = piece_copies(pieces, matrix, out, raw, rows, sem_raw, sem_in, sem_out)
    tops_in = [pltpu.make_async_copy(ref, tops.at[pl.ds(n * WIDE, WIDE)], sem_top.at[n])
               for n, ref in enumerate((w_hi, w_hi, w_lo))]
    for copy in raws[:8] + tops_in + ins[:8]:
        copy.start()
    for s in range(1, 4):
        for copy in raws[8 * s:8 * s + 8] + ins[8 * s:8 * s + 8]:
            copy.start()
    own = pl.ds(pl.multiple_of(col_block * B, B), B)
    for s in range(4):
        span = slice(s * PART, (s + 1) * PART)
        live = row_blocks(s, p, x, y) > k0 + STEPS - 1
        for copy in raws[8 * s:8 * s + 8]:
            copy.wait()
        for t in range(STEPS):
            high, low = split(jnp.where(live, raw[span, t * B:(t + 1) * B], 0.0))
            for n, part in enumerate((high, low, high)):
                left[:, n * WIDE + t * B:n * WIDE + (t + 1) * B] = part
        if s == 0:
            for copy in tops_in:
                copy.wait()
        for copy in ins[8 * s:8 * s + 8]:
            copy.wait()
        value = left[...]
        for start in range(0, OUTER, TILE):
            change = mul(value, tops[:, start:start + TILE])
            if start + TILE <= COLS:
                rows[span, start:start + TILE] += change
            else:
                rows[span, start:COLS] += change[:, :B]

                @pl.when(own_col < STEPS)
                def _():
                    rows[span, own] = jnp.where(live, change[:, B:], rows[span, own])
        for copy in outs[8 * s:8 * s + 8]:
            copy.start()
    finish(outs, own_row, row_block, patch, out, sem_patch)


def stepwise_corner_kernel(first, lower, upper, *refs):
    c_hi, c_lo, p_hi, p_lo, cur, sem = refs[6:]
    bring_corner(first, refs[:6], cur, sem)
    for t in range(STEPS - 1):
        here = slice(t * B, (t + 1) * B)
        after = slice((t + 1) * B, WIDE)
        tops = split(dot3(split(lower[t]), split(cur[here, after])))
        panels = split(dot3(split(cur[after, here]), split(upper[t])))
        c_hi[here, after], c_lo[here, after] = tops
        p_hi[after, here], p_lo[after, here] = panels
        cur[after, after] -= dot3(panels, tops)


def stepwise_top_kernel(first, lower, p_hi, p_lo, tops, t_hi, t_lo, patch, cur, sem):
    k0, p, q, own_col, own_row, col_block, row_block = place(first)
    bring_tops(first, tops, cur, sem)
    lane_block = (lax.broadcasted_iota(jnp.int32, (1, COLS), 1) >> 7) * N_COL + q
    for t in range(STEPS):
        here = slice(t * B, (t + 1) * B)
        after = slice((t + 1) * B, WIDE)
        live = lane_block > k0 + t
        top = jnp.where(live, dot3(split(lower[t]), split(cur[here, :])), 0.0)
        tops = split(top)
        t_hi[here, :], t_lo[here, :] = tops

        @pl.when(own_row == t)
        def _():
            patch[...] = jnp.where(live, top, cur[here, :])
            if t > 0:
                @pl.when(own_col < t)
                def _():
                    source = pl.ds(pl.multiple_of(own_col * B, B), B)
                    target = pl.ds(pl.multiple_of(col_block * B, B), B)
                    patch[:, target] = p_hi[here, source].astype(F32) + p_lo[here, source].astype(F32)
        if t + 1 < STEPS:
            cur[after, :] -= dot3((p_hi[after, here], p_lo[after, here]), tops)


def stepwise_update_kernel(first, patch, upper, t_hi, t_lo, c_hi, c_lo, matrix, *refs):
    pieces = refs[:16]
    out, raw, rows, high, low, panel, sem_raw, sem_in, sem_out, sem_patch = refs[16:]
    k0, p, q, own_col, own_row, col_block, row_block = place(first)
    x = lax.div(q, 4)
    y = lax.rem(q, 4)
    raws, ins, outs = piece_copies(pieces, matrix, out, raw, rows, sem_raw, sem_in, sem_out)
    for copy in raws + ins:
        copy.start()
    for copy in raws + ins:
        copy.wait()
    own = pl.ds(pl.multiple_of(col_block * B, B), B)

    @pl.loop(0, 4)
    def _(s):
        span = pl.ds(pl.multiple_of(s * PART, PART), PART)
        block = row_blocks(s, p, x, y)
        for t in range(STEPS):
            lanes = slice(t * B, (t + 1) * B)
            value = raw[span, lanes]
            if t > 0:
                value = value - dot3((high[:, :t * B], low[:, :t * B]), (c_hi[:t * B, lanes], c_lo[:t * B, lanes]))
            value = jnp.where(block > k0 + t, dot3(split(value), split(upper[t])), 0.0)
            high[:, lanes], low[:, lanes] = split(value)

            @pl.when(own_col == t)
            def _():
                panel[...] = value
        for start in range(0, COLS, TILE):
            lanes = slice(start, min(start + TILE, COLS))
            rows[span, lanes] -= dot3((high[...], low[...]), (t_hi[:, lanes], t_lo[:, lanes]))

        @pl.when(own_col < STEPS)
        def _():
            rows[span, own] = jnp.where(block > k0 + own_col, panel[...], rows[span, own])
    for copy in outs:
        copy.start()
    finish(outs, own_row, row_block, patch, out, sem_patch)


def shards(matrix, first_step, lower_inverse, upper_inverse):
    def shape(*dims, dtype=F32):
        return jax.ShapeDtypeStruct(dims, dtype)

    dma = pltpu.SemaphoreType.DMA

    def call(kernel, outs, in_specs, out_specs, scratch, args, flops=1_000_000, megabytes=48):
        return pl.pallas_call(
            kernel, out_shape=outs, in_specs=[SM] + in_specs, out_specs=out_specs, scratch_shapes=scratch,
            compiler_params=params(megabytes),
            cost_estimate=pl.CostEstimate(flops=flops, bytes_accessed=4_000_000, transcendentals=0),
        )(first_step, *args)

    def along_x(value, distance):
        return lax.ppermute(value, "col", [(i, (i + 4 * distance) % N_COL) for i in range(N_COL)])

    def along_y(value, distance):
        return lax.ppermute(value, "col", [(i, i // 4 * 4 + (i + distance) % 4) for i in range(N_COL)])

    def along_z(value, distance):
        return lax.ppermute(value, "row", [(i, (i + 2 * distance) % N_ROW) for i in range(N_ROW)])

    def swap(value):
        return lax.ppermute(value, "row", [(i, i ^ 1) for i in range(N_ROW)])

    def depth(value):
        ahead, back = along_z(value, 1), along_z(value, 3)
        far = jnp.stack([along_z(ahead[0], 1), along_z(back[1], 3)])
        mine = (value, jnp.stack([ahead, back]), far)
        return mine + tuple(swap(v) for v in mine)

    def ring(move, pieces):
        a, b = jnp.stack(pieces[:2]), jnp.stack(pieces[2:])
        a1, b1 = move(a, 1), move(b, 1)
        a3, b3 = move(a, 3), move(b, 3)
        a2, b2 = move(a1, 1), move(b3, 3)
        return [a, b, a1, b1, a2, b2, a3, b3]

    messages, top = call(send_kernel, [shape(N_COL, SHARE + B, B), shape(B, COLS)], [ANY], [ANY] * 2,
                         [dma((2 * N_COL + 1,))], [matrix])
    tops = lax.all_gather(top, "row")
    got = lax.all_to_all(messages, "col", 0, 0)
    corner, one, two = call(select_kernel, [shape(2, 64, WIDE)] + [shape(HALF, WIDE)] * 2, [ANY], [ANY] * 3,
                            [dma((STEPS, 4))], [got])
    corners = depth(corner)
    pieces = (ring(along_y, [one] + [along_x(one, d) for d in (1, 2, 3)])
              + ring(along_x, [two] + [along_y(two, d) for d in (1, 2, 3)]))

    *factors, safe = call(
        corner_kernel,
        [shape(WIDE, WIDE, dtype=BF16)] * 2 + [shape(WIDE, B, dtype=BF16)] * 2
        + [shape(B, WIDE, dtype=BF16)] * 2 + [shape(B, B), shape(1, dtype=jnp.int32)],
        [VM] * 2 + [ANY] * 6, [VM] * 7 + [SM],
        [pltpu.VMEM((WIDE, WIDE), F32), pltpu.VMEM((WIDE, B), F32), dma((STEPS, 2))],
        [lower_inverse, upper_inverse, *corners], flops=6_000_000_000)
    w_hi, w_lo, patch = call(
        top_kernel, [shape(WIDE, OUTER, dtype=BF16)] * 2 + [shape(B, COLS)],
        [VM] * 7 + [ANY], [VM] * 3, [pltpu.VMEM((WIDE, COLS), F32), dma((STEPS,))],
        [*factors, tops], flops=4_000_000_000)

    def together():
        return call(
            update_kernel, shape(ROWS, COLS), [VM] + [ANY] * 19, ANY,
            [pltpu.VMEM((ROWS, WIDE), F32), pltpu.VMEM((ROWS, COLS), F32), pltpu.VMEM((PART, 3 * WIDE), BF16),
             pltpu.VMEM((3 * WIDE, OUTER), BF16), dma((32,)), dma((32,)), dma((32,)), dma((3,)), dma],
            [patch, matrix, w_hi, w_lo, *pieces], flops=14_000_000_000, megabytes=56)

    def stepwise():
        c_hi, c_lo, p_hi, p_lo = call(
            stepwise_corner_kernel, [shape(WIDE, WIDE, dtype=BF16)] * 4, [VM] * 2 + [ANY] * 6, [VM] * 4,
            [pltpu.VMEM((WIDE, WIDE), F32), dma((STEPS, 2))], [lower_inverse, upper_inverse, *corners])
        t_hi, t_lo, last = call(
            stepwise_top_kernel, [shape(WIDE, COLS, dtype=BF16)] * 2 + [shape(B, COLS)],
            [VM] * 3 + [ANY], [VM] * 3, [pltpu.VMEM((WIDE, COLS), F32), dma((STEPS,))],
            [lower_inverse, p_hi, p_lo, tops])
        return call(
            stepwise_update_kernel, shape(ROWS, COLS), [VM] * 6 + [ANY] * 17, ANY,
            [pltpu.VMEM((ROWS, WIDE), F32), pltpu.VMEM((ROWS, COLS), F32), pltpu.VMEM((PART, WIDE), BF16),
             pltpu.VMEM((PART, WIDE), BF16), pltpu.VMEM((PART, B), F32),
             dma((32,)), dma((32,)), dma((32,)), dma],
            [last, upper_inverse, t_hi, t_lo, c_hi, c_lo, matrix, *pieces], megabytes=56)

    return lax.cond(safe[0] == 1, together, stepwise)


def solution(mesh):
    placed = (P("row", "col"), P(), P(), P())
    return jax.shard_map(
        shards, mesh=mesh, in_specs=placed, out_specs=P("row", "col"), check_vma=False
    )
```

```python
import functools

import jax
import jax.numpy as jnp
from jax import lax
from jax.experimental import pallas as pl
from jax.experimental.pallas import tpu as pltpu
from jax.sharding import PartitionSpec as P

B = 128
STEPS = 6
ROWS = 2304
COLS = 1152
SHARE = 144
HALF = 72
N_ROW = 8
N_COL = 16
WIDE = STEPS * B
PART = 8 * HALF
SAFE = 100.0
TILE = 256

F32 = jnp.float32
BF16 = jnp.bfloat16
ANY = pl.BlockSpec(memory_space=pl.ANY)
VM = pl.BlockSpec(memory_space=pltpu.VMEM)
SM = pl.BlockSpec(memory_space=pltpu.SMEM)


def params(mebibytes):
    return pltpu.CompilerParams(vmem_limit_bytes=mebibytes * 1024 * 1024)


def split(value):
    high = value.astype(BF16)
    low = (value - high.astype(F32)).astype(BF16)
    return high, low


def mul(left, right):
    return jnp.dot(left, right, preferred_element_type=F32)


def wide(parts):
    return jnp.concatenate([parts[0], parts[1], parts[0]], axis=1)


def tall(parts):
    return jnp.concatenate([parts[0], parts[0], parts[1]], axis=0)


def dot3(left, right):
    lh, ll = left
    rh, rl = right
    return mul(lh, rh) + (mul(ll, rh) + mul(lh, rl))


def place(first):
    k0 = first[0]
    p = lax.axis_index("row")
    q = lax.axis_index("col")
    own_col = lax.rem(q - k0 + 8 * N_COL, N_COL)
    own_row = lax.rem(p - k0 + 16 * N_ROW, N_ROW)
    col_block = lax.div(k0 + jnp.minimum(own_col, STEPS - 1), N_COL)
    row_block = lax.div(k0 + jnp.minimum(own_row, STEPS - 1), N_ROW)
    return k0, p, q, own_col, own_row, col_block, row_block


def send_kernel(first, matrix, messages, top, sem):
    k0, p, q, own_col, own_row, col_block, row_block = place(first)
    lanes = pl.ds(pl.multiple_of(col_block * B, B), B)
    pivot = pl.ds(pl.multiple_of(row_block * B, B), B)
    copies = [pltpu.make_async_copy(matrix.at[pivot], top, sem.at[2 * N_COL])]
    for j in range(N_COL):
        copies.append(pltpu.make_async_copy(
            matrix.at[pivot, lanes], messages.at[j, pl.ds(SHARE, B)], sem.at[2 * j]))
        copies.append(pltpu.make_async_copy(
            matrix.at[pl.ds(j * SHARE, SHARE), lanes], messages.at[j, pl.ds(0, SHARE)], sem.at[2 * j + 1]))
    for copy in copies:
        copy.start()
    for copy in copies:
        copy.wait()


def select_kernel(first, messages, corner, one, two, sem):
    k0 = first[0]
    copies = []
    for t in range(STEPS):
        owner = lax.rem(k0 + t, N_COL)
        lanes = pl.ds(t * B, B)
        for n, (target, start, size) in enumerate((
                (corner.at[0, :, lanes], SHARE, 64), (corner.at[1, :, lanes], SHARE + 64, 64),
                (one.at[:, lanes], 0, HALF), (two.at[:, lanes], HALF, HALF))):
            copies.append(pltpu.make_async_copy(messages.at[owner, pl.ds(start, size)], target, sem.at[t, n]))
    for copy in copies:
        copy.start()
    for copy in copies:
        copy.wait()


def pick(refs, index, target, sem):
    for n, ref in enumerate(refs):
        @pl.when(index == n)
        def _():
            pltpu.make_async_copy(ref, target, sem).start()
    return pltpu.make_async_copy(refs[0], target, sem)


def ring_pieces(own, near, far):
    return [(own.at[0], own.at[1]), (near.at[0, 0], near.at[0, 1]),
            (far.at[0], far.at[1]), (near.at[1, 0], near.at[1, 1])]


def bring_corner(first, refs, target, sem):
    k0, p = first[0], lax.axis_index("row")
    z = lax.div(p, 2)
    core = lax.rem(p, 2)
    pieces = ring_pieces(*refs[0:3]) + ring_pieces(*refs[3:6])
    waits = []
    for a in range(STEPS):
        source = lax.rem(k0 + a, N_ROW)
        dz = lax.rem(z - lax.div(source, 2) + 4, 4)
        index = jnp.where(lax.rem(source, 2) == core, 0, 4) + dz
        for h in range(2):
            waits.append(pick([piece[h] for piece in pieces], index,
                              target.at[pl.ds(a * B + h * 64, 64)], sem.at[a, h]))
    for wait in waits:
        wait.wait()


def bring_tops(first, tops, target, sem):
    copies = []
    for a in range(STEPS):
        source = lax.rem(first[0] + a, N_ROW)
        copies.append(pltpu.make_async_copy(tops.at[source], target.at[pl.ds(a * B, B)], sem.at[a]))
    for copy in copies:
        copy.start()
    for copy in copies:
        copy.wait()


def largest(value):
    value = jnp.abs(value)
    return jnp.max(value.reshape(-1, 8, value.shape[-1]), axis=0)


def factor_kernel(first, lower, upper, *refs):
    corners, tops = refs[:6], refs[6]
    right_all, patch, safe, cur, rows, panel, special, n_own, m_own, sem, sem_top = refs[7:]
    k0, p, q, own_col, own_row, col_block, row_block = place(first)
    copies = []
    for a in range(STEPS):
        source = lax.rem(k0 + a, N_ROW)
        copies.append(pltpu.make_async_copy(tops.at[source], rows.at[pl.ds(a * B, B)], sem_top.at[a]))
    for copy in copies:
        copy.start()
    bring_corner(first, corners, cur, sem)
    ones = jnp.where(lax.broadcasted_iota(jnp.int32, (B, B), 0) == lax.broadcasted_iota(jnp.int32, (B, B), 1),
                     jnp.float32(1.0), jnp.float32(0.0))
    peak_col = jnp.zeros((8, B), F32)
    peak_row = jnp.zeros((8, WIDE), F32)
    for t in range(STEPS):
        here = slice(t * B, (t + 1) * B)
        diagonal = cur[here, here]
        cur[here, here] = ones
        left = mul(wide(split(cur[:, here])), tall(split(upper[t])))
        right = mul(wide(split(lower[t])), tall(split(cur[here, :])))
        peak_col = jnp.maximum(peak_col, largest(left))
        peak_row = jnp.maximum(peak_row, largest(right))

        @pl.when(own_col == t)
        def _():
            panel[...] = left
            m_own[...] = jnp.zeros((WIDE, B), F32)
            m_own[:(t + 1) * B, :] = left[:(t + 1) * B]

        @pl.when(own_row == t)
        def _():
            n_own[...] = jnp.zeros((B, WIDE), F32)
            n_own[:, :(t + 1) * B] = right[:, :(t + 1) * B]

            @pl.when(own_col == t)
            def _():
                special[...] = diagonal
        cur[:, here] = jnp.zeros((WIDE, B), F32)
        cur[here, :] = jnp.zeros((B, WIDE), F32)
        lefts = wide(split(left))
        rights = tall(split(right))
        for start in range(0, WIDE, TILE):
            cur[:, start:start + TILE] -= mul(lefts, rights[:, start:start + TILE])

    @pl.when((own_col < own_row) & (own_row < STEPS))
    def _():
        special[...] = panel[pl.ds(pl.multiple_of(own_row * B, B), B), :]
    peak = jnp.maximum(jnp.max(peak_col), jnp.max(peak_row))
    safe[0] = jnp.where(peak < SAFE, 1, 0)
    for copy in copies:
        copy.wait()
    own = pl.ds(pl.multiple_of(jnp.minimum(own_row, STEPS - 1) * B, B), B)
    left = wide(split(cur[...]))
    left_own = wide(split(n_own[...]))
    for start in range(0, COLS, TILE):
        size = min(TILE, COLS - start)
        lanes = slice(start, start + size)
        block = ((lax.broadcasted_iota(jnp.int32, (1, size), 1) + start) >> 7) * N_COL + q
        values = tall(split(rows[:, lanes]))
        high, low = split(jnp.where(block > k0 + STEPS - 1, mul(left, values), 0.0))
        for n, part in enumerate((high, high, low)):
            right_all[n * WIDE:(n + 1) * WIDE, lanes] = part
        patch[:, lanes] = jnp.where(block > k0 + own_row, mul(left_own, values), rows[own, lanes])
    own_lanes = pl.ds(pl.multiple_of(col_block * B, B), B)

    @pl.when(own_col < STEPS)
    def _():
        high, low = split(m_own[...])
        for n, part in enumerate((high, high, low)):
            right_all[n * WIDE:(n + 1) * WIDE, own_lanes] = part

    @pl.when((own_col <= own_row) & (own_row < STEPS))
    def _():
        patch[:, own_lanes] = special[...]


def raw_copies(near, far, raw, sem):
    q = lax.axis_index("col")
    x = lax.div(q, 4)
    y = lax.rem(q, 4)
    copies = []
    for dy in range(4):
        for dx in range(4):
            owner = lax.rem(x + 4 - dx, 4) * 4 + lax.rem(y + 4 - dy, 4)
            start = pl.multiple_of(owner * SHARE, 8)
            copies.append(pltpu.make_async_copy(
                near[2 * dy + dx // 2].at[dx % 2], raw.at[pl.ds(start, HALF)], sem.at[len(copies)]))
    for owner in range(N_COL):
        copies.append(pltpu.make_async_copy(
            far.at[owner], raw.at[pl.ds(owner * SHARE + HALF, HALF)], sem.at[len(copies)]))
    return copies


def row_blocks(start, count, p):
    return ((lax.broadcasted_iota(jnp.int32, (count, B), 0) + start) >> 7) * N_ROW + p


def left_kernel(first, *refs):
    near, far = refs[:8], refs[8]
    left, raw, buffer, sem, sem_out = refs[9:]
    k0, p = first[0], lax.axis_index("row")
    copies = raw_copies(near, far, raw, sem)
    for copy in copies:
        copy.start()
    for copy in copies:
        copy.wait()
    outs = []
    size = ROWS // 6
    for s in range(6):
        slot = s % 2
        if s > 1:
            outs[s - 2].wait()
        span = slice(s * size, (s + 1) * size)
        live = row_blocks(s * size, size, p) > k0 + STEPS - 1
        for t in range(STEPS):
            high, low = split(jnp.where(live, raw[span, t * B:(t + 1) * B], 0.0))
            for n, part in enumerate((high, low, high)):
                buffer[slot, :, n * WIDE + t * B:n * WIDE + (t + 1) * B] = part
        outs.append(pltpu.make_async_copy(buffer.at[slot], left.at[pl.ds(s * size, size)], sem_out.at[slot]))
        outs[-1].start()
    outs[4].wait()
    outs[5].wait()


def stepwise_corner_kernel(first, lower, upper, *refs):
    c_hi, c_lo, p_hi, p_lo, cur, sem = refs[6:]
    bring_corner(first, refs[:6], cur, sem)
    for t in range(STEPS - 1):
        here = slice(t * B, (t + 1) * B)
        after = slice((t + 1) * B, WIDE)
        tops = split(dot3(split(lower[t]), split(cur[here, after])))
        panels = split(dot3(split(cur[after, here]), split(upper[t])))
        c_hi[here, after], c_lo[here, after] = tops
        p_hi[after, here], p_lo[after, here] = panels
        cur[after, after] -= dot3(panels, tops)


def stepwise_top_kernel(first, lower, p_hi, p_lo, tops, t_hi, t_lo, patch, cur, sem):
    k0, p, q, own_col, own_row, col_block, row_block = place(first)
    bring_tops(first, tops, cur, sem)
    lane_block = (lax.broadcasted_iota(jnp.int32, (1, COLS), 1) >> 7) * N_COL + q
    for t in range(STEPS):
        here = slice(t * B, (t + 1) * B)
        after = slice((t + 1) * B, WIDE)
        live = lane_block > k0 + t
        top = jnp.where(live, dot3(split(lower[t]), split(cur[here, :])), 0.0)
        tops = split(top)
        t_hi[here, :], t_lo[here, :] = tops

        @pl.when(own_row == t)
        def _():
            patch[...] = jnp.where(live, top, cur[here, :])
            if t > 0:
                @pl.when(own_col < t)
                def _():
                    source = pl.ds(pl.multiple_of(own_col * B, B), B)
                    target = pl.ds(pl.multiple_of(col_block * B, B), B)
                    patch[:, target] = p_hi[here, source].astype(F32) + p_lo[here, source].astype(F32)
        if t + 1 < STEPS:
            cur[after, :] -= dot3((p_hi[after, here], p_lo[after, here]), tops)


def stepwise_update_kernel(first, patch, upper, t_hi, t_lo, c_hi, c_lo, matrix, *refs):
    near, far = refs[:8], refs[8]
    out, raw, rows, high, low, panel, sem_raw, sem_in, sem_patch = refs[9:]
    k0, p, q, own_col, own_row, col_block, row_block = place(first)
    copies = raw_copies(near, far, raw, sem_raw) + [pltpu.make_async_copy(matrix, rows, sem_in)]
    for copy in copies:
        copy.start()
    for copy in copies:
        copy.wait()
    own = pl.ds(pl.multiple_of(col_block * B, B), B)

    @pl.loop(0, 4)
    def _(s):
        start = pl.multiple_of(s * PART, PART)
        span = pl.ds(start, PART)
        block = row_blocks(start, PART, p)
        for t in range(STEPS):
            lanes = slice(t * B, (t + 1) * B)
            value = raw[span, lanes]
            if t > 0:
                value = value - dot3((high[:, :t * B], low[:, :t * B]), (c_hi[:t * B, lanes], c_lo[:t * B, lanes]))
            value = jnp.where(block > k0 + t, dot3(split(value), split(upper[t])), 0.0)
            high[:, lanes], low[:, lanes] = split(value)

            @pl.when(own_col == t)
            def _():
                panel[...] = value
        for start in range(0, COLS, TILE):
            lanes = slice(start, min(start + TILE, COLS))
            rows[span, lanes] -= dot3((high[...], low[...]), (t_hi[:, lanes], t_lo[:, lanes]))

        @pl.when(own_col < STEPS)
        def _():
            rows[span, own] = jnp.where(block > k0 + own_col, panel[...], rows[span, own])
    copy = pltpu.make_async_copy(rows, out, sem_in)
    copy.start()
    copy.wait()

    @pl.when(own_row < STEPS)
    def _():
        last = pltpu.make_async_copy(patch, out.at[pl.ds(pl.multiple_of(row_block * B, B), B)], sem_patch)
        last.start()
        last.wait()


def shards(matrix, first_step, lower_inverse, upper_inverse):
    def shape(*dims, dtype=F32):
        return jax.ShapeDtypeStruct(dims, dtype)

    dma = pltpu.SemaphoreType.DMA

    def call(kernel, outs, in_specs, out_specs, scratch, args, flops=1_000_000, megabytes=48):
        return pl.pallas_call(
            kernel, out_shape=outs, in_specs=[SM] + in_specs, out_specs=out_specs, scratch_shapes=scratch,
            compiler_params=params(megabytes),
            cost_estimate=pl.CostEstimate(flops=flops, bytes_accessed=4_000_000, transcendentals=0),
        )(first_step, *args)

    def along_x(value, distance):
        return lax.ppermute(value, "col", [(i, (i + 4 * distance) % N_COL) for i in range(N_COL)])

    def along_y(value, distance):
        return lax.ppermute(value, "col", [(i, i // 4 * 4 + (i + distance) % 4) for i in range(N_COL)])

    def along_z(value, distance):
        return lax.ppermute(value, "row", [(i, (i + 2 * distance) % N_ROW) for i in range(N_ROW)])

    def swap(value):
        return lax.ppermute(value, "row", [(i, i ^ 1) for i in range(N_ROW)])

    def depth(value):
        ahead, back = along_z(value, 1), along_z(value, 3)
        far = jnp.stack([along_z(ahead[0], 1), along_z(back[1], 3)])
        mine = (value, jnp.stack([ahead, back]), far)
        return mine + tuple(swap(v) for v in mine)

    def ring(move, pieces):
        a, b = jnp.stack(pieces[:2]), jnp.stack(pieces[2:])
        a1, b1 = move(a, 1), move(b, 1)
        a3, b3 = move(a, 3), move(b, 3)
        a2, b2 = move(a1, 1), move(b3, 3)
        return [a, b, a1, b1, a2, b2, a3, b3]

    messages, top = call(send_kernel, [shape(N_COL, SHARE + B, B), shape(B, COLS)], [ANY], [VM] * 2,
                         [dma((2 * N_COL + 1,))], [matrix])
    tops = lax.all_gather(top, "row")
    got = lax.all_to_all(messages, "col", 0, 0)
    corner, one, two = call(select_kernel, [shape(2, 64, WIDE)] + [shape(HALF, WIDE)] * 2, [ANY], [VM] * 3,
                            [dma((STEPS, 4))], [got])
    far = lax.all_gather(two, "col")
    corners = depth(corner)
    near = ring(along_y, [one] + [along_x(one, d) for d in (1, 2, 3)])

    right, patch, safe = call(
        factor_kernel,
        [shape(3 * WIDE, COLS, dtype=BF16), shape(B, COLS), shape(1, dtype=jnp.int32)],
        [VM] * 2 + [ANY] * 7, [VM] * 2 + [SM],
        [pltpu.VMEM((WIDE, WIDE), F32), pltpu.VMEM((WIDE, COLS), F32), pltpu.VMEM((WIDE, B), F32),
         pltpu.VMEM((B, B), F32), pltpu.VMEM((B, WIDE), F32), pltpu.VMEM((WIDE, B), F32),
         dma((STEPS, 2)), dma((STEPS,))],
        [lower_inverse, upper_inverse, *corners, tops], flops=12_000_000_000)
    left = call(
        left_kernel, shape(ROWS, 3 * WIDE, dtype=BF16), [ANY] * 9, ANY,
        [pltpu.VMEM((ROWS, WIDE), F32), pltpu.VMEM((2, ROWS // 6, 3 * WIDE), BF16), dma((32,)), dma((2,))],
        [*near, far], flops=3_000_000_000)

    def together():
        k0 = first_step[0]
        p, q = lax.axis_index("row"), lax.axis_index("col")
        own_row = (p - k0) % N_ROW
        row_block = jnp.arange(ROWS, dtype=jnp.int32) // B * N_ROW + p
        col_block = jnp.arange(COLS, dtype=jnp.int32) // B * N_COL + q
        taken = (row_block >= k0 + STEPS)[:, None] & ((col_block >= k0) & (col_block < k0 + STEPS))[None, :]
        full = jnp.where(taken, jnp.float32(0.0), matrix) + mul(left, right)
        start = (k0 + jnp.minimum(own_row, STEPS - 1)) // N_ROW * B
        old = lax.dynamic_slice_in_dim(full, start, B, 0)
        return lax.dynamic_update_slice_in_dim(full, jnp.where(own_row < STEPS, patch, old), start, 0)

    def stepwise():
        c_hi, c_lo, p_hi, p_lo = call(
            stepwise_corner_kernel, [shape(WIDE, WIDE, dtype=BF16)] * 4, [VM] * 2 + [ANY] * 6, [VM] * 4,
            [pltpu.VMEM((WIDE, WIDE), F32), dma((STEPS, 2))], [lower_inverse, upper_inverse, *corners])
        t_hi, t_lo, last = call(
            stepwise_top_kernel, [shape(WIDE, COLS, dtype=BF16)] * 2 + [shape(B, COLS)],
            [VM] * 3 + [ANY], [VM] * 3, [pltpu.VMEM((WIDE, COLS), F32), dma((STEPS,))],
            [lower_inverse, p_hi, p_lo, tops])
        return call(
            stepwise_update_kernel, shape(ROWS, COLS), [VM] * 6 + [ANY] * 10, ANY,
            [pltpu.VMEM((ROWS, WIDE), F32), pltpu.VMEM((ROWS, COLS), F32), pltpu.VMEM((PART, WIDE), BF16),
             pltpu.VMEM((PART, WIDE), BF16), pltpu.VMEM((PART, B), F32), dma((32,)), dma, dma],
            [last, upper_inverse, t_hi, t_lo, c_hi, c_lo, matrix, *near, far], megabytes=56)

    return lax.cond(safe[0] == 1, together, stepwise)


def solution(mesh):
    placed = (P("row", "col"), P(), P(), P())
    return jax.shard_map(
        shards, mesh=mesh, in_specs=placed, out_specs=P("row", "col"), check_vma=False
    )
```

```python
import functools

import jax
import jax.numpy as jnp
from jax import lax
from jax.experimental import pallas as pl
from jax.experimental.pallas import tpu as pltpu
from jax.sharding import PartitionSpec as P

B = 128
STEPS = 6
ROWS = 2304
COLS = 1152
N_ROW = 8
N_COL = 16
WIDE = STEPS * B
CLASSES = 5
SAFE = 100.0
TILE = 256

F32 = jnp.float32
BF16 = jnp.bfloat16
ANY = pl.BlockSpec(memory_space=pl.ANY)
VM = pl.BlockSpec(memory_space=pltpu.VMEM)
SM = pl.BlockSpec(memory_space=pltpu.SMEM)


def params(mebibytes):
    return pltpu.CompilerParams(vmem_limit_bytes=mebibytes * 1024 * 1024)


def split(value):
    high = value.astype(BF16)
    low = (value - high.astype(F32)).astype(BF16)
    return high, low


def mul(left, right):
    return jnp.dot(left, right, preferred_element_type=F32)


def wide(parts):
    return jnp.concatenate([parts[0], parts[1], parts[0]], axis=1)


def tall(parts):
    return jnp.concatenate([parts[0], parts[0], parts[1]], axis=0)


def dot3(left, right):
    lh, ll = left
    rh, rl = right
    return mul(lh, rh) + (mul(ll, rh) + mul(lh, rl))


def place(skip, first):
    k0 = first[0] - N_COL * skip
    p = lax.axis_index("row")
    q = lax.axis_index("col")
    own_col = lax.rem(q - k0 + 8 * N_COL, N_COL)
    own_row = lax.rem(p - k0 + 16 * N_ROW, N_ROW)
    col_block = lax.div(k0 + jnp.minimum(own_col, STEPS - 1), N_COL)
    row_block = lax.div(k0 + jnp.minimum(own_row, STEPS - 1), N_ROW)
    return k0, p, q, own_col, own_row, col_block, row_block


def send_kernel(skip, first, matrix, panels, corners, top, sem):
    k0, p, q, own_col, own_row, col_block, row_block = place(skip, first)
    half = panels.shape[1] // 2
    left = skip * B
    lanes = pl.ds(pl.multiple_of(left + col_block * B, B), B)
    pivot = pl.multiple_of(2 * left + row_block * B, B)
    copies = []
    for j in range(N_COL):
        for h in range(2):
            start = 2 * left + (h * N_COL + j) * half
            copies.append(pltpu.make_async_copy(
                matrix.at[pl.ds(start, half), lanes], panels.at[j, pl.ds(h * half, half)], sem.at[3 * j + h]))
        copies.append(pltpu.make_async_copy(matrix.at[pl.ds(pivot, B), lanes], corners.at[j], sem.at[3 * j + 2]))
    for h in range(2):
        copies.append(pltpu.make_async_copy(
            matrix.at[pl.ds(pivot + 64 * h, 64), pl.ds(left, COLS - left)], top.at[h], sem.at[3 * N_COL + h]))
    for copy in copies:
        copy.start()
    for copy in copies:
        copy.wait()


def share_kernel(skip, first, panels, one, two, sem):
    k0 = first[0]
    half = one.shape[0]
    copies = []
    for t in range(STEPS):
        owner = lax.rem(k0 + t, N_COL)
        for n, target in enumerate((one, two)):
            copies.append(pltpu.make_async_copy(
                panels.at[owner, pl.ds(n * half, half)], target.at[:, pl.ds(t * B, B)], sem.at[t, n]))
    for copy in copies:
        copy.start()
    for copy in copies:
        copy.wait()


def corner_kernel(skip, first, blocks, corner, sem):
    k0 = first[0]
    copies = []
    for t in range(STEPS):
        owner = lax.rem(k0 + t, N_COL)
        for h in range(2):
            copies.append(pltpu.make_async_copy(
                blocks.at[owner, pl.ds(64 * h, 64)], corner.at[h, :, pl.ds(t * B, B)], sem.at[t, h]))
    for copy in copies:
        copy.start()
    for copy in copies:
        copy.wait()


def pick(refs, index, target, sem):
    for n, ref in enumerate(refs):
        @pl.when(index == n)
        def _():
            pltpu.make_async_copy(ref, target, sem).start()
    return pltpu.make_async_copy(refs[0], target, sem)


def ring_pieces(own, near, far):
    return [(own.at[0], own.at[1]), (near.at[0, 0], near.at[0, 1]),
            (far.at[0], far.at[1]), (near.at[1, 0], near.at[1, 1])]


def bring(first, refs, target, sem):
    k0, p = first[0], lax.axis_index("row")
    z = lax.div(p, 2)
    core = lax.rem(p, 2)
    pieces = ring_pieces(*refs[0:3]) + ring_pieces(*refs[3:6])
    waits = []
    for a in range(STEPS):
        source = lax.rem(k0 + a, N_ROW)
        dz = lax.rem(z - lax.div(source, 2) + 4, 4)
        index = jnp.where(lax.rem(source, 2) == core, 0, 4) + dz
        for h in range(2):
            waits.append(pick([piece[h] for piece in pieces], index,
                              target.at[pl.ds(a * B + h * 64, 64)], sem.at[a, h]))
    return waits


def largest(value):
    value = jnp.abs(value)
    return jnp.max(value.reshape(-1, 8, value.shape[-1]), axis=0)


def factor_kernel(skip, first, lower, upper, *refs):
    right_all, patch, safe, cur, rows, panel, special, n_own, m_own, sem, sem_top = refs[12:]
    cols = rows.shape[1]
    k0, p, q, own_col, own_row, col_block, row_block = place(skip, first)
    waits = bring(first, refs[:6], cur, sem)
    waits_top = bring(first, refs[6:12], rows, sem_top)
    for wait in waits:
        wait.wait()
    ones = jnp.where(lax.broadcasted_iota(jnp.int32, (B, B), 0) == lax.broadcasted_iota(jnp.int32, (B, B), 1),
                     jnp.float32(1.0), jnp.float32(0.0))
    peak_col = jnp.zeros((8, B), F32)
    peak_row = jnp.zeros((8, WIDE), F32)
    for t in range(STEPS):
        here = slice(t * B, (t + 1) * B)
        diagonal = cur[here, here]
        cur[here, here] = ones
        left = mul(wide(split(cur[:, here])), tall(split(upper[t])))
        right = mul(wide(split(lower[t])), tall(split(cur[here, :])))
        peak_col = jnp.maximum(peak_col, largest(left))
        peak_row = jnp.maximum(peak_row, largest(right))

        @pl.when(own_col == t)
        def _():
            panel[...] = left
            m_own[...] = jnp.zeros((WIDE, B), F32)
            m_own[:(t + 1) * B, :] = left[:(t + 1) * B]

        @pl.when(own_row == t)
        def _():
            n_own[...] = jnp.zeros((B, WIDE), F32)
            n_own[:, :(t + 1) * B] = right[:, :(t + 1) * B]

            @pl.when(own_col == t)
            def _():
                special[...] = diagonal
        cur[:, here] = jnp.zeros((WIDE, B), F32)
        cur[here, :] = jnp.zeros((B, WIDE), F32)
        lefts = wide(split(left))
        rights = tall(split(right))
        for start in range(0, WIDE, TILE):
            cur[:, start:start + TILE] -= mul(lefts, rights[:, start:start + TILE])

    @pl.when((own_col < own_row) & (own_row < STEPS))
    def _():
        special[...] = panel[pl.ds(pl.multiple_of(own_row * B, B), B), :]
    peak = jnp.maximum(jnp.max(peak_col), jnp.max(peak_row))
    safe[0] = jnp.where(peak < SAFE, 1, 0)
    for wait in waits_top:
        wait.wait()
    own = pl.ds(pl.multiple_of(jnp.minimum(own_row, STEPS - 1) * B, B), B)
    left = wide(split(cur[...]))
    left_own = wide(split(n_own[...]))
    for start in range(0, cols, TILE):
        size = min(TILE, cols - start)
        lanes = slice(start, start + size)
        block = ((lax.broadcasted_iota(jnp.int32, (1, size), 1) + start) >> 7) * N_COL + q
        values = tall(split(rows[:, lanes]))
        high, low = split(jnp.where(block > k0 + STEPS - 1, mul(left, values), 0.0))
        for n, part in enumerate((high, high, low)):
            right_all[n * WIDE:(n + 1) * WIDE, lanes] = part
        patch[:, lanes] = jnp.where(block > k0 + own_row, mul(left_own, values), rows[own, lanes])
    own_lanes = pl.ds(pl.multiple_of(col_block * B, B), B)

    @pl.when(own_col < STEPS)
    def _():
        high, low = split(m_own[...])
        for n, part in enumerate((high, high, low)):
            right_all[n * WIDE:(n + 1) * WIDE, own_lanes] = part

    @pl.when((own_col <= own_row) & (own_row < STEPS))
    def _():
        patch[:, own_lanes] = special[...]


def near_copies(near, raw, sem):
    q = lax.axis_index("col")
    x = lax.div(q, 4)
    y = lax.rem(q, 4)
    copies = []
    for dy in range(4):
        for dx in range(4):
            owner = lax.rem(x + 4 - dx, 4) * 4 + lax.rem(y + 4 - dy, 4)
            copies.append(pltpu.make_async_copy(
                near[2 * dy + dx // 2].at[dx % 2], raw.at[owner], sem.at[len(copies)]))
    return copies


def row_blocks(start, count, p):
    return ((lax.broadcasted_iota(jnp.int32, (count, B), 0) + start) >> 7) * N_ROW + p


def left_kernel(skip, first, *refs):
    left, raw, buffer, sem, sem_out = refs[-5:]
    count = 8 if len(refs) > 7 else 1
    pieces = refs[:count]
    k0, p = place(skip, first)[:2]
    half = raw.shape[1]
    if count == 1:
        copies = [pltpu.make_async_copy(pieces[0].at[n], raw.at[n], sem.at[n]) for n in range(N_COL)]
    else:
        copies = near_copies(pieces, raw, sem)
    for copy in copies:
        copy.start()
    for copy in copies:
        copy.wait()
    offset = N_COL * half if count == 1 else 0
    for n in range(N_COL):
        live = row_blocks(n * half + offset, half, p) > k0 + STEPS - 1
        for t in range(STEPS):
            high, low = split(jnp.where(live, raw[n, :, t * B:(t + 1) * B], 0.0))
            for m, part in enumerate((high, low, high)):
                buffer[n * half:(n + 1) * half, m * WIDE + t * B:m * WIDE + (t + 1) * B] = part
    copy = pltpu.make_async_copy(buffer, left.at[pl.ds(offset, N_COL * half)], sem_out)
    copy.start()
    copy.wait()


def stepwise_corner_kernel(skip, first, lower, upper, *refs):
    c_hi, c_lo, p_hi, p_lo, cur, sem = refs[6:]
    for wait in bring(first, refs[:6], cur, sem):
        wait.wait()
    for t in range(STEPS - 1):
        here = slice(t * B, (t + 1) * B)
        after = slice((t + 1) * B, WIDE)
        tops = split(dot3(split(lower[t]), split(cur[here, after])))
        panels = split(dot3(split(cur[after, here]), split(upper[t])))
        c_hi[here, after], c_lo[here, after] = tops
        p_hi[after, here], p_lo[after, here] = panels
        cur[after, after] -= dot3(panels, tops)


def stepwise_top_kernel(skip, first, lower, p_hi, p_lo, *refs):
    t_hi, t_lo, patch, cur, sem = refs[6:]
    cols = cur.shape[1]
    k0, p, q, own_col, own_row, col_block, row_block = place(skip, first)
    for wait in bring(first, refs[:6], cur, sem):
        wait.wait()
    lane_block = (lax.broadcasted_iota(jnp.int32, (1, cols), 1) >> 7) * N_COL + q
    for t in range(STEPS):
        here = slice(t * B, (t + 1) * B)
        after = slice((t + 1) * B, WIDE)
        live = lane_block > k0 + t
        top = jnp.where(live, dot3(split(lower[t]), split(cur[here, :])), 0.0)
        tops = split(top)
        t_hi[here, :], t_lo[here, :] = tops

        @pl.when(own_row == t)
        def _():
            patch[...] = jnp.where(live, top, cur[here, :])
            if t > 0:
                @pl.when(own_col < t)
                def _():
                    source = pl.ds(pl.multiple_of(own_col * B, B), B)
                    target = pl.ds(pl.multiple_of(col_block * B, B), B)
                    patch[:, target] = p_hi[here, source].astype(F32) + p_lo[here, source].astype(F32)
        if t + 1 < STEPS:
            cur[after, :] -= dot3((p_hi[after, here], p_lo[after, here]), tops)


def stepwise_update_kernel(skip, first, patch, upper, t_hi, t_lo, c_hi, c_lo, matrix, *refs):
    near, far = refs[:8], refs[8]
    out, raw, rows, high, panel, sem_raw, sem_far, sem_in = refs[9:]
    k0, p, q, own_col, own_row, col_block, row_block = place(skip, first)
    half, cols = raw.shape[2], t_hi.shape[1]
    copies = near_copies(near, raw.at[0], sem_raw)
    copies += [pltpu.make_async_copy(far, raw.at[1], sem_far), pltpu.make_async_copy(matrix, rows, sem_in)]
    for copy in copies:
        copy.start()
    for copy in copies:
        copy.wait()
    own = pl.ds(pl.multiple_of((skip + col_block) * B, B), B)

    @pl.loop(0, 2 * N_COL)
    def _(n):
        owner = lax.div(n, 2)
        second = lax.rem(n, 2)
        start = pl.multiple_of((second * N_COL + owner) * half, 8)
        span = pl.ds(pl.multiple_of(2 * skip * B + start, 8), half)
        block = row_blocks(start, half, p)
        for t in range(STEPS):
            lanes = slice(t * B, (t + 1) * B)
            value = raw[second, owner, :, lanes]
            if t > 0:
                value = value - dot3(split(high[:, :t * B]), (c_hi[:t * B, lanes], c_lo[:t * B, lanes]))
            value = jnp.where(block > k0 + t, dot3(split(value), split(upper[t])), 0.0)
            high[:, lanes] = value

            @pl.when(own_col == t)
            def _():
                panel[...] = value
        left = split(high[...])
        for begin in range(0, cols, TILE):
            stop = min(begin + TILE, cols)
            lanes = slice(begin, stop)
            rows[span, skip * B + begin:skip * B + stop] -= dot3(left, (t_hi[:, lanes], t_lo[:, lanes]))

        @pl.when(own_col < STEPS)
        def _():
            rows[span, own] = jnp.where(block > k0 + own_col, panel[...], rows[span, own])

    @pl.when(own_row < STEPS)
    def _():
        rows[pl.ds(pl.multiple_of((2 * skip + row_block) * B, B), B), skip * B:] = patch[...]
    copy = pltpu.make_async_copy(rows, out, sem_in)
    copy.start()
    copy.wait()


def shards(matrix, first_step, lower_inverse, upper_inverse):
    programs = [functools.partial(steps, skip) for skip in range(CLASSES)]
    return lax.switch(first_step[0] // N_COL, programs, matrix, first_step, lower_inverse, upper_inverse)


def steps(skip, matrix, first_step, lower_inverse, upper_inverse):
    top_rows, left_cols = 2 * skip * B, skip * B
    rows, cols = ROWS - top_rows, COLS - left_cols
    share = rows // N_COL
    half = share // 2

    def shape(*dims, dtype=F32):
        return jax.ShapeDtypeStruct(dims, dtype)

    dma = pltpu.SemaphoreType.DMA

    def call(kernel, outs, in_specs, out_specs, scratch, args, flops=1_000_000, megabytes=48, **kwargs):
        return pl.pallas_call(
            functools.partial(kernel, skip), out_shape=outs, in_specs=[SM] + in_specs, out_specs=out_specs, scratch_shapes=scratch,
            compiler_params=params(megabytes),
            cost_estimate=pl.CostEstimate(flops=flops, bytes_accessed=4_000_000, transcendentals=0),
            **kwargs,
        )(first_step, *args)

    def along_x(value, distance):
        return lax.ppermute(value, "col", [(i, (i + 4 * distance) % N_COL) for i in range(N_COL)])

    def along_y(value, distance):
        return lax.ppermute(value, "col", [(i, i // 4 * 4 + (i + distance) % 4) for i in range(N_COL)])

    def along_z(value, distance):
        return lax.ppermute(value, "row", [(i, (i + 2 * distance) % N_ROW) for i in range(N_ROW)])

    def swap(value):
        return lax.ppermute(value, "row", [(i, i ^ 1) for i in range(N_ROW)])

    def depth(value):
        ahead, back = along_z(value, 1), along_z(value, 3)
        far = jnp.stack([along_z(ahead[0], 1), along_z(back[1], 3)])
        mine = (value, jnp.stack([ahead, back]), far)
        return mine + tuple(swap(v) for v in mine)

    def ring(move, pieces):
        a, b = jnp.stack(pieces[:2]), jnp.stack(pieces[2:])
        a1, b1 = move(a, 1), move(b, 1)
        a3, b3 = move(a, 3), move(b, 3)
        a2, b2 = move(a1, 1), move(b3, 3)
        return [a, b, a1, b1, a2, b2, a3, b3]

    panels, corner, top = call(
        send_kernel, [shape(N_COL, share, B), shape(N_COL, B, B), shape(2, 64, cols)],
        [ANY], [VM] * 3, [dma((3 * N_COL + 2,))], [matrix])
    panels = lax.all_to_all(panels, "col", 0, 0)
    corner, panels = lax.optimization_barrier((corner, panels))
    one, two = call(share_kernel, [shape(half, WIDE)] * 2, [ANY], [VM] * 2, [dma((STEPS, 2))], [panels])
    far = lax.all_gather(two, "col")
    corner = lax.all_to_all(corner, "col", 0, 0)
    corner, = call(corner_kernel, [shape(2, 64, WIDE)], [ANY], [VM], [dma((STEPS, 2))], [corner])
    corners = depth(corner)
    tops = depth(top)
    near = ring(along_y, [one] + [along_x(one, d) for d in (1, 2, 3)])

    right, patch, safe = call(
        factor_kernel,
        [shape(3 * WIDE, cols, dtype=BF16), shape(B, cols), shape(1, dtype=jnp.int32)],
        [VM] * 2 + [ANY] * 12, [VM] * 2 + [SM],
        [pltpu.VMEM((WIDE, WIDE), F32), pltpu.VMEM((WIDE, cols), F32), pltpu.VMEM((WIDE, B), F32),
         pltpu.VMEM((B, B), F32), pltpu.VMEM((B, WIDE), F32), pltpu.VMEM((WIDE, B), F32),
         dma((STEPS, 2)), dma((STEPS, 2))],
        [lower_inverse, upper_inverse, *corners, *tops], flops=12_000_000_000)
    def assemble(*pieces, **kwargs):
        return call(left_kernel, shape(rows, 3 * WIDE, dtype=BF16), [ANY] * len(pieces), ANY,
                    [pltpu.VMEM((N_COL, half, WIDE), F32), pltpu.VMEM((N_COL * half, 3 * WIDE), BF16),
                     dma((N_COL,)), dma], pieces, flops=2_000_000_000, **kwargs)

    left = assemble(*near)
    left = assemble(far, left, input_output_aliases={2: 0})

    def together():
        k0 = first_step[0] - N_COL * skip
        p, q = lax.axis_index("row"), lax.axis_index("col")
        own_row = (p - k0) % N_ROW
        row_block = jnp.arange(rows, dtype=jnp.int32) // B * N_ROW + p
        col_block = jnp.arange(cols, dtype=jnp.int32) // B * N_COL + q
        taken = (row_block >= k0 + STEPS)[:, None] & ((col_block >= k0) & (col_block < k0 + STEPS))[None, :]
        full = jnp.where(taken, jnp.float32(0.0), matrix[top_rows:, left_cols:]) + mul(left, right)
        if skip:
            full = matrix.at[top_rows:, left_cols:].set(full)
        start = top_rows + (k0 + jnp.minimum(own_row, STEPS - 1)) // N_ROW * B
        old = lax.dynamic_slice(full, (start, left_cols), (B, cols))
        return lax.dynamic_update_slice(full, jnp.where(own_row < STEPS, patch, old), (start, left_cols))

    def stepwise():
        c_hi, c_lo, p_hi, p_lo = call(
            stepwise_corner_kernel, [shape(WIDE, WIDE, dtype=BF16)] * 4, [VM] * 2 + [ANY] * 6, [VM] * 4,
            [pltpu.VMEM((WIDE, WIDE), F32), dma((STEPS, 2))], [lower_inverse, upper_inverse, *corners])
        t_hi, t_lo, last = call(
            stepwise_top_kernel, [shape(WIDE, cols, dtype=BF16)] * 2 + [shape(B, cols)],
            [VM] * 3 + [ANY] * 6, [VM] * 3, [pltpu.VMEM((WIDE, cols), F32), dma((STEPS, 2))],
            [lower_inverse, p_hi, p_lo, *tops])
        return call(
            stepwise_update_kernel, shape(ROWS, COLS), [VM] * 6 + [ANY] * 10, ANY,
            [pltpu.VMEM((2, N_COL, half, WIDE), F32), pltpu.VMEM((ROWS, COLS), F32),
             pltpu.VMEM((half, WIDE), F32), pltpu.VMEM((half, B), F32), dma((N_COL,)), dma, dma],
            [last, upper_inverse, t_hi, t_lo, c_hi, c_lo, matrix, *near, far], megabytes=56)

    return lax.cond(safe[0] == 1, together, stepwise)


def solution(mesh):
    placed = (P("row", "col"), P(), P(), P())
    return jax.shard_map(
        shards, mesh=mesh, in_specs=placed, out_specs=P("row", "col"), check_vma=False
    )
```

```python
import functools

import jax
import jax.numpy as jnp
from jax import lax
from jax.experimental import pallas as pl
from jax.experimental.pallas import tpu as pltpu
from jax.sharding import PartitionSpec as P

B = 128
STEPS = 6
ROWS = 2304
COLS = 1152
SHARE = 144
HALF = 72
N_ROW = 8
N_COL = 16
WIDE = STEPS * B
PART = 8 * HALF
SAFE = 100.0
TILE = 256

F32 = jnp.float32
BF16 = jnp.bfloat16
ANY = pl.BlockSpec(memory_space=pl.ANY)
VM = pl.BlockSpec(memory_space=pltpu.VMEM)
SM = pl.BlockSpec(memory_space=pltpu.SMEM)


def params(mebibytes):
    return pltpu.CompilerParams(vmem_limit_bytes=mebibytes * 1024 * 1024)


def split(value):
    high = value.astype(BF16)
    low = (value - high.astype(F32)).astype(BF16)
    return high, low


def mul(left, right):
    return jnp.dot(left, right, preferred_element_type=F32)


def wide(parts):
    return jnp.concatenate([parts[0], parts[1], parts[0]], axis=1)


def tall(parts):
    return jnp.concatenate([parts[0], parts[0], parts[1]], axis=0)


def dot3(left, right):
    lh, ll = left
    rh, rl = right
    return mul(lh, rh) + (mul(ll, rh) + mul(lh, rl))


def place(first):
    k0 = first[0]
    p = lax.axis_index("row")
    q = lax.axis_index("col")
    own_col = lax.rem(q - k0 + 8 * N_COL, N_COL)
    own_row = lax.rem(p - k0 + 16 * N_ROW, N_ROW)
    col_block = lax.div(k0 + jnp.minimum(own_col, STEPS - 1), N_COL)
    row_block = lax.div(k0 + jnp.minimum(own_row, STEPS - 1), N_ROW)
    return k0, p, q, own_col, own_row, col_block, row_block


def send_kernel(first, matrix, messages, top, sem):
    k0, p, q, own_col, own_row, col_block, row_block = place(first)
    lanes = pl.ds(pl.multiple_of(col_block * B, B), B)
    pivot = pl.ds(pl.multiple_of(row_block * B, B), B)
    copies = [pltpu.make_async_copy(matrix.at[pivot], top, sem.at[2 * N_COL])]
    for j in range(N_COL):
        copies.append(pltpu.make_async_copy(
            matrix.at[pivot, lanes], messages.at[j, pl.ds(SHARE, B)], sem.at[j]))
        for h in range(2):
            copies.append(pltpu.make_async_copy(
                matrix.at[pl.ds((h * N_COL + j) * HALF, HALF), lanes], messages.at[j, pl.ds(h * HALF, HALF)],
                sem.at[2 * N_COL + 1 + 2 * j + h]))
    for copy in copies:
        copy.start()
    for copy in copies:
        copy.wait()


def select_kernel(first, messages, corner, one, two, sem):
    k0 = first[0]
    copies = []
    for t in range(STEPS):
        owner = lax.rem(k0 + t, N_COL)
        lanes = pl.ds(t * B, B)
        for n, (target, start, size) in enumerate((
                (corner.at[0, :, lanes], SHARE, 64), (corner.at[1, :, lanes], SHARE + 64, 64),
                (one.at[:, lanes], 0, HALF), (two.at[:, lanes], HALF, HALF))):
            copies.append(pltpu.make_async_copy(messages.at[owner, pl.ds(start, size)], target, sem.at[t, n]))
    for copy in copies:
        copy.start()
    for copy in copies:
        copy.wait()


def pick(refs, index, target, sem):
    for n, ref in enumerate(refs):
        @pl.when(index == n)
        def _():
            pltpu.make_async_copy(ref, target, sem).start()
    return pltpu.make_async_copy(refs[0], target, sem)


def ring_pieces(own, near, far):
    return [(own.at[0], own.at[1]), (near.at[0, 0], near.at[0, 1]),
            (far.at[0], far.at[1]), (near.at[1, 0], near.at[1, 1])]


def bring_corner(first, refs, target, sem):
    k0, p = first[0], lax.axis_index("row")
    z = lax.div(p, 2)
    core = lax.rem(p, 2)
    pieces = ring_pieces(*refs[0:3]) + ring_pieces(*refs[3:6])
    waits = []
    for a in range(STEPS):
        source = lax.rem(k0 + a, N_ROW)
        dz = lax.rem(z - lax.div(source, 2) + 4, 4)
        index = jnp.where(lax.rem(source, 2) == core, 0, 4) + dz
        for h in range(2):
            waits.append(pick([piece[h] for piece in pieces], index,
                              target.at[pl.ds(a * B + h * 64, 64)], sem.at[a, h]))
    for wait in waits:
        wait.wait()


def bring_tops(first, tops, target, sem):
    copies = []
    for a in range(STEPS):
        source = lax.rem(first[0] + a, N_ROW)
        copies.append(pltpu.make_async_copy(tops.at[source], target.at[pl.ds(a * B, B)], sem.at[a]))
    for copy in copies:
        copy.start()
    for copy in copies:
        copy.wait()


def load_corner(first, refs, target):
    k0, p = first[0], lax.axis_index("row")
    z = lax.div(p, 2)
    core = lax.rem(p, 2)
    pieces = ring_pieces(*refs[0:3]) + ring_pieces(*refs[3:6])
    for a in range(STEPS):
        source = lax.rem(k0 + a, N_ROW)
        dz = lax.rem(z - lax.div(source, 2) + 4, 4)
        index = jnp.where(lax.rem(source, 2) == core, 0, 4) + dz
        for n, piece in enumerate(pieces):
            @pl.when(index == n)
            def _():
                for h in range(2):
                    target[a * B + h * 64:a * B + h * 64 + 64, :] = piece[h][...]


def largest(value):
    value = jnp.abs(value)
    return jnp.max(value.reshape(-1, 8, value.shape[-1]), axis=0)


def factor_kernel(first, lower, upper, *refs):
    corners, tops = refs[:6], refs[6]
    right_all, patch, safe, cur, rows, panel, special, n_own, m_own, sem_top = refs[7:]
    k0, p, q, own_col, own_row, col_block, row_block = place(first)
    copies = []
    for a in range(STEPS):
        source = lax.rem(k0 + a, N_ROW)
        copies.append(pltpu.make_async_copy(tops.at[source], rows.at[pl.ds(a * B, B)], sem_top.at[a]))
    for copy in copies:
        copy.start()
    load_corner(first, corners, cur)
    ones = jnp.where(lax.broadcasted_iota(jnp.int32, (B, B), 0) == lax.broadcasted_iota(jnp.int32, (B, B), 1),
                     jnp.float32(1.0), jnp.float32(0.0))
    peak_col = jnp.zeros((8, B), F32)
    peak_row = jnp.zeros((8, WIDE), F32)
    for t in range(STEPS):
        here = slice(t * B, (t + 1) * B)
        diagonal = cur[here, here]
        cur[here, here] = ones
        left = mul(wide(split(cur[:, here])), tall(split(upper[t])))
        right = mul(wide(split(lower[t])), tall(split(cur[here, :])))
        peak_col = jnp.maximum(peak_col, largest(left))
        peak_row = jnp.maximum(peak_row, largest(right))

        @pl.when(own_col == t)
        def _():
            panel[...] = left
            m_own[...] = jnp.zeros((WIDE, B), F32)
            m_own[:(t + 1) * B, :] = left[:(t + 1) * B]

        @pl.when(own_row == t)
        def _():
            n_own[...] = jnp.zeros((B, WIDE), F32)
            n_own[:, :(t + 1) * B] = right[:, :(t + 1) * B]

            @pl.when(own_col == t)
            def _():
                special[...] = diagonal
        cur[:, here] = jnp.zeros((WIDE, B), F32)
        cur[here, :] = jnp.zeros((B, WIDE), F32)
        lefts = wide(split(left))
        rights = tall(split(right))
        for start in range(0, WIDE, TILE):
            cur[:, start:start + TILE] -= mul(lefts, rights[:, start:start + TILE])

    @pl.when((own_col < own_row) & (own_row < STEPS))
    def _():
        special[...] = panel[pl.ds(pl.multiple_of(own_row * B, B), B), :]
    peak = jnp.maximum(jnp.max(peak_col), jnp.max(peak_row))
    safe[0] = jnp.where(peak < SAFE, 1, 0)
    for copy in copies:
        copy.wait()
    own = pl.ds(pl.multiple_of(jnp.minimum(own_row, STEPS - 1) * B, B), B)
    left = wide(split(cur[...]))
    left_own = wide(split(n_own[...]))
    for start in range(0, COLS, TILE):
        size = min(TILE, COLS - start)
        lanes = slice(start, start + size)
        block = ((lax.broadcasted_iota(jnp.int32, (1, size), 1) + start) >> 7) * N_COL + q
        values = tall(split(rows[:, lanes]))
        high, low = split(jnp.where(block > k0 + STEPS - 1, mul(left, values), 0.0))
        for n, part in enumerate((high, high, low)):
            right_all[n * WIDE:(n + 1) * WIDE, lanes] = part
        patch[:, lanes] = jnp.where(block > k0 + own_row, mul(left_own, values), rows[own, lanes])
    own_lanes = pl.ds(pl.multiple_of(col_block * B, B), B)

    @pl.when(own_col < STEPS)
    def _():
        high, low = split(m_own[...])
        for n, part in enumerate((high, high, low)):
            right_all[n * WIDE:(n + 1) * WIDE, own_lanes] = part

    @pl.when((own_col <= own_row) & (own_row < STEPS))
    def _():
        patch[:, own_lanes] = special[...]


def near_copies(near, raw, sem):
    q = lax.axis_index("col")
    x = lax.div(q, 4)
    y = lax.rem(q, 4)
    copies = []
    for dx in range(4):
        for dy in range(4):
            owner = lax.rem(x + 4 - dx, 4) * 4 + lax.rem(y + 4 - dy, 4)
            copies.append(pltpu.make_async_copy(
                near[2 * dx + dy // 2].at[dy % 2], raw.at[owner], sem.at[len(copies)]))
    return copies


def row_blocks(start, count, p):
    return ((lax.broadcasted_iota(jnp.int32, (count, B), 0) + start) >> 7) * N_ROW + p


def left_kernel(offset, first, *refs):
    left, raw, buffer, sem, sem_out = refs[-5:]
    k0, p = first[0], lax.axis_index("row")
    if offset:
        copies = [pltpu.make_async_copy(refs[0].at[n], raw.at[n], sem.at[n]) for n in range(N_COL)]
    else:
        copies = near_copies(refs[:8], raw, sem)
    for copy in copies:
        copy.start()
    for copy in copies:
        copy.wait()
    outs = []
    for s in range(4):
        span = slice(s * 4 * HALF, (s + 1) * 4 * HALF)
        live = row_blocks(span.start + offset, 4 * HALF, p) > k0 + STEPS - 1
        for t in range(STEPS):
            value = jnp.concatenate([raw[n, :, t * B:(t + 1) * B] for n in range(4 * s, 4 * s + 4)], axis=0)
            high, low = split(jnp.where(live, value, 0.0))
            for m, part in enumerate((high, low, high)):
                buffer[span, m * WIDE + t * B:m * WIDE + (t + 1) * B] = part
        outs.append(pltpu.make_async_copy(
            buffer.at[pl.ds(span.start, 4 * HALF)], left.at[pl.ds(offset + span.start, 4 * HALF)], sem_out.at[s]))
        outs[-1].start()
    for copy in outs:
        copy.wait()


def patch_kernel(first, full, patch, out, sem):
    own_row, row_block = place(first)[4], place(first)[6]

    @pl.when(own_row < STEPS)
    def _():
        copy = pltpu.make_async_copy(patch, out.at[pl.ds(pl.multiple_of(row_block * B, B), B)], sem)
        copy.start()
        copy.wait()


def stepwise_corner_kernel(first, lower, upper, *refs):
    c_hi, c_lo, p_hi, p_lo, cur, sem = refs[6:]
    bring_corner(first, refs[:6], cur, sem)
    for t in range(STEPS - 1):
        here = slice(t * B, (t + 1) * B)
        after = slice((t + 1) * B, WIDE)
        tops = split(dot3(split(lower[t]), split(cur[here, after])))
        panels = split(dot3(split(cur[after, here]), split(upper[t])))
        c_hi[here, after], c_lo[here, after] = tops
        p_hi[after, here], p_lo[after, here] = panels
        cur[after, after] -= dot3(panels, tops)


def stepwise_top_kernel(first, lower, p_hi, p_lo, tops, t_hi, t_lo, patch, cur, sem):
    k0, p, q, own_col, own_row, col_block, row_block = place(first)
    bring_tops(first, tops, cur, sem)
    lane_block = (lax.broadcasted_iota(jnp.int32, (1, COLS), 1) >> 7) * N_COL + q
    for t in range(STEPS):
        here = slice(t * B, (t + 1) * B)
        after = slice((t + 1) * B, WIDE)
        live = lane_block > k0 + t
        top = jnp.where(live, dot3(split(lower[t]), split(cur[here, :])), 0.0)
        tops = split(top)
        t_hi[here, :], t_lo[here, :] = tops

        @pl.when(own_row == t)
        def _():
            patch[...] = jnp.where(live, top, cur[here, :])
            if t > 0:
                @pl.when(own_col < t)
                def _():
                    source = pl.ds(pl.multiple_of(own_col * B, B), B)
                    target = pl.ds(pl.multiple_of(col_block * B, B), B)
                    patch[:, target] = p_hi[here, source].astype(F32) + p_lo[here, source].astype(F32)
        if t + 1 < STEPS:
            cur[after, :] -= dot3((p_hi[after, here], p_lo[after, here]), tops)


def stepwise_update_kernel(first, patch, upper, t_hi, t_lo, c_hi, c_lo, matrix, *refs):
    near, far = refs[:8], refs[8]
    out, raw, rows, high, low, panel, sem_raw, sem_far, sem_in, sem_patch = refs[9:]
    k0, p, q, own_col, own_row, col_block, row_block = place(first)
    copies = near_copies(near, raw.at[pl.ds(0, N_COL)], sem_raw)
    copies += [pltpu.make_async_copy(far, raw.at[pl.ds(N_COL, N_COL)], sem_far),
               pltpu.make_async_copy(matrix, rows, sem_in)]
    for copy in copies:
        copy.start()
    for copy in copies:
        copy.wait()
    own = pl.ds(pl.multiple_of(col_block * B, B), B)

    @pl.loop(0, 4)
    def _(s):
        start = pl.multiple_of(s * PART, PART)
        span = pl.ds(start, PART)
        block = row_blocks(start, PART, p)
        for t in range(STEPS):
            lanes = slice(t * B, (t + 1) * B)
            value = jnp.concatenate([raw[8 * s + n, :, lanes] for n in range(8)], axis=0)
            if t > 0:
                value = value - dot3((high[:, :t * B], low[:, :t * B]), (c_hi[:t * B, lanes], c_lo[:t * B, lanes]))
            value = jnp.where(block > k0 + t, dot3(split(value), split(upper[t])), 0.0)
            high[:, lanes], low[:, lanes] = split(value)

            @pl.when(own_col == t)
            def _():
                panel[...] = value
        for start in range(0, COLS, TILE):
            lanes = slice(start, min(start + TILE, COLS))
            rows[span, lanes] -= dot3((high[...], low[...]), (t_hi[:, lanes], t_lo[:, lanes]))

        @pl.when(own_col < STEPS)
        def _():
            rows[span, own] = jnp.where(block > k0 + own_col, panel[...], rows[span, own])
    copy = pltpu.make_async_copy(rows, out, sem_in)
    copy.start()
    copy.wait()

    @pl.when(own_row < STEPS)
    def _():
        last = pltpu.make_async_copy(patch, out.at[pl.ds(pl.multiple_of(row_block * B, B), B)], sem_patch)
        last.start()
        last.wait()


def shards(matrix, first_step, lower_inverse, upper_inverse):
    def shape(*dims, dtype=F32):
        return jax.ShapeDtypeStruct(dims, dtype)

    dma = pltpu.SemaphoreType.DMA

    def call(kernel, outs, in_specs, out_specs, scratch, args, flops=1_000_000, megabytes=48, **kwargs):
        return pl.pallas_call(
            kernel, out_shape=outs, in_specs=[SM] + in_specs, out_specs=out_specs, scratch_shapes=scratch,
            compiler_params=params(megabytes),
            cost_estimate=pl.CostEstimate(flops=flops, bytes_accessed=4_000_000, transcendentals=0),
            **kwargs,
        )(first_step, *args)

    def along_x(value, distance):
        return lax.ppermute(value, "col", [(i, (i + 4 * distance) % N_COL) for i in range(N_COL)])

    def along_y(value, distance):
        return lax.ppermute(value, "col", [(i, i // 4 * 4 + (i + distance) % 4) for i in range(N_COL)])

    def along_z(value, distance):
        return lax.ppermute(value, "row", [(i, (i + 2 * distance) % N_ROW) for i in range(N_ROW)])

    def swap(value):
        return lax.ppermute(value, "row", [(i, i ^ 1) for i in range(N_ROW)])

    def depth(value):
        ahead, back = along_z(value, 1), along_z(value, 3)
        far = jnp.stack([along_z(ahead[0], 1), along_z(back[1], 3)])
        mine = (value, jnp.stack([ahead, back]), far)
        return mine + tuple(swap(v) for v in mine)

    def ring(move, pieces):
        a, b = jnp.stack(pieces[:2]), jnp.stack(pieces[2:])
        a1, b1 = move(a, 1), move(b, 1)
        a3, b3 = move(a, 3), move(b, 3)
        a2, b2 = move(a1, 1), move(b3, 3)
        return [a, b, a1, b1, a2, b2, a3, b3]

    messages, top = call(send_kernel, [shape(N_COL, SHARE + B, B), shape(B, COLS)], [ANY], [VM] * 2,
                         [dma((4 * N_COL + 1,))], [matrix])
    tops = lax.all_gather(top, "row")
    got = lax.all_to_all(messages, "col", 0, 0)
    corner, one, two = call(select_kernel, [shape(2, 64, WIDE)] + [shape(HALF, WIDE)] * 2, [ANY], [VM] * 3,
                            [dma((STEPS, 4))], [got])
    far = lax.all_gather(two, "col")
    corners = depth(corner)
    near = ring(along_x, [one] + [along_y(one, d) for d in (1, 2, 3)])

    right, patch, safe = call(
        factor_kernel,
        [shape(3 * WIDE, COLS, dtype=BF16), shape(B, COLS), shape(1, dtype=jnp.int32)],
        [VM] * 8 + [ANY], [VM] * 2 + [SM],
        [pltpu.VMEM((WIDE, WIDE), F32), pltpu.VMEM((WIDE, COLS), F32), pltpu.VMEM((WIDE, B), F32),
         pltpu.VMEM((B, B), F32), pltpu.VMEM((B, WIDE), F32), pltpu.VMEM((WIDE, B), F32),
         dma((STEPS,))],
        [lower_inverse, upper_inverse, *corners, tops], flops=12_000_000_000)
    left = None
    for offset, shares in ((0, near), (ROWS // 2, [far])):
        held = [] if left is None else [left]
        left = call(
            functools.partial(left_kernel, offset), shape(ROWS, 3 * WIDE, dtype=BF16), [ANY] * len(shares + held), ANY,
            [pltpu.VMEM((N_COL, HALF, WIDE), F32), pltpu.VMEM((ROWS // 2, 3 * WIDE), BF16),
             dma((N_COL,)), dma((4,))],
            shares + held, flops=2_000_000_000, input_output_aliases={2: 0} if held else {})

    def together():
        k0 = first_step[0]
        p, q = lax.axis_index("row"), lax.axis_index("col")
        row_block = jnp.arange(ROWS, dtype=jnp.int32) // B * N_ROW + p
        col_block = jnp.arange(COLS, dtype=jnp.int32) // B * N_COL + q
        taken = (row_block >= k0 + STEPS)[:, None] & ((col_block >= k0) & (col_block < k0 + STEPS))[None, :]
        full = jnp.where(taken, jnp.float32(0.0), matrix) + mul(left, right)
        return call(patch_kernel, shape(ROWS, COLS), [ANY, VM], ANY, [dma], [full, patch], megabytes=60,
                    input_output_aliases={1: 0})

    def stepwise():
        c_hi, c_lo, p_hi, p_lo = call(
            stepwise_corner_kernel, [shape(WIDE, WIDE, dtype=BF16)] * 4, [VM] * 2 + [ANY] * 6, [VM] * 4,
            [pltpu.VMEM((WIDE, WIDE), F32), dma((STEPS, 2))], [lower_inverse, upper_inverse, *corners])
        t_hi, t_lo, last = call(
            stepwise_top_kernel, [shape(WIDE, COLS, dtype=BF16)] * 2 + [shape(B, COLS)],
            [VM] * 3 + [ANY], [VM] * 3, [pltpu.VMEM((WIDE, COLS), F32), dma((STEPS,))],
            [lower_inverse, p_hi, p_lo, tops])
        return call(
            stepwise_update_kernel, shape(ROWS, COLS), [VM] * 6 + [ANY] * 10, ANY,
            [pltpu.VMEM((2 * N_COL, HALF, WIDE), F32), pltpu.VMEM((ROWS, COLS), F32), pltpu.VMEM((PART, WIDE), BF16),
             pltpu.VMEM((PART, WIDE), BF16), pltpu.VMEM((PART, B), F32), dma((N_COL,)), dma, dma, dma],
            [last, upper_inverse, t_hi, t_lo, c_hi, c_lo, matrix, *near, far], megabytes=56)

    return lax.cond(safe[0] == 1, together, stepwise)


def solution(mesh):
    placed = (P("row", "col"), P(), P(), P())
    return jax.shard_map(
        shards, mesh=mesh, in_specs=placed, out_specs=P("row", "col"), check_vma=False
    )
```

```python
import functools

import jax
import jax.numpy as jnp
from jax import lax
from jax.experimental import pallas as pl
from jax.experimental.pallas import tpu as pltpu
from jax.sharding import PartitionSpec as P

B = 128
STEPS = 6
ROWS = 2304
COLS = 1152
SHARE = 144
HALF = 72
N_ROW = 8
N_COL = 16
WIDE = STEPS * B
PART = 8 * HALF
SAFE = 100.0
TILE = 256

F32 = jnp.float32
BF16 = jnp.bfloat16
ANY = pl.BlockSpec(memory_space=pl.ANY)
VM = pl.BlockSpec(memory_space=pltpu.VMEM)
SM = pl.BlockSpec(memory_space=pltpu.SMEM)


def params(mebibytes):
    return pltpu.CompilerParams(vmem_limit_bytes=mebibytes * 1024 * 1024)


def split(value):
    high = value.astype(BF16)
    low = (value - high.astype(F32)).astype(BF16)
    return high, low


def mul(left, right):
    return jnp.dot(left, right, preferred_element_type=F32)


def wide(parts):
    return jnp.concatenate([parts[0], parts[1], parts[0]], axis=1)


def tall(parts):
    return jnp.concatenate([parts[0], parts[0], parts[1]], axis=0)


def dot3(left, right):
    lh, ll = left
    rh, rl = right
    return mul(lh, rh) + (mul(ll, rh) + mul(lh, rl))


def place(first):
    k0 = first[0]
    p = lax.axis_index("row")
    q = lax.axis_index("col")
    own_col = lax.rem(q - k0 + 8 * N_COL, N_COL)
    own_row = lax.rem(p - k0 + 16 * N_ROW, N_ROW)
    col_block = lax.div(k0 + jnp.minimum(own_col, STEPS - 1), N_COL)
    row_block = lax.div(k0 + jnp.minimum(own_row, STEPS - 1), N_ROW)
    return k0, p, q, own_col, own_row, col_block, row_block


def send_kernel(first, matrix, messages, top, sem):
    k0, p, q, own_col, own_row, col_block, row_block = place(first)
    lanes = pl.ds(pl.multiple_of(col_block * B, B), B)
    pivot = pl.ds(pl.multiple_of(row_block * B, B), B)
    copies = [pltpu.make_async_copy(matrix.at[pivot], top, sem.at[2 * N_COL])]
    for j in range(N_COL):
        copies.append(pltpu.make_async_copy(
            matrix.at[pivot, lanes], messages.at[j, pl.ds(SHARE, B)], sem.at[j]))
        for h in range(2):
            copies.append(pltpu.make_async_copy(
                matrix.at[pl.ds((h * N_COL + j) * HALF, HALF), lanes], messages.at[j, pl.ds(h * HALF, HALF)],
                sem.at[2 * N_COL + 1 + 2 * j + h]))
    for copy in copies:
        copy.start()
    for copy in copies:
        copy.wait()


def select_kernel(first, messages, corner, one, two, sem):
    k0 = first[0]
    copies = []
    for t in range(STEPS):
        owner = lax.rem(k0 + t, N_COL)
        lanes = pl.ds(t * B, B)
        for n, (target, start, size) in enumerate((
                (corner.at[0, :, lanes], SHARE, 64), (corner.at[1, :, lanes], SHARE + 64, 64),
                (one.at[:, lanes], 0, HALF), (two.at[:, lanes], HALF, HALF))):
            copies.append(pltpu.make_async_copy(messages.at[owner, pl.ds(start, size)], target, sem.at[t, n]))
    for copy in copies:
        copy.start()
    for copy in copies:
        copy.wait()


def pick(refs, index, target, sem):
    for n, ref in enumerate(refs):
        @pl.when(index == n)
        def _():
            pltpu.make_async_copy(ref, target, sem).start()
    return pltpu.make_async_copy(refs[0], target, sem)


def ring_pieces(own, near, far):
    return [(own.at[0], own.at[1]), (near.at[0, 0], near.at[0, 1]),
            (far.at[0], far.at[1]), (near.at[1, 0], near.at[1, 1])]


def bring_corner(first, refs, target, sem):
    k0, p = first[0], lax.axis_index("row")
    z = lax.div(p, 2)
    core = lax.rem(p, 2)
    pieces = ring_pieces(*refs[0:3]) + ring_pieces(*refs[3:6])
    waits = []
    for a in range(STEPS):
        source = lax.rem(k0 + a, N_ROW)
        dz = lax.rem(z - lax.div(source, 2) + 4, 4)
        index = jnp.where(lax.rem(source, 2) == core, 0, 4) + dz
        for h in range(2):
            waits.append(pick([piece[h] for piece in pieces], index,
                              target.at[pl.ds(a * B + h * 64, 64)], sem.at[a, h]))
    for wait in waits:
        wait.wait()


def bring_tops(first, tops, target, sem):
    copies = []
    for a in range(STEPS):
        source = lax.rem(first[0] + a, N_ROW)
        copies.append(pltpu.make_async_copy(tops.at[source], target.at[pl.ds(a * B, B)], sem.at[a]))
    for copy in copies:
        copy.start()
    for copy in copies:
        copy.wait()


def load_corner(first, refs, target):
    k0, p = first[0], lax.axis_index("row")
    z = lax.div(p, 2)
    core = lax.rem(p, 2)
    pieces = ring_pieces(*refs[0:3]) + ring_pieces(*refs[3:6])
    for a in range(STEPS):
        source = lax.rem(k0 + a, N_ROW)
        dz = lax.rem(z - lax.div(source, 2) + 4, 4)
        index = jnp.where(lax.rem(source, 2) == core, 0, 4) + dz
        for n, piece in enumerate(pieces):
            @pl.when(index == n)
            def _():
                for h in range(2):
                    target[a * B + h * 64:a * B + h * 64 + 64, :] = piece[h][...]


def largest(value):
    value = jnp.abs(value)
    return jnp.max(value.reshape(-1, 8, value.shape[-1]), axis=0)


def factor_kernel(first, lower, upper, *refs):
    corners, tops = refs[:6], refs[6]
    right_all, patch, safe, cur, rows, panel, special, n_own, m_own, sem_top = refs[7:]
    k0, p, q, own_col, own_row, col_block, row_block = place(first)
    copies = []
    for a in range(STEPS):
        source = lax.rem(k0 + a, N_ROW)
        copies.append(pltpu.make_async_copy(tops.at[source], rows.at[pl.ds(a * B, B)], sem_top.at[a]))
    for copy in copies:
        copy.start()
    load_corner(first, corners, cur)
    ones = jnp.where(lax.broadcasted_iota(jnp.int32, (B, B), 0) == lax.broadcasted_iota(jnp.int32, (B, B), 1),
                     jnp.float32(1.0), jnp.float32(0.0))
    peak_col = jnp.zeros((8, B), F32)
    peak_row = jnp.zeros((8, WIDE), F32)
    for t in range(STEPS):
        here = slice(t * B, (t + 1) * B)
        diagonal = cur[here, here]
        cur[here, here] = ones
        left = mul(wide(split(cur[:, here])), tall(split(upper[t])))
        right = mul(wide(split(lower[t])), tall(split(cur[here, :])))
        peak_col = jnp.maximum(peak_col, largest(left))
        peak_row = jnp.maximum(peak_row, largest(right))

        @pl.when(own_col == t)
        def _():
            panel[...] = left
            m_own[...] = jnp.zeros((WIDE, B), F32)
            m_own[:(t + 1) * B, :] = left[:(t + 1) * B]

        @pl.when(own_row == t)
        def _():
            n_own[...] = jnp.zeros((B, WIDE), F32)
            n_own[:, :(t + 1) * B] = right[:, :(t + 1) * B]

            @pl.when(own_col == t)
            def _():
                special[...] = diagonal
        cur[:, here] = jnp.zeros((WIDE, B), F32)
        cur[here, :] = jnp.zeros((B, WIDE), F32)
        lefts = wide(split(left))
        rights = tall(split(right))
        for start in range(0, WIDE, TILE):
            cur[:, start:start + TILE] -= mul(lefts, rights[:, start:start + TILE])

    @pl.when((own_col < own_row) & (own_row < STEPS))
    def _():
        special[...] = panel[pl.ds(pl.multiple_of(own_row * B, B), B), :]
    peak = jnp.maximum(jnp.max(peak_col), jnp.max(peak_row))
    safe[0] = jnp.where(peak < SAFE, 1, 0)
    for copy in copies:
        copy.wait()
    own = pl.ds(pl.multiple_of(jnp.minimum(own_row, STEPS - 1) * B, B), B)
    left = wide(split(cur[...]))
    left_own = wide(split(n_own[...]))
    for start in range(0, COLS, TILE):
        size = min(TILE, COLS - start)
        lanes = slice(start, start + size)
        block = ((lax.broadcasted_iota(jnp.int32, (1, size), 1) + start) >> 7) * N_COL + q
        values = tall(split(rows[:, lanes]))
        high, low = split(jnp.where(block > k0 + STEPS - 1, mul(left, values), 0.0))
        for n, part in enumerate((high, high, low)):
            right_all[n * WIDE:(n + 1) * WIDE, lanes] = part
        patch[:, lanes] = jnp.where(block > k0 + own_row, mul(left_own, values), rows[own, lanes])
    own_lanes = pl.ds(pl.multiple_of(col_block * B, B), B)

    @pl.when(own_col < STEPS)
    def _():
        high, low = split(m_own[...])
        for n, part in enumerate((high, high, low)):
            right_all[n * WIDE:(n + 1) * WIDE, own_lanes] = part

    @pl.when((own_col <= own_row) & (own_row < STEPS))
    def _():
        patch[:, own_lanes] = special[...]


def near_copies(near, raw, sem):
    q = lax.axis_index("col")
    x = lax.div(q, 4)
    y = lax.rem(q, 4)
    copies = []
    for dx in range(4):
        for dy in range(4):
            owner = lax.rem(x + 4 - dx, 4) * 4 + lax.rem(y + 4 - dy, 4)
            copies.append(pltpu.make_async_copy(
                near[2 * dx + dy // 2].at[dy % 2], raw.at[owner], sem.at[len(copies)]))
    return copies


def row_blocks(start, count, p):
    return ((lax.broadcasted_iota(jnp.int32, (count, B), 0) + start) >> 7) * N_ROW + p


def left_kernel(offset, first, *refs):
    left, raw, buffer, sem, sem_out = refs[-5:]
    k0, p = first[0], lax.axis_index("row")
    if offset:
        copies = [pltpu.make_async_copy(refs[0].at[n], raw.at[n], sem.at[n]) for n in range(N_COL)]
    else:
        copies = near_copies(refs[:8], raw, sem)
    for copy in copies:
        copy.start()
    for copy in copies:
        copy.wait()
    outs = []
    for s in range(4):
        span = slice(s * 4 * HALF, (s + 1) * 4 * HALF)
        live = row_blocks(span.start + offset, 4 * HALF, p) > k0 + STEPS - 1
        for t in range(STEPS):
            value = jnp.concatenate([raw[n, :, t * B:(t + 1) * B] for n in range(4 * s, 4 * s + 4)], axis=0)
            high, low = split(jnp.where(live, value, 0.0))
            for m, part in enumerate((high, low, high)):
                buffer[span, m * WIDE + t * B:m * WIDE + (t + 1) * B] = part
        outs.append(pltpu.make_async_copy(
            buffer.at[pl.ds(span.start, 4 * HALF)], left.at[pl.ds(offset + span.start, 4 * HALF)], sem_out.at[s]))
        outs[-1].start()
    for copy in outs:
        copy.wait()


def patch_kernel(first, full, patch, out, sem):
    own_row, row_block = place(first)[4], place(first)[6]

    @pl.when(own_row < STEPS)
    def _():
        copy = pltpu.make_async_copy(patch, out.at[pl.ds(pl.multiple_of(row_block * B, B), B)], sem)
        copy.start()
        copy.wait()


def stepwise_corner_kernel(first, lower, upper, *refs):
    c_hi, c_lo, p_hi, p_lo, cur, sem = refs[6:]
    bring_corner(first, refs[:6], cur, sem)
    for t in range(STEPS - 1):
        here = slice(t * B, (t + 1) * B)
        after = slice((t + 1) * B, WIDE)
        tops = split(dot3(split(lower[t]), split(cur[here, after])))
        panels = split(dot3(split(cur[after, here]), split(upper[t])))
        c_hi[here, after], c_lo[here, after] = tops
        p_hi[after, here], p_lo[after, here] = panels
        cur[after, after] -= dot3(panels, tops)


def stepwise_top_kernel(first, lower, p_hi, p_lo, tops, t_hi, t_lo, patch, cur, sem):
    k0, p, q, own_col, own_row, col_block, row_block = place(first)
    bring_tops(first, tops, cur, sem)
    lane_block = (lax.broadcasted_iota(jnp.int32, (1, COLS), 1) >> 7) * N_COL + q
    for t in range(STEPS):
        here = slice(t * B, (t + 1) * B)
        after = slice((t + 1) * B, WIDE)
        live = lane_block > k0 + t
        top = jnp.where(live, dot3(split(lower[t]), split(cur[here, :])), 0.0)
        tops = split(top)
        t_hi[here, :], t_lo[here, :] = tops

        @pl.when(own_row == t)
        def _():
            patch[...] = jnp.where(live, top, cur[here, :])
            if t > 0:
                @pl.when(own_col < t)
                def _():
                    source = pl.ds(pl.multiple_of(own_col * B, B), B)
                    target = pl.ds(pl.multiple_of(col_block * B, B), B)
                    patch[:, target] = p_hi[here, source].astype(F32) + p_lo[here, source].astype(F32)
        if t + 1 < STEPS:
            cur[after, :] -= dot3((p_hi[after, here], p_lo[after, here]), tops)


def stepwise_update_kernel(first, patch, upper, t_hi, t_lo, c_hi, c_lo, matrix, *refs):
    near, far = refs[:8], refs[8]
    out, raw, rows, high, low, panel, sem_raw, sem_far, sem_in, sem_patch = refs[9:]
    k0, p, q, own_col, own_row, col_block, row_block = place(first)
    copies = near_copies(near, raw.at[pl.ds(0, N_COL)], sem_raw)
    copies += [pltpu.make_async_copy(far, raw.at[pl.ds(N_COL, N_COL)], sem_far),
               pltpu.make_async_copy(matrix, rows, sem_in)]
    for copy in copies:
        copy.start()
    for copy in copies:
        copy.wait()
    own = pl.ds(pl.multiple_of(col_block * B, B), B)

    @pl.loop(0, 4)
    def _(s):
        start = pl.multiple_of(s * PART, PART)
        span = pl.ds(start, PART)
        block = row_blocks(start, PART, p)
        for t in range(STEPS):
            lanes = slice(t * B, (t + 1) * B)
            value = jnp.concatenate([raw[8 * s + n, :, lanes] for n in range(8)], axis=0)
            if t > 0:
                value = value - dot3((high[:, :t * B], low[:, :t * B]), (c_hi[:t * B, lanes], c_lo[:t * B, lanes]))
            value = jnp.where(block > k0 + t, dot3(split(value), split(upper[t])), 0.0)
            high[:, lanes], low[:, lanes] = split(value)

            @pl.when(own_col == t)
            def _():
                panel[...] = value
        for start in range(0, COLS, TILE):
            lanes = slice(start, min(start + TILE, COLS))
            rows[span, lanes] -= dot3((high[...], low[...]), (t_hi[:, lanes], t_lo[:, lanes]))

        @pl.when(own_col < STEPS)
        def _():
            rows[span, own] = jnp.where(block > k0 + own_col, panel[...], rows[span, own])
    copy = pltpu.make_async_copy(rows, out, sem_in)
    copy.start()
    copy.wait()

    @pl.when(own_row < STEPS)
    def _():
        last = pltpu.make_async_copy(patch, out.at[pl.ds(pl.multiple_of(row_block * B, B), B)], sem_patch)
        last.start()
        last.wait()


def shards(matrix, first_step, lower_inverse, upper_inverse):
    def shape(*dims, dtype=F32):
        return jax.ShapeDtypeStruct(dims, dtype)

    dma = pltpu.SemaphoreType.DMA

    def call(kernel, outs, in_specs, out_specs, scratch, args, flops=1_000_000, megabytes=48, **kwargs):
        return pl.pallas_call(
            kernel, out_shape=outs, in_specs=[SM] + in_specs, out_specs=out_specs, scratch_shapes=scratch,
            compiler_params=params(megabytes),
            cost_estimate=pl.CostEstimate(flops=flops, bytes_accessed=4_000_000, transcendentals=0),
            **kwargs,
        )(first_step, *args)

    def along_x(value, distance):
        return lax.ppermute(value, "col", [(i, (i + 4 * distance) % N_COL) for i in range(N_COL)])

    def along_y(value, distance):
        return lax.ppermute(value, "col", [(i, i // 4 * 4 + (i + distance) % 4) for i in range(N_COL)])

    def along_z(value, distance):
        return lax.ppermute(value, "row", [(i, (i + 2 * distance) % N_ROW) for i in range(N_ROW)])

    def swap(value):
        return lax.ppermute(value, "row", [(i, i ^ 1) for i in range(N_ROW)])

    def depth(value):
        ahead, back = along_z(value, 1), along_z(value, 3)
        far = jnp.stack([along_z(ahead[0], 1), along_z(back[1], 3)])
        mine = (value, jnp.stack([ahead, back]), far)
        return mine + tuple(swap(v) for v in mine)

    def ring(move, pieces):
        a, b = jnp.stack(pieces[:2]), jnp.stack(pieces[2:])
        a1, b1 = move(a, 1), move(b, 1)
        a3, b3 = move(a, 3), move(b, 3)
        a2, b2 = move(a1, 1), move(b3, 3)
        return [a, b, a1, b1, a2, b2, a3, b3]

    messages, top = call(send_kernel, [shape(N_COL, SHARE + B, B), shape(B, COLS)], [ANY], [VM] * 2,
                         [dma((4 * N_COL + 1,))], [matrix])
    tops = lax.all_gather(top, "row")
    got = lax.all_to_all(messages, "col", 0, 0)
    corner, one, two = call(select_kernel, [shape(2, 64, WIDE)] + [shape(HALF, WIDE)] * 2, [ANY], [VM] * 3,
                            [dma((STEPS, 4))], [got])
    far = lax.all_gather(two, "col")
    corners = depth(corner)
    near = ring(along_x, [one] + [along_y(one, d) for d in (1, 2, 3)])

    right, patch, safe = call(
        factor_kernel,
        [shape(3 * WIDE, COLS, dtype=BF16), shape(B, COLS), shape(1, dtype=jnp.int32)],
        [VM] * 8 + [ANY], [VM] * 2 + [SM],
        [pltpu.VMEM((WIDE, WIDE), F32), pltpu.VMEM((WIDE, COLS), F32), pltpu.VMEM((WIDE, B), F32),
         pltpu.VMEM((B, B), F32), pltpu.VMEM((B, WIDE), F32), pltpu.VMEM((WIDE, B), F32),
         dma((STEPS,))],
        [lower_inverse, upper_inverse, *corners, tops], flops=12_000_000_000)
    near, patch = lax.optimization_barrier((near, patch))
    left = None
    for offset, shares in ((0, near), (ROWS // 2, [far])):
        held = [] if left is None else [left]
        left = call(
            functools.partial(left_kernel, offset), shape(ROWS, 3 * WIDE, dtype=BF16), [ANY] * len(shares + held), ANY,
            [pltpu.VMEM((N_COL, HALF, WIDE), F32), pltpu.VMEM((ROWS // 2, 3 * WIDE), BF16),
             dma((N_COL,)), dma((4,))],
            shares + held, flops=2_000_000_000, input_output_aliases={2: 0} if held else {})

    def together():
        k0 = first_step[0]
        p, q = lax.axis_index("row"), lax.axis_index("col")
        row_block = jnp.arange(ROWS, dtype=jnp.int32) // B * N_ROW + p
        col_block = jnp.arange(COLS, dtype=jnp.int32) // B * N_COL + q
        taken = (row_block >= k0 + STEPS)[:, None] & ((col_block >= k0) & (col_block < k0 + STEPS))[None, :]
        full = jnp.where(taken, jnp.float32(0.0), matrix) + mul(left, right)
        return call(patch_kernel, shape(ROWS, COLS), [ANY, VM], ANY, [dma], [full, patch], megabytes=60,
                    input_output_aliases={1: 0})

    def stepwise():
        c_hi, c_lo, p_hi, p_lo = call(
            stepwise_corner_kernel, [shape(WIDE, WIDE, dtype=BF16)] * 4, [VM] * 2 + [ANY] * 6, [VM] * 4,
            [pltpu.VMEM((WIDE, WIDE), F32), dma((STEPS, 2))], [lower_inverse, upper_inverse, *corners])
        t_hi, t_lo, last = call(
            stepwise_top_kernel, [shape(WIDE, COLS, dtype=BF16)] * 2 + [shape(B, COLS)],
            [VM] * 3 + [ANY], [VM] * 3, [pltpu.VMEM((WIDE, COLS), F32), dma((STEPS,))],
            [lower_inverse, p_hi, p_lo, tops])
        return call(
            stepwise_update_kernel, shape(ROWS, COLS), [VM] * 6 + [ANY] * 10, ANY,
            [pltpu.VMEM((2 * N_COL, HALF, WIDE), F32), pltpu.VMEM((ROWS, COLS), F32), pltpu.VMEM((PART, WIDE), BF16),
             pltpu.VMEM((PART, WIDE), BF16), pltpu.VMEM((PART, B), F32), dma((N_COL,)), dma, dma, dma],
            [last, upper_inverse, t_hi, t_lo, c_hi, c_lo, matrix, *near, far], megabytes=56)

    return lax.cond(safe[0] == 1, together, stepwise)


def solution(mesh):
    placed = (P("row", "col"), P(), P(), P())
    return jax.shard_map(
        shards, mesh=mesh, in_specs=placed, out_specs=P("row", "col"), check_vma=False
    )
```

```python
import functools

import jax
import jax.numpy as jnp
from jax import lax
from jax.experimental import pallas as pl
from jax.experimental.pallas import tpu as pltpu
from jax.sharding import PartitionSpec as P

B = 128
STEPS = 6
ROWS = 2304
COLS = 1152
SHARE = 144
HALF = 72
N_ROW = 8
N_COL = 16
WIDE = STEPS * B
PART = 8 * HALF
SAFE = 100.0
TILE = 256

F32 = jnp.float32
BF16 = jnp.bfloat16
ANY = pl.BlockSpec(memory_space=pl.ANY)
VM = pl.BlockSpec(memory_space=pltpu.VMEM)
SM = pl.BlockSpec(memory_space=pltpu.SMEM)


def params(mebibytes):
    return pltpu.CompilerParams(vmem_limit_bytes=mebibytes * 1024 * 1024)


def split(value):
    high = value.astype(BF16)
    low = (value - high.astype(F32)).astype(BF16)
    return high, low


def mul(left, right):
    return jnp.dot(left, right, preferred_element_type=F32)


def wide(parts):
    return jnp.concatenate([parts[0], parts[1], parts[0]], axis=1)


def tall(parts):
    return jnp.concatenate([parts[0], parts[0], parts[1]], axis=0)


def dot3(left, right):
    lh, ll = left
    rh, rl = right
    return mul(lh, rh) + (mul(ll, rh) + mul(lh, rl))


def place(first):
    k0 = first[0]
    p = lax.axis_index("row")
    q = lax.axis_index("col")
    own_col = lax.rem(q - k0 + 8 * N_COL, N_COL)
    own_row = lax.rem(p - k0 + 16 * N_ROW, N_ROW)
    col_block = lax.div(k0 + jnp.minimum(own_col, STEPS - 1), N_COL)
    row_block = lax.div(k0 + jnp.minimum(own_row, STEPS - 1), N_ROW)
    return k0, p, q, own_col, own_row, col_block, row_block


def send_kernel(first, matrix, messages, top, sem):
    k0, p, q, own_col, own_row, col_block, row_block = place(first)
    lanes = pl.ds(pl.multiple_of(col_block * B, B), B)
    pivot = pl.ds(pl.multiple_of(row_block * B, B), B)
    copies = [pltpu.make_async_copy(matrix.at[pivot], top, sem.at[2 * N_COL])]
    for j in range(N_COL):
        copies.append(pltpu.make_async_copy(
            matrix.at[pivot, lanes], messages.at[j, pl.ds(SHARE, B)], sem.at[j]))
        for h in range(2):
            copies.append(pltpu.make_async_copy(
                matrix.at[pl.ds((h * N_COL + j) * HALF, HALF), lanes], messages.at[j, pl.ds(h * HALF, HALF)],
                sem.at[2 * N_COL + 1 + 2 * j + h]))
    for copy in copies:
        copy.start()
    for copy in copies:
        copy.wait()


def select_kernel(first, messages, corner, one, two, sem):
    k0 = first[0]
    copies = []
    for t in range(STEPS):
        owner = lax.rem(k0 + t, N_COL)
        lanes = pl.ds(t * B, B)
        for n, (target, start, size) in enumerate((
                (corner.at[0, :, lanes], SHARE, 64), (corner.at[1, :, lanes], SHARE + 64, 64),
                (one.at[:, lanes], 0, HALF), (two.at[:, lanes], HALF, HALF))):
            copies.append(pltpu.make_async_copy(messages.at[owner, pl.ds(start, size)], target, sem.at[t, n]))
    for copy in copies:
        copy.start()
    for copy in copies:
        copy.wait()


def pick(refs, index, target, sem):
    for n, ref in enumerate(refs):
        @pl.when(index == n)
        def _():
            pltpu.make_async_copy(ref, target, sem).start()
    return pltpu.make_async_copy(refs[0], target, sem)


def ring_pieces(own, near, far):
    return [(own.at[0], own.at[1]), (near.at[0, 0], near.at[0, 1]),
            (far.at[0], far.at[1]), (near.at[1, 0], near.at[1, 1])]


def bring_corner(first, refs, target, sem):
    k0, p = first[0], lax.axis_index("row")
    z = lax.div(p, 2)
    core = lax.rem(p, 2)
    pieces = ring_pieces(*refs[0:3]) + ring_pieces(*refs[3:6])
    waits = []
    for a in range(STEPS):
        source = lax.rem(k0 + a, N_ROW)
        dz = lax.rem(z - lax.div(source, 2) + 4, 4)
        index = jnp.where(lax.rem(source, 2) == core, 0, 4) + dz
        for h in range(2):
            waits.append(pick([piece[h] for piece in pieces], index,
                              target.at[pl.ds(a * B + h * 64, 64)], sem.at[a, h]))
    for wait in waits:
        wait.wait()


def bring_tops(first, tops, target, sem):
    copies = []
    for a in range(STEPS):
        source = lax.rem(first[0] + a, N_ROW)
        copies.append(pltpu.make_async_copy(tops.at[source], target.at[pl.ds(a * B, B)], sem.at[a]))
    for copy in copies:
        copy.start()
    for copy in copies:
        copy.wait()


def load_corner(first, refs, target):
    k0, p = first[0], lax.axis_index("row")
    z = lax.div(p, 2)
    core = lax.rem(p, 2)
    pieces = ring_pieces(*refs[0:3]) + ring_pieces(*refs[3:6])
    for a in range(STEPS):
        source = lax.rem(k0 + a, N_ROW)
        dz = lax.rem(z - lax.div(source, 2) + 4, 4)
        index = jnp.where(lax.rem(source, 2) == core, 0, 4) + dz
        for n, piece in enumerate(pieces):
            @pl.when(index == n)
            def _():
                for h in range(2):
                    target[a * B + h * 64:a * B + h * 64 + 64, :] = piece[h][...]


def largest(value):
    value = jnp.abs(value)
    return jnp.max(value.reshape(-1, 8, value.shape[-1]), axis=0)


def factor_kernel(first, lower, upper, *refs):
    corners, tops = refs[:6], refs[6]
    right_all, patch, safe, cur, rows, panel, special, n_own, m_own, sem_top = refs[7:]
    k0, p, q, own_col, own_row, col_block, row_block = place(first)
    copies = []
    for a in range(STEPS):
        source = lax.rem(k0 + a, N_ROW)
        copies.append(pltpu.make_async_copy(tops.at[source], rows.at[pl.ds(a * B, B)], sem_top.at[a]))
    for copy in copies:
        copy.start()
    load_corner(first, corners, cur)
    ones = jnp.where(lax.broadcasted_iota(jnp.int32, (B, B), 0) == lax.broadcasted_iota(jnp.int32, (B, B), 1),
                     jnp.float32(1.0), jnp.float32(0.0))
    peak_col = jnp.zeros((8, B), F32)
    peak_row = jnp.zeros((8, WIDE), F32)
    for t in range(STEPS):
        here = slice(t * B, (t + 1) * B)
        diagonal = cur[here, here]
        cur[here, here] = ones
        left = mul(wide(split(cur[:, here])), tall(split(upper[t])))
        right = mul(wide(split(lower[t])), tall(split(cur[here, :])))
        peak_col = jnp.maximum(peak_col, largest(left))
        peak_row = jnp.maximum(peak_row, largest(right))

        @pl.when(own_col == t)
        def _():
            panel[...] = left
            m_own[...] = jnp.zeros((WIDE, B), F32)
            m_own[:(t + 1) * B, :] = left[:(t + 1) * B]

        @pl.when(own_row == t)
        def _():
            n_own[...] = jnp.zeros((B, WIDE), F32)
            n_own[:, :(t + 1) * B] = right[:, :(t + 1) * B]

            @pl.when(own_col == t)
            def _():
                special[...] = diagonal
        cur[:, here] = jnp.zeros((WIDE, B), F32)
        cur[here, :] = jnp.zeros((B, WIDE), F32)
        lefts = wide(split(left))
        rights = tall(split(right))
        for start in range(0, WIDE, TILE):
            cur[:, start:start + TILE] -= mul(lefts, rights[:, start:start + TILE])

    @pl.when((own_col < own_row) & (own_row < STEPS))
    def _():
        special[...] = panel[pl.ds(pl.multiple_of(own_row * B, B), B), :]
    peak = jnp.maximum(jnp.max(peak_col), jnp.max(peak_row))
    safe[0] = jnp.where(peak < SAFE, 1, 0)
    for copy in copies:
        copy.wait()
    own = pl.ds(pl.multiple_of(jnp.minimum(own_row, STEPS - 1) * B, B), B)
    left = wide(split(cur[...]))
    left_own = wide(split(n_own[...]))
    for start in range(0, COLS, TILE):
        size = min(TILE, COLS - start)
        lanes = slice(start, start + size)
        block = ((lax.broadcasted_iota(jnp.int32, (1, size), 1) + start) >> 7) * N_COL + q
        values = tall(split(rows[:, lanes]))
        high, low = split(jnp.where(block > k0 + STEPS - 1, mul(left, values), 0.0))
        for n, part in enumerate((high, high, low)):
            right_all[n * WIDE:(n + 1) * WIDE, lanes] = part
        patch[:, lanes] = jnp.where(block > k0 + own_row, mul(left_own, values), rows[own, lanes])
    own_lanes = pl.ds(pl.multiple_of(col_block * B, B), B)

    @pl.when(own_col < STEPS)
    def _():
        high, low = split(m_own[...])
        for n, part in enumerate((high, high, low)):
            right_all[n * WIDE:(n + 1) * WIDE, own_lanes] = part

    @pl.when((own_col <= own_row) & (own_row < STEPS))
    def _():
        patch[:, own_lanes] = special[...]


def near_copies(near, raw, sem):
    q = lax.axis_index("col")
    x = lax.div(q, 4)
    y = lax.rem(q, 4)
    copies = []
    for dx in range(4):
        for dy in range(4):
            owner = lax.rem(x + 4 - dx, 4) * 4 + lax.rem(y + 4 - dy, 4)
            copies.append(pltpu.make_async_copy(
                near[2 * dx + dy // 2].at[dy % 2], raw.at[owner], sem.at[len(copies)]))
    return copies


def row_blocks(start, count, p):
    return ((lax.broadcasted_iota(jnp.int32, (count, B), 0) + start) >> 7) * N_ROW + p


def left_kernel(offset, first, *refs):
    left, raw, buffer, sem, sem_out = refs[-5:]
    k0, p = first[0], lax.axis_index("row")
    if offset:
        copies = [pltpu.make_async_copy(refs[0].at[n], raw.at[n], sem.at[n]) for n in range(N_COL)]
    else:
        copies = near_copies(refs[:8], raw, sem)
    for copy in copies:
        copy.start()
    for copy in copies:
        copy.wait()
    outs = []
    for s in range(4):
        span = slice(s * 4 * HALF, (s + 1) * 4 * HALF)
        live = row_blocks(span.start + offset, 4 * HALF, p) > k0 + STEPS - 1
        for t in range(STEPS):
            value = jnp.concatenate([raw[n, :, t * B:(t + 1) * B] for n in range(4 * s, 4 * s + 4)], axis=0)
            high, low = split(jnp.where(live, value, 0.0))
            for m, part in enumerate((high, low, high)):
                buffer[span, m * WIDE + t * B:m * WIDE + (t + 1) * B] = part
        outs.append(pltpu.make_async_copy(
            buffer.at[pl.ds(span.start, 4 * HALF)], left.at[pl.ds(offset + span.start, 4 * HALF)], sem_out.at[s]))
        outs[-1].start()
    for copy in outs:
        copy.wait()


def patch_kernel(first, full, patch, out, sem):
    own_row, row_block = place(first)[4], place(first)[6]

    @pl.when(own_row < STEPS)
    def _():
        copy = pltpu.make_async_copy(patch, out.at[pl.ds(pl.multiple_of(row_block * B, B), B)], sem)
        copy.start()
        copy.wait()


def stepwise_corner_kernel(first, lower, upper, *refs):
    c_hi, c_lo, p_hi, p_lo, cur, sem = refs[6:]
    bring_corner(first, refs[:6], cur, sem)
    for t in range(STEPS - 1):
        here = slice(t * B, (t + 1) * B)
        after = slice((t + 1) * B, WIDE)
        tops = split(dot3(split(lower[t]), split(cur[here, after])))
        panels = split(dot3(split(cur[after, here]), split(upper[t])))
        c_hi[here, after], c_lo[here, after] = tops
        p_hi[after, here], p_lo[after, here] = panels
        cur[after, after] -= dot3(panels, tops)


def stepwise_top_kernel(first, lower, p_hi, p_lo, tops, t_hi, t_lo, patch, cur, sem):
    k0, p, q, own_col, own_row, col_block, row_block = place(first)
    bring_tops(first, tops, cur, sem)
    lane_block = (lax.broadcasted_iota(jnp.int32, (1, COLS), 1) >> 7) * N_COL + q
    for t in range(STEPS):
        here = slice(t * B, (t + 1) * B)
        after = slice((t + 1) * B, WIDE)
        live = lane_block > k0 + t
        top = jnp.where(live, dot3(split(lower[t]), split(cur[here, :])), 0.0)
        tops = split(top)
        t_hi[here, :], t_lo[here, :] = tops

        @pl.when(own_row == t)
        def _():
            patch[...] = jnp.where(live, top, cur[here, :])
            if t > 0:
                @pl.when(own_col < t)
                def _():
                    source = pl.ds(pl.multiple_of(own_col * B, B), B)
                    target = pl.ds(pl.multiple_of(col_block * B, B), B)
                    patch[:, target] = p_hi[here, source].astype(F32) + p_lo[here, source].astype(F32)
        if t + 1 < STEPS:
            cur[after, :] -= dot3((p_hi[after, here], p_lo[after, here]), tops)


def stepwise_update_kernel(first, patch, upper, t_hi, t_lo, c_hi, c_lo, matrix, *refs):
    near, far = refs[:8], refs[8]
    out, raw, rows, high, low, panel, sem_raw, sem_far, sem_in, sem_patch = refs[9:]
    k0, p, q, own_col, own_row, col_block, row_block = place(first)
    copies = near_copies(near, raw.at[pl.ds(0, N_COL)], sem_raw)
    copies += [pltpu.make_async_copy(far, raw.at[pl.ds(N_COL, N_COL)], sem_far),
               pltpu.make_async_copy(matrix, rows, sem_in)]
    for copy in copies:
        copy.start()
    for copy in copies:
        copy.wait()
    own = pl.ds(pl.multiple_of(col_block * B, B), B)

    @pl.loop(0, 4)
    def _(s):
        start = pl.multiple_of(s * PART, PART)
        span = pl.ds(start, PART)
        block = row_blocks(start, PART, p)
        for t in range(STEPS):
            lanes = slice(t * B, (t + 1) * B)
            value = jnp.concatenate([raw[8 * s + n, :, lanes] for n in range(8)], axis=0)
            if t > 0:
                value = value - dot3((high[:, :t * B], low[:, :t * B]), (c_hi[:t * B, lanes], c_lo[:t * B, lanes]))
            value = jnp.where(block > k0 + t, dot3(split(value), split(upper[t])), 0.0)
            high[:, lanes], low[:, lanes] = split(value)

            @pl.when(own_col == t)
            def _():
                panel[...] = value
        for start in range(0, COLS, TILE):
            lanes = slice(start, min(start + TILE, COLS))
            rows[span, lanes] -= dot3((high[...], low[...]), (t_hi[:, lanes], t_lo[:, lanes]))

        @pl.when(own_col < STEPS)
        def _():
            rows[span, own] = jnp.where(block > k0 + own_col, panel[...], rows[span, own])
    copy = pltpu.make_async_copy(rows, out, sem_in)
    copy.start()
    copy.wait()

    @pl.when(own_row < STEPS)
    def _():
        last = pltpu.make_async_copy(patch, out.at[pl.ds(pl.multiple_of(row_block * B, B), B)], sem_patch)
        last.start()
        last.wait()


def shards(matrix, first_step, lower_inverse, upper_inverse):
    def shape(*dims, dtype=F32):
        return jax.ShapeDtypeStruct(dims, dtype)

    dma = pltpu.SemaphoreType.DMA

    def call(kernel, outs, in_specs, out_specs, scratch, args, flops=1_000_000, megabytes=48, **kwargs):
        return pl.pallas_call(
            kernel, out_shape=outs, in_specs=[SM] + in_specs, out_specs=out_specs, scratch_shapes=scratch,
            compiler_params=params(megabytes),
            cost_estimate=pl.CostEstimate(flops=flops, bytes_accessed=4_000_000, transcendentals=0),
            **kwargs,
        )(first_step, *args)

    def along_x(value, distance):
        return lax.ppermute(value, "col", [(i, (i + 4 * distance) % N_COL) for i in range(N_COL)])

    def along_y(value, distance):
        return lax.ppermute(value, "col", [(i, i // 4 * 4 + (i + distance) % 4) for i in range(N_COL)])

    def along_z(value, distance):
        return lax.ppermute(value, "row", [(i, (i + 2 * distance) % N_ROW) for i in range(N_ROW)])

    def swap(value):
        return lax.ppermute(value, "row", [(i, i ^ 1) for i in range(N_ROW)])

    def depth(value):
        ahead, back = along_z(value, 1), along_z(value, 3)
        far = jnp.stack([along_z(ahead[0], 1), along_z(back[1], 3)])
        mine = (value, jnp.stack([ahead, back]), far)
        return mine + tuple(swap(v) for v in mine)

    def ring(move, pieces):
        a, b = jnp.stack(pieces[:2]), jnp.stack(pieces[2:])
        a1, b1 = move(a, 1), move(b, 1)
        a3, b3 = move(a, 3), move(b, 3)
        a2, b2 = move(a1, 1), move(b3, 3)
        return [a, b, a1, b1, a2, b2, a3, b3]

    messages, top = call(send_kernel, [shape(N_COL, SHARE + B, B), shape(B, COLS)], [ANY], [VM] * 2,
                         [dma((4 * N_COL + 1,))], [matrix])
    tops = lax.all_gather(top, "row")
    got = lax.all_to_all(messages, "col", 0, 0)
    corner, one, two = call(select_kernel, [shape(2, 64, WIDE)] + [shape(HALF, WIDE)] * 2, [ANY], [VM] * 3,
                            [dma((STEPS, 4))], [got])
    far = lax.all_gather(two, "col")
    corners = depth(corner)
    near = ring(along_x, [one] + [along_y(one, d) for d in (1, 2, 3)])

    right, patch, safe = call(
        factor_kernel,
        [shape(3 * WIDE, COLS, dtype=BF16), shape(B, COLS), shape(1, dtype=jnp.int32)],
        [VM] * 8 + [ANY], [VM] * 2 + [SM],
        [pltpu.VMEM((WIDE, WIDE), F32), pltpu.VMEM((WIDE, COLS), F32), pltpu.VMEM((WIDE, B), F32),
         pltpu.VMEM((B, B), F32), pltpu.VMEM((B, WIDE), F32), pltpu.VMEM((WIDE, B), F32),
         dma((STEPS,))],
        [lower_inverse, upper_inverse, *corners, tops], flops=12_000_000_000)
    far, patch = lax.optimization_barrier((far, patch))
    left = None
    for offset, shares in ((ROWS // 2, [far]), (0, near)):
        if left is not None:
            shares, left = lax.optimization_barrier((shares, left))
        held = [] if left is None else [left]
        left = call(
            functools.partial(left_kernel, offset), shape(ROWS, 3 * WIDE, dtype=BF16), [ANY] * len(shares + held), ANY,
            [pltpu.VMEM((N_COL, HALF, WIDE), F32), pltpu.VMEM((ROWS // 2, 3 * WIDE), BF16),
             dma((N_COL,)), dma((4,))],
            shares + held, flops=2_000_000_000, input_output_aliases={1 + len(shares): 0} if held else {})

    def together():
        k0 = first_step[0]
        p, q = lax.axis_index("row"), lax.axis_index("col")
        row_block = jnp.arange(ROWS, dtype=jnp.int32) // B * N_ROW + p
        col_block = jnp.arange(COLS, dtype=jnp.int32) // B * N_COL + q
        taken = (row_block >= k0 + STEPS)[:, None] & ((col_block >= k0) & (col_block < k0 + STEPS))[None, :]
        full = jnp.where(taken, jnp.float32(0.0), matrix) + mul(left, right)
        return call(patch_kernel, shape(ROWS, COLS), [ANY, VM], ANY, [dma], [full, patch], megabytes=60,
                    input_output_aliases={1: 0})

    def stepwise():
        c_hi, c_lo, p_hi, p_lo = call(
            stepwise_corner_kernel, [shape(WIDE, WIDE, dtype=BF16)] * 4, [VM] * 2 + [ANY] * 6, [VM] * 4,
            [pltpu.VMEM((WIDE, WIDE), F32), dma((STEPS, 2))], [lower_inverse, upper_inverse, *corners])
        t_hi, t_lo, last = call(
            stepwise_top_kernel, [shape(WIDE, COLS, dtype=BF16)] * 2 + [shape(B, COLS)],
            [VM] * 3 + [ANY], [VM] * 3, [pltpu.VMEM((WIDE, COLS), F32), dma((STEPS,))],
            [lower_inverse, p_hi, p_lo, tops])
        return call(
            stepwise_update_kernel, shape(ROWS, COLS), [VM] * 6 + [ANY] * 10, ANY,
            [pltpu.VMEM((2 * N_COL, HALF, WIDE), F32), pltpu.VMEM((ROWS, COLS), F32), pltpu.VMEM((PART, WIDE), BF16),
             pltpu.VMEM((PART, WIDE), BF16), pltpu.VMEM((PART, B), F32), dma((N_COL,)), dma, dma, dma],
            [last, upper_inverse, t_hi, t_lo, c_hi, c_lo, matrix, *near, far], megabytes=56)

    return lax.cond(safe[0] == 1, together, stepwise)


def solution(mesh):
    placed = (P("row", "col"), P(), P(), P())
    return jax.shard_map(
        shards, mesh=mesh, in_specs=placed, out_specs=P("row", "col"), check_vma=False
    )
```

```python
import functools

import jax
import jax.numpy as jnp
from jax import lax
from jax.experimental import pallas as pl
from jax.experimental.pallas import tpu as pltpu
from jax.sharding import PartitionSpec as P

B = 128
STEPS = 6
ROWS = 2304
COLS = 1152
SHARE = 144
HALF = 72
N_ROW = 8
N_COL = 16
WIDE = STEPS * B
PART = 8 * HALF
SAFE = 100.0
TILE = 256

F32 = jnp.float32
BF16 = jnp.bfloat16
ANY = pl.BlockSpec(memory_space=pl.ANY)
VM = pl.BlockSpec(memory_space=pltpu.VMEM)
SM = pl.BlockSpec(memory_space=pltpu.SMEM)


def params(mebibytes):
    return pltpu.CompilerParams(vmem_limit_bytes=mebibytes * 1024 * 1024)


def split(value):
    high = value.astype(BF16)
    low = (value - high.astype(F32)).astype(BF16)
    return high, low


def mul(left, right):
    return jnp.dot(left, right, preferred_element_type=F32)


def wide(parts):
    return jnp.concatenate([parts[0], parts[1], parts[0]], axis=1)


def tall(parts):
    return jnp.concatenate([parts[0], parts[0], parts[1]], axis=0)


def dot3(left, right):
    lh, ll = left
    rh, rl = right
    return mul(lh, rh) + (mul(ll, rh) + mul(lh, rl))


def place(first):
    k0 = first[0]
    p = lax.axis_index("row")
    q = lax.axis_index("col")
    own_col = lax.rem(q - k0 + 8 * N_COL, N_COL)
    own_row = lax.rem(p - k0 + 16 * N_ROW, N_ROW)
    col_block = lax.div(k0 + jnp.minimum(own_col, STEPS - 1), N_COL)
    row_block = lax.div(k0 + jnp.minimum(own_row, STEPS - 1), N_ROW)
    return k0, p, q, own_col, own_row, col_block, row_block


def send_kernel(first, matrix, messages, top, sem):
    k0, p, q, own_col, own_row, col_block, row_block = place(first)
    lanes = pl.ds(pl.multiple_of(col_block * B, B), B)
    pivot = pl.ds(pl.multiple_of(row_block * B, B), B)
    copies = [pltpu.make_async_copy(matrix.at[pivot], top, sem.at[2 * N_COL])]
    for j in range(N_COL):
        copies.append(pltpu.make_async_copy(
            matrix.at[pivot, lanes], messages.at[j, pl.ds(SHARE, B)], sem.at[j]))
        for h in range(2):
            copies.append(pltpu.make_async_copy(
                matrix.at[pl.ds((h * N_COL + j) * HALF, HALF), lanes], messages.at[j, pl.ds(h * HALF, HALF)],
                sem.at[2 * N_COL + 1 + 2 * j + h]))
    for copy in copies:
        copy.start()
    for copy in copies:
        copy.wait()


def select_kernel(first, messages, corner, one, two, sem):
    k0 = first[0]
    copies = []
    for t in range(STEPS):
        owner = lax.rem(k0 + t, N_COL)
        lanes = pl.ds(t * B, B)
        for n, (target, start, size) in enumerate((
                (corner.at[0, :, lanes], SHARE, 64), (corner.at[1, :, lanes], SHARE + 64, 64),
                (one.at[:, lanes], 0, HALF), (two.at[:, lanes], HALF, HALF))):
            copies.append(pltpu.make_async_copy(messages.at[owner, pl.ds(start, size)], target, sem.at[t, n]))
    for copy in copies:
        copy.start()
    for copy in copies:
        copy.wait()


def pick(refs, index, target, sem):
    for n, ref in enumerate(refs):
        @pl.when(index == n)
        def _():
            pltpu.make_async_copy(ref, target, sem).start()
    return pltpu.make_async_copy(refs[0], target, sem)


def ring_pieces(own, near, far):
    return [(own.at[0], own.at[1]), (near.at[0, 0], near.at[0, 1]),
            (far.at[0], far.at[1]), (near.at[1, 0], near.at[1, 1])]


def bring_corner(first, refs, target, sem):
    k0, p = first[0], lax.axis_index("row")
    z = lax.div(p, 2)
    core = lax.rem(p, 2)
    pieces = ring_pieces(*refs[0:3]) + ring_pieces(*refs[3:6])
    waits = []
    for a in range(STEPS):
        source = lax.rem(k0 + a, N_ROW)
        dz = lax.rem(z - lax.div(source, 2) + 4, 4)
        index = jnp.where(lax.rem(source, 2) == core, 0, 4) + dz
        for h in range(2):
            waits.append(pick([piece[h] for piece in pieces], index,
                              target.at[pl.ds(a * B + h * 64, 64)], sem.at[a, h]))
    for wait in waits:
        wait.wait()


def bring_tops(first, tops, target, sem):
    copies = []
    for a in range(STEPS):
        source = lax.rem(first[0] + a, N_ROW)
        copies.append(pltpu.make_async_copy(tops.at[source], target.at[pl.ds(a * B, B)], sem.at[a]))
    for copy in copies:
        copy.start()
    for copy in copies:
        copy.wait()


def load_corner(first, refs, target):
    k0, p = first[0], lax.axis_index("row")
    z = lax.div(p, 2)
    core = lax.rem(p, 2)
    pieces = ring_pieces(*refs[0:3]) + ring_pieces(*refs[3:6])
    for a in range(STEPS):
        source = lax.rem(k0 + a, N_ROW)
        dz = lax.rem(z - lax.div(source, 2) + 4, 4)
        index = jnp.where(lax.rem(source, 2) == core, 0, 4) + dz
        for n, piece in enumerate(pieces):
            @pl.when(index == n)
            def _():
                for h in range(2):
                    target[a * B + h * 64:a * B + h * 64 + 64, :] = piece[h][...]


def largest(value):
    value = jnp.abs(value)
    return jnp.max(value.reshape(-1, 8, value.shape[-1]), axis=0)


def factor_kernel(first, lower, upper, *refs):
    corners, tops = refs[:6], refs[6]
    right_all, patch, safe, cur, rows, panel, special, n_own, m_own, sem_top = refs[7:]
    k0, p, q, own_col, own_row, col_block, row_block = place(first)
    copies = []
    for a in range(STEPS):
        source = lax.rem(k0 + a, N_ROW)
        copies.append(pltpu.make_async_copy(tops.at[source], rows.at[pl.ds(a * B, B)], sem_top.at[a]))
    for copy in copies:
        copy.start()
    load_corner(first, corners, cur)
    ones = jnp.where(lax.broadcasted_iota(jnp.int32, (B, B), 0) == lax.broadcasted_iota(jnp.int32, (B, B), 1),
                     jnp.float32(1.0), jnp.float32(0.0))
    peak_col = jnp.zeros((8, B), F32)
    peak_row = jnp.zeros((8, WIDE), F32)
    for t in range(STEPS):
        here = slice(t * B, (t + 1) * B)
        diagonal = cur[here, here]
        cur[here, here] = ones
        left = mul(wide(split(cur[:, here])), tall(split(upper[t])))
        right = mul(wide(split(lower[t])), tall(split(cur[here, :])))
        peak_col = jnp.maximum(peak_col, largest(left))
        peak_row = jnp.maximum(peak_row, largest(right))

        @pl.when(own_col == t)
        def _():
            panel[...] = left
            m_own[...] = jnp.zeros((WIDE, B), F32)
            m_own[:(t + 1) * B, :] = left[:(t + 1) * B]

        @pl.when(own_row == t)
        def _():
            n_own[...] = jnp.zeros((B, WIDE), F32)
            n_own[:, :(t + 1) * B] = right[:, :(t + 1) * B]

            @pl.when(own_col == t)
            def _():
                special[...] = diagonal
        cur[:, here] = jnp.zeros((WIDE, B), F32)
        cur[here, :] = jnp.zeros((B, WIDE), F32)
        lefts = wide(split(left))
        rights = tall(split(right))
        for start in range(0, WIDE, TILE):
            cur[:, start:start + TILE] -= mul(lefts, rights[:, start:start + TILE])

    @pl.when((own_col < own_row) & (own_row < STEPS))
    def _():
        special[...] = panel[pl.ds(pl.multiple_of(own_row * B, B), B), :]
    peak = jnp.maximum(jnp.max(peak_col), jnp.max(peak_row))
    safe[0] = jnp.where(peak < SAFE, 1, 0)
    for copy in copies:
        copy.wait()
    own = pl.ds(pl.multiple_of(jnp.minimum(own_row, STEPS - 1) * B, B), B)
    left = wide(split(cur[...]))
    left_own = wide(split(n_own[...]))
    for start in range(0, COLS, TILE):
        size = min(TILE, COLS - start)
        lanes = slice(start, start + size)
        block = ((lax.broadcasted_iota(jnp.int32, (1, size), 1) + start) >> 7) * N_COL + q
        values = tall(split(rows[:, lanes]))
        high, low = split(jnp.where(block > k0 + STEPS - 1, mul(left, values), 0.0))
        for n, part in enumerate((high, high, low)):
            right_all[n * WIDE:(n + 1) * WIDE, lanes] = part
        patch[:, lanes] = jnp.where(block > k0 + own_row, mul(left_own, values), rows[own, lanes])
    own_lanes = pl.ds(pl.multiple_of(col_block * B, B), B)

    @pl.when(own_col < STEPS)
    def _():
        high, low = split(m_own[...])
        for n, part in enumerate((high, high, low)):
            right_all[n * WIDE:(n + 1) * WIDE, own_lanes] = part

    @pl.when((own_col <= own_row) & (own_row < STEPS))
    def _():
        patch[:, own_lanes] = special[...]


def near_copies(near, raw, sem):
    q = lax.axis_index("col")
    x = lax.div(q, 4)
    y = lax.rem(q, 4)
    copies = []
    for dx in range(4):
        for dy in range(4):
            owner = lax.rem(x + 4 - dx, 4) * 4 + lax.rem(y + 4 - dy, 4)
            copies.append(pltpu.make_async_copy(
                near[2 * dx + dy // 2].at[dy % 2], raw.at[owner], sem.at[len(copies)]))
    return copies


def row_blocks(start, count, p):
    return ((lax.broadcasted_iota(jnp.int32, (count, B), 0) + start) >> 7) * N_ROW + p


def left_kernel(offset, first, *refs):
    left, raw, buffer, sem, sem_out = refs[-5:]
    k0, p = first[0], lax.axis_index("row")
    if offset:
        copies = [pltpu.make_async_copy(refs[0].at[n], raw.at[n], sem.at[n]) for n in range(N_COL)]
    else:
        copies = near_copies(refs[:8], raw, sem)
    for copy in copies:
        copy.start()
    if not offset:
        for copy in copies:
            copy.wait()
    outs = []
    for s in range(4):
        if offset:
            for copy in copies[4 * s:4 * s + 4]:
                copy.wait()
        span = slice(s * 4 * HALF, (s + 1) * 4 * HALF)
        live = row_blocks(span.start + offset, 4 * HALF, p) > k0 + STEPS - 1
        for t in range(STEPS):
            value = jnp.concatenate([raw[n, :, t * B:(t + 1) * B] for n in range(4 * s, 4 * s + 4)], axis=0)
            high, low = split(jnp.where(live, value, 0.0))
            for m, part in enumerate((high, low, high)):
                buffer[span, m * WIDE + t * B:m * WIDE + (t + 1) * B] = part
        outs.append(pltpu.make_async_copy(
            buffer.at[pl.ds(span.start, 4 * HALF)], left.at[pl.ds(offset + span.start, 4 * HALF)], sem_out.at[s]))
        outs[-1].start()
    for copy in outs:
        copy.wait()


def patch_kernel(first, full, patch, out, sem):
    own_row, row_block = place(first)[4], place(first)[6]

    @pl.when(own_row < STEPS)
    def _():
        copy = pltpu.make_async_copy(patch, out.at[pl.ds(pl.multiple_of(row_block * B, B), B)], sem)
        copy.start()
        copy.wait()


def stepwise_corner_kernel(first, lower, upper, *refs):
    c_hi, c_lo, p_hi, p_lo, cur, sem = refs[6:]
    bring_corner(first, refs[:6], cur, sem)
    for t in range(STEPS - 1):
        here = slice(t * B, (t + 1) * B)
        after = slice((t + 1) * B, WIDE)
        tops = split(dot3(split(lower[t]), split(cur[here, after])))
        panels = split(dot3(split(cur[after, here]), split(upper[t])))
        c_hi[here, after], c_lo[here, after] = tops
        p_hi[after, here], p_lo[after, here] = panels
        cur[after, after] -= dot3(panels, tops)


def stepwise_top_kernel(first, lower, p_hi, p_lo, tops, t_hi, t_lo, patch, cur, sem):
    k0, p, q, own_col, own_row, col_block, row_block = place(first)
    bring_tops(first, tops, cur, sem)
    lane_block = (lax.broadcasted_iota(jnp.int32, (1, COLS), 1) >> 7) * N_COL + q
    for t in range(STEPS):
        here = slice(t * B, (t + 1) * B)
        after = slice((t + 1) * B, WIDE)
        live = lane_block > k0 + t
        top = jnp.where(live, dot3(split(lower[t]), split(cur[here, :])), 0.0)
        tops = split(top)
        t_hi[here, :], t_lo[here, :] = tops

        @pl.when(own_row == t)
        def _():
            patch[...] = jnp.where(live, top, cur[here, :])
            if t > 0:
                @pl.when(own_col < t)
                def _():
                    source = pl.ds(pl.multiple_of(own_col * B, B), B)
                    target = pl.ds(pl.multiple_of(col_block * B, B), B)
                    patch[:, target] = p_hi[here, source].astype(F32) + p_lo[here, source].astype(F32)
        if t + 1 < STEPS:
            cur[after, :] -= dot3((p_hi[after, here], p_lo[after, here]), tops)


def stepwise_update_kernel(first, patch, upper, t_hi, t_lo, c_hi, c_lo, matrix, *refs):
    near, far = refs[:8], refs[8]
    out, raw, rows, high, low, panel, sem_raw, sem_far, sem_in, sem_patch = refs[9:]
    k0, p, q, own_col, own_row, col_block, row_block = place(first)
    copies = near_copies(near, raw.at[pl.ds(0, N_COL)], sem_raw)
    copies += [pltpu.make_async_copy(far, raw.at[pl.ds(N_COL, N_COL)], sem_far),
               pltpu.make_async_copy(matrix, rows, sem_in)]
    for copy in copies:
        copy.start()
    for copy in copies:
        copy.wait()
    own = pl.ds(pl.multiple_of(col_block * B, B), B)

    @pl.loop(0, 4)
    def _(s):
        start = pl.multiple_of(s * PART, PART)
        span = pl.ds(start, PART)
        block = row_blocks(start, PART, p)
        for t in range(STEPS):
            lanes = slice(t * B, (t + 1) * B)
            value = jnp.concatenate([raw[8 * s + n, :, lanes] for n in range(8)], axis=0)
            if t > 0:
                value = value - dot3((high[:, :t * B], low[:, :t * B]), (c_hi[:t * B, lanes], c_lo[:t * B, lanes]))
            value = jnp.where(block > k0 + t, dot3(split(value), split(upper[t])), 0.0)
            high[:, lanes], low[:, lanes] = split(value)

            @pl.when(own_col == t)
            def _():
                panel[...] = value
        for start in range(0, COLS, TILE):
            lanes = slice(start, min(start + TILE, COLS))
            rows[span, lanes] -= dot3((high[...], low[...]), (t_hi[:, lanes], t_lo[:, lanes]))

        @pl.when(own_col < STEPS)
        def _():
            rows[span, own] = jnp.where(block > k0 + own_col, panel[...], rows[span, own])
    copy = pltpu.make_async_copy(rows, out, sem_in)
    copy.start()
    copy.wait()

    @pl.when(own_row < STEPS)
    def _():
        last = pltpu.make_async_copy(patch, out.at[pl.ds(pl.multiple_of(row_block * B, B), B)], sem_patch)
        last.start()
        last.wait()


def shards(matrix, first_step, lower_inverse, upper_inverse):
    def shape(*dims, dtype=F32):
        return jax.ShapeDtypeStruct(dims, dtype)

    dma = pltpu.SemaphoreType.DMA

    def call(kernel, outs, in_specs, out_specs, scratch, args, flops=1_000_000, megabytes=48, **kwargs):
        return pl.pallas_call(
            kernel, out_shape=outs, in_specs=[SM] + in_specs, out_specs=out_specs, scratch_shapes=scratch,
            compiler_params=params(megabytes),
            cost_estimate=pl.CostEstimate(flops=flops, bytes_accessed=4_000_000, transcendentals=0),
            **kwargs,
        )(first_step, *args)

    def along_x(value, distance):
        return lax.ppermute(value, "col", [(i, (i + 4 * distance) % N_COL) for i in range(N_COL)])

    def along_y(value, distance):
        return lax.ppermute(value, "col", [(i, i // 4 * 4 + (i + distance) % 4) for i in range(N_COL)])

    def along_z(value, distance):
        return lax.ppermute(value, "row", [(i, (i + 2 * distance) % N_ROW) for i in range(N_ROW)])

    def swap(value):
        return lax.ppermute(value, "row", [(i, i ^ 1) for i in range(N_ROW)])

    def depth(value):
        ahead, back = along_z(value, 1), along_z(value, 3)
        far = jnp.stack([along_z(ahead[0], 1), along_z(back[1], 3)])
        mine = (value, jnp.stack([ahead, back]), far)
        return mine + tuple(swap(v) for v in mine)

    def ring(move, pieces):
        a, b = jnp.stack(pieces[:2]), jnp.stack(pieces[2:])
        a1, b1 = move(a, 1), move(b, 1)
        a3, b3 = move(a, 3), move(b, 3)
        a2, b2 = move(a1, 1), move(b3, 3)
        return [a, b, a1, b1, a2, b2, a3, b3]

    messages, top = call(send_kernel, [shape(N_COL, SHARE + B, B), shape(B, COLS)], [ANY], [VM] * 2,
                         [dma((4 * N_COL + 1,))], [matrix])
    tops = lax.all_gather(top, "row")
    got = lax.all_to_all(messages, "col", 0, 0)
    corner, one, two = call(select_kernel, [shape(2, 64, WIDE)] + [shape(HALF, WIDE)] * 2, [ANY], [VM] * 3,
                            [dma((STEPS, 4))], [got])
    far = lax.all_gather(two, "col")
    corners = depth(corner)
    near = ring(along_x, [one] + [along_y(one, d) for d in (1, 2, 3)])

    right, patch, safe = call(
        factor_kernel,
        [shape(3 * WIDE, COLS, dtype=BF16), shape(B, COLS), shape(1, dtype=jnp.int32)],
        [VM] * 8 + [ANY], [VM] * 2 + [SM],
        [pltpu.VMEM((WIDE, WIDE), F32), pltpu.VMEM((WIDE, COLS), F32), pltpu.VMEM((WIDE, B), F32),
         pltpu.VMEM((B, B), F32), pltpu.VMEM((B, WIDE), F32), pltpu.VMEM((WIDE, B), F32),
         dma((STEPS,))],
        [lower_inverse, upper_inverse, *corners, tops], flops=12_000_000_000)
    far, patch = lax.optimization_barrier((far, patch))
    left = None
    for offset, shares in ((ROWS // 2, [far]), (0, near)):
        if left is not None:
            shares, left = lax.optimization_barrier((shares, left))
        held = [] if left is None else [left]
        left = call(
            functools.partial(left_kernel, offset), shape(ROWS, 3 * WIDE, dtype=BF16), [ANY] * len(shares + held), ANY,
            [pltpu.VMEM((N_COL, HALF, WIDE), F32), pltpu.VMEM((ROWS // 2, 3 * WIDE), BF16),
             dma((N_COL,)), dma((4,))],
            shares + held, flops=2_000_000_000, input_output_aliases={1 + len(shares): 0} if held else {})

    def together():
        k0 = first_step[0]
        p, q = lax.axis_index("row"), lax.axis_index("col")
        row_block = jnp.arange(ROWS, dtype=jnp.int32) // B * N_ROW + p
        col_block = jnp.arange(COLS, dtype=jnp.int32) // B * N_COL + q
        taken = (row_block >= k0 + STEPS)[:, None] & ((col_block >= k0) & (col_block < k0 + STEPS))[None, :]
        full = jnp.where(taken, jnp.float32(0.0), matrix) + mul(left, right)
        return call(patch_kernel, shape(ROWS, COLS), [ANY, VM], ANY, [dma], [full, patch], megabytes=60,
                    input_output_aliases={1: 0})

    def stepwise():
        c_hi, c_lo, p_hi, p_lo = call(
            stepwise_corner_kernel, [shape(WIDE, WIDE, dtype=BF16)] * 4, [VM] * 2 + [ANY] * 6, [VM] * 4,
            [pltpu.VMEM((WIDE, WIDE), F32), dma((STEPS, 2))], [lower_inverse, upper_inverse, *corners])
        t_hi, t_lo, last = call(
            stepwise_top_kernel, [shape(WIDE, COLS, dtype=BF16)] * 2 + [shape(B, COLS)],
            [VM] * 3 + [ANY], [VM] * 3, [pltpu.VMEM((WIDE, COLS), F32), dma((STEPS,))],
            [lower_inverse, p_hi, p_lo, tops])
        return call(
            stepwise_update_kernel, shape(ROWS, COLS), [VM] * 6 + [ANY] * 10, ANY,
            [pltpu.VMEM((2 * N_COL, HALF, WIDE), F32), pltpu.VMEM((ROWS, COLS), F32), pltpu.VMEM((PART, WIDE), BF16),
             pltpu.VMEM((PART, WIDE), BF16), pltpu.VMEM((PART, B), F32), dma((N_COL,)), dma, dma, dma],
            [last, upper_inverse, t_hi, t_lo, c_hi, c_lo, matrix, *near, far], megabytes=56)

    return lax.cond(safe[0] == 1, together, stepwise)


def solution(mesh):
    placed = (P("row", "col"), P(), P(), P())
    return jax.shard_map(
        shards, mesh=mesh, in_specs=placed, out_specs=P("row", "col"), check_vma=False
    )
```
